256 devices in a mesh: gx: 32 (over z_lo, x, core), gy: 8 (over z_hi, y).
Axes of the slice: x: 4, y: 4, z: 8 (z_hi: 2, z_lo: 4; z = z_hi * 4 + z_lo), core: 2. Of those that a mesh axis runs over, the one named last changes fastest.
Arguments:
- fields: float32 [3, 8, 768, 3072], P(None, None, 'gx', 'gy'), may hold values from -6 to 6
- east_band: float32 [2, 3, 8, 2, 1024], P(None, None, None, None, 'gy'), may hold values from -6 to 6
- north_band: float32 [2, 3, 8, 2, 256], P(None, None, None, None, 'gx'), may hold values from -6 to 6
- east_index: int32 [2, 3072], P(None, 'gy'), may hold values from 0 to 1022, as said below
- north_index: int32 [2, 768], P(None, 'gx'), may hold values from 0 to 254, as said below
- east_weight: float32 [2, 3072], P(None, 'gy'), may hold values from 0.15 to 0.85
- north_weight: float32 [2, 768], P(None, 'gx'), may hold values from 0.15 to 0.85
- nest_moves: int32 [2, 2], replicated, may hold values from -1 to 1, as said below
- courant: float32 [8], replicated, may hold values from 0.15 to 0.6
- diffuse: float32 [8], replicated, may hold values from 0.02 to 0.12
Outputs:
- advanced: float32 [3, 8, 768, 3072], P(None, None, 'gx', 'gy')
The draws below stay inside these ranges and needn't reach their ends.
Inputs may be any that keep to these rules, and one draw needn't show every extreme that they name: `nest_moves`: each offset is -1 or 1, and the second move is the first reversed in both components. `east_index`: for each side, the donor row of nest row y is y//3 - 1 or y//3, clamped to 0 and 1022. `north_index`: for each side, the donor column of nest column x is x//3 - 1 or x//3, clamped to 0 and 254.
All inputs are finite; a program needn't handle non-finite values.
Results may differ from the reference program's by a relative error of at most 0.000096.
Values sent between devices are 32-bit elements; how exact they have to be, the bound alone decides.
A program may use at most 64 MiB of HBM per device.

```python
import math
import jax
import jax.numpy as jnp
from jax import lax

CX = 24
CY = 384
LEV = 8
NX = 768
NY = 3072
NPX = 256
NPY = 1024


def donor_rows(key, length, block, limit):
    picks = jax.random.randint(key, (2, length), 0, 2, dtype=jnp.int32)
    places = jnp.arange(length, dtype=jnp.int32)[None, :]
    picks = jnp.where(places % block == 0, 0, picks)
    picks = jnp.where(places % block == block - 1, 1, picks)
    return jnp.clip(places // 3 - 1 + picks, 0, limit - 2).astype(jnp.int32)


def draw_east_index(key, part):
    key = jax.random.fold_in(key, 11)
    return donor_rows(key, NY, CY, NPY)


def draw_north_index(key, part):
    key = jax.random.fold_in(key, 12)
    return donor_rows(key, NX, CX, NPX)


def draw_nest_moves(key, part):
    key = jax.random.fold_in(key, 13)
    signs = jax.random.randint(key, (2,), 0, 2, dtype=jnp.int32) * 2 - 1
    return jnp.stack([signs, -signs]).astype(jnp.int32)


def block_scale(stream_key, extent, cuts, least, largest):
    loudness, own = 1.0, jax.random.fold_in(stream_key, 6)
    for axis_at, parts in cuts:
        draws = jnp.exp(jax.random.uniform(jax.random.fold_in(own, axis_at), (parts,), jnp.float32, least / len(cuts), largest / len(cuts)))
        loudness = loudness * jnp.repeat(draws, extent[axis_at] // parts).reshape([-1 if axis == axis_at else 1 for axis in range(len(extent))])
    return loudness


def scatter_about(stream_key, dims, scale, most, cuts=(), kind=jnp.bfloat16):
    values = scale * jax.random.normal(stream_key, dims, jnp.float32)
    if cuts:
        values = values * block_scale(stream_key, dims, cuts, -0.22, 0.18)
    return jnp.clip(values, -most, most).astype(kind)


def setup_inputs(seed: int = 0) -> dict:
    splits = jax.random.split(jax.random.key(seed), 11)
    fields = scatter_about(splits[0], (3, LEV, NX, NY), 1.0, 6.0, ((2, 32), (3, 8)), jnp.float32)
    east_band = scatter_about(splits[1], (2, 3, LEV, 2, NPY), 1.0, 6.0, ((4, 8),), jnp.float32)
    north_band = scatter_about(splits[2], (2, 3, LEV, 2, NPX), 1.0, 6.0, ((4, 32),), jnp.float32)
    east_index = draw_east_index(jax.random.fold_in(splits[10], 71), 0)
    north_index = draw_north_index(jax.random.fold_in(splits[10], 71), 0)
    east_weight = jnp.clip(0.15 + 0.70000002 * jax.random.uniform(splits[5], (2, NY), jnp.float32) ** block_scale(splits[5], (2, NY), ((1, 8),), -0.2, 0.2), 0.15, 0.85)
    north_weight = jnp.clip(0.15 + 0.70000002 * jax.random.uniform(splits[6], (2, NX), jnp.float32) ** block_scale(splits[6], (2, NX), ((1, 32),), -0.2, 0.2), 0.15, 0.85)
    nest_moves = draw_nest_moves(jax.random.fold_in(splits[10], 71), 0)
    courant = jnp.clip(jnp.exp(jax.random.uniform(splits[8], (LEV,), jnp.float32, math.log(0.15), math.log(0.6))), 0.15, 0.6)
    diffuse = jnp.clip(jnp.exp(jax.random.uniform(splits[9], (LEV,), jnp.float32, math.log(0.02), math.log(0.12))), 0.02, 0.12)
    return {"fields": fields, "east_band": east_band, "north_band": north_band, "east_index": east_index, "north_index": north_index, "east_weight": east_weight, "north_weight": north_weight, "nest_moves": nest_moves, "courant": courant, "diffuse": diffuse}


def outward_weights(direction):
    places = jnp.arange(3).astype(jnp.float32)
    return jnp.where(direction > 0, (2.0 * places + 1.0) / 6.0, (5.0 - 2.0 * places) / 6.0)


def edge_values(banded, index_row, weight_row, direction):
    outward = outward_weights(direction)
    blended = banded[:, :, 0, None, :] * (1.0 - outward)[None, None, :, None] + banded[:, :, 1, None, :] * outward[None, None, :, None]
    lower = jnp.take(blended, index_row, axis=3)
    upper = jnp.take(blended, index_row + 1, axis=3)
    return lower * (1.0 - weight_row) + upper * weight_row


def move_nest(fields, shift_east, shift_north, east_band, north_band, east_index, north_index, east_weight, north_weight):
    total_east = fields.shape[2]
    total_north = fields.shape[3]
    padded = jnp.pad(fields, ((0, 0), (0, 0), (3, 3), (3, 3)))
    anchor = jnp.zeros((), jnp.int32)
    start_east = (3 + 3 * shift_east).astype(jnp.int32)
    start_north = (3 + 3 * shift_north).astype(jnp.int32)
    shifted = lax.dynamic_slice(padded, (anchor, anchor, start_east, start_north), fields.shape)
    side_east = (shift_east + 1) // 2
    strip_east = edge_values(east_band[side_east], east_index[side_east], east_weight[side_east], shift_east)
    place_east = jnp.where(shift_east > 0, total_east - 3, 0).astype(jnp.int32)
    placed = lax.dynamic_update_slice(jnp.zeros_like(fields), strip_east, (anchor, anchor, place_east, anchor))
    columns = jnp.arange(total_east)
    leading = jnp.where(shift_east > 0, columns >= total_east - 3, columns < 3)
    shifted = jnp.where(leading[None, None, :, None], placed, shifted)
    side_north = (shift_north + 1) // 2
    strip_north = edge_values(north_band[side_north], north_index[side_north], north_weight[side_north], shift_north)
    strip_north = jnp.swapaxes(strip_north, 2, 3)
    place_north = jnp.where(shift_north > 0, total_north - 3, 0).astype(jnp.int32)
    placed = lax.dynamic_update_slice(jnp.zeros_like(fields), strip_north, (anchor, anchor, anchor, place_north))
    rows_north = jnp.arange(total_north)
    leading = jnp.where(shift_north > 0, rows_north >= total_north - 3, rows_north < 3)
    return jnp.where(leading[None, None, None, :], placed, shifted)


def laplace(padded, center):
    return padded[:, 2:, 1:-1] + padded[:, :-2, 1:-1] + padded[:, 1:-1, 2:] + padded[:, 1:-1, :-2] - 4.0 * center


def substep(fields, courant, diffuse):
    pressure = fields[0]
    zonal_wind = fields[1]
    meridional = fields[2]
    courant_col = courant[:, None, None]
    viscous = diffuse[:, None, None]
    padded = jnp.pad(pressure, ((0, 0), (1, 1), (1, 1)))
    zonal_mid = zonal_wind - 0.5 * courant_col * (padded[:, 2:, 1:-1] - padded[:, :-2, 1:-1])
    merid_mid = meridional - 0.5 * courant_col * (padded[:, 1:-1, 2:] - padded[:, 1:-1, :-2])
    zonal_pad = jnp.pad(zonal_mid, ((0, 0), (1, 1), (1, 1)))
    merid_pad = jnp.pad(merid_mid, ((0, 0), (1, 1), (1, 1)))
    zonal_new = zonal_mid + viscous * laplace(zonal_pad, zonal_mid)
    merid_new = merid_mid + viscous * laplace(merid_pad, merid_mid)
    pressure_new = pressure - 0.5 * courant_col * ((zonal_pad[:, 2:, 1:-1] - zonal_pad[:, :-2, 1:-1]) + (merid_pad[:, 1:-1, 2:] - merid_pad[:, 1:-1, :-2]))
    return jnp.stack([pressure_new, zonal_new, merid_new])


def reference(fields, east_band, north_band, east_index, north_index, east_weight, north_weight, nest_moves, courant, diffuse):
    current = fields
    for number in range(2):
        current = move_nest(current, nest_moves[number, 0], nest_moves[number, 1], east_band, north_band, east_index, north_index, east_weight, north_weight)
        current = substep(current, courant, diffuse)
    return current
```

```python
import functools

import jax
import jax.numpy as jnp
from jax import lax
from jax.experimental import pallas as pl
from jax.experimental.pallas import tpu as pltpu
from jax.sharding import PartitionSpec as P

MESH = pl.DeviceIdType.MESH
F32 = jnp.float32
I32 = jnp.int32
HALO = 4
ROWS = 24
SPAN = ROWS + 2 * HALO
WIDE = 384
LANES = 128
LEVELS = 8
X_ROWS = (4, 3, 2)


def third(v):
    return (((v + 48) * 43691) >> 17) - 16


def roll(v, by):
    size = v.shape[1]
    by = by % size
    return pltpu.roll(v, by, 1) if by else v


def iota():
    return lax.broadcasted_iota(I32, (LEVELS, LANES), 1)


def take(v, at):
    return jnp.take_along_axis(v, at & (LANES - 1), axis=1)


def pick_shift(v, by, step):
    return jnp.where(by > 0, roll(v, step), jnp.where(by < 0, roll(v, -step), v))


def edge_block(head, tail):
    lane = iota()
    return jnp.where((lane >= 32) & (lane < 64), roll(tail, 64), head)


def edge_cells():
    lane = iota()
    return jnp.where(lane < 32, lane, jnp.where(lane < 96, lane + (WIDE - 64), lane - LANES))


def slots():
    lane = iota()
    return jnp.where((lane & 7) < 4, ((lane + 64) & 127) >> 3, ((lane + 4) & 127) >> 3)


def advance(load, store, lo, hi, kk, kk_row, visc, unroll):
    def first(r, p_below, p_here, p_above):
        k = kk_row(r)
        u = load(1, r) - k * (p_above - p_below)
        v = load(2, r) - k * (roll(p_here, -1) - roll(p_here, 1))
        return u, v

    def row(r, carry):
        p0, p1, ub, u0, vb, v0 = carry
        p2 = load(0, r + 2)
        ua, va = first(r + 1, p0, p1, p2)
        un, us, vn, vs = roll(u0, -1), roll(u0, 1), roll(v0, -1), roll(v0, 1)
        store(0, r, p0 - kk * ((ua - ub) + (vn - vs)))
        store(1, r, u0 + visc * (((ua + ub) + (un + us)) - 4.0 * u0))
        store(2, r, v0 + visc * (((va + vb) + (vn + vs)) - 4.0 * v0))
        return p1, p2, u0, ua, v0, va

    p = [load(0, lo - 2 + i) for i in range(4)]
    ub, vb = first(lo - 1, p[0], p[1], p[2])
    u0, v0 = first(lo, p[1], p[2], p[3])
    carry = (p[2], p[3], ub, u0, vb, v0)
    if unroll is None:
        for r in range(lo, hi):
            carry = row(r, carry)
    else:
        lax.fori_loop(lo, hi, row, carry, unroll=unroll)


def exchange_kernel(
    sizes,
    fields,
    east_band,
    north_band,
    east_index,
    north_index,
    east_weight,
    north_weight,
    moves,
    courant,
    diffuse,
    out,
    ext,
    gxt,
    mid,
    midg,
    packed,
    from_y,
    from_d,
    east_out,
    east_in,
    north_out,
    north_in,
    strip,
    strip_g,
    ns,
    eb,
    ei,
    ew,
    nb,
    nbw,
    ni,
    nw,
    ntab,
    mv,
    ks,
    qs,
    in_sem,
    small_sem,
    x_send,
    x_recv,
    y_send,
    y_recv,
    d_send,
    d_recv,
    ea_send,
    ea_recv,
    na_send,
    na_recv,
):
    nx, ny = sizes
    gx = lax.axis_index("gx")
    gy = lax.axis_index("gy")
    total_x = nx * ROWS
    total_y = ny * WIDE
    west, east = gx == 0, gx == nx - 1
    south, north = gy == 0, gy == ny - 1
    x_edge = jnp.logical_or(west, east)
    y_edge = jnp.logical_or(south, north)
    has_x = {-1: gx > 0, 1: gx < nx - 1}
    has_y = {-1: gy > 0, 1: gy < ny - 1}

    def has(dx, dy):
        if dx and dy:
            return jnp.logical_and(has_x[dx], has_y[dy])
        return has_x[dx] if dx else has_y[dy]

    around = [(dx, dy) for dy in (-1, 1, 0) for dx in (-1, 0, 1) if dx or dy]
    barrier = pltpu.get_barrier_semaphore()
    for dx, dy in around:

        @pl.when(has(dx, dy))
        def _(dx=dx, dy=dy):
            pl.semaphore_signal(barrier, inc=1, device_id=(gx + dx, gy + dy), device_id_type=MESH)

    loads = [
        pltpu.make_async_copy(fields.at[f, l], ext.at[f, HALO : HALO + ROWS, l, :], in_sem.at[f * LEVELS + l])
        for f in range(3)
        for l in range(LEVELS)
    ]
    smalls = [
        pltpu.make_async_copy(s, d, small_sem.at[k])
        for k, (s, d) in enumerate(
            (
                (moves, mv),
                (courant, ks),
                (diffuse, qs),
                (east_band, eb),
                (east_index, ei),
                (east_weight, ew),
                (north_band, nb),
                (north_index, ni),
                (north_weight, nw),
            )
        )
    ]
    for c in loads + smalls:
        c.start()
    for c in loads:
        c.wait()

    lane = iota()
    slot = slots()
    keep = {}
    for r in range(HALO, HALO + ROWS):
        h, i = divmod(r, 16)
        for f in range(3):
            block = edge_block(ext[f, r, :, 0:LANES], ext[f, r, :, 2 * LANES : WIDE])
            gxt[f, r] = block
            moved = roll(block, 8 * i + 64)
            keep[h, f] = jnp.where(slot == i, moved, keep[h, f]) if (h, f) in keep else moved
    for (h, f), v in keep.items():
        packed[h, f] = v
    for c in smalls:
        c.wait()

    shift_x = mv[0, 0]
    shift_y = mv[0, 1]
    side_x = jnp.where(west, 0, 1)
    side_y = jnp.where(south, 0, 1)
    out_x = shift_x == 2 * side_x - 1
    out_y = shift_y == 2 * side_y - 1
    by_y = jnp.where(out_x, shift_y, 0)
    by_x = jnp.where(out_y, shift_x, 0)

    def table(head, tail):
        return head, tail

    def east_rows():
        cell = lax.broadcasted_iota(I32, (1, WIDE), 1)
        index = jnp.where(side_x == 0, ei[0:1, :], ei[1:2, :])
        upper = (index - (gy * LANES + third(cell)) + 1).astype(F32)
        weight = jnp.where(side_x == 0, ew[0:1, :], ew[1:2, :])
        wide = (LEVELS, WIDE)
        return jnp.broadcast_to(upper, wide), jnp.broadcast_to(weight, wide)

    def east_parents(b, f):
        return eb[pl.ds(side_x * 48 + f * 16 + b, LEVELS, stride=2), :]

    def north_parents(b, f):
        return nbw[pl.ds(side_y * 48 + f * 16 + b, LEVELS, stride=2), :]

    @pl.when(x_edge)
    def _():
        acc = jnp.zeros((LEVELS, LANES), F32)
        for b in range(2):
            for f in range(3):
                k = 3 * b + f
                near = (((lane - 8 * k + 4) & 127) >> 3) == 0
                acc = jnp.where(near, roll(east_parents(b, f), 8 * k), acc)
        east_out[0] = acc
        upper, weight = east_rows()
        first = lax.broadcasted_iota(I32, (LEVELS, LANES), 0) == 0
        rows = []
        for v in (upper, weight):
            rows.append(jnp.where(lane < 96, roll(v[:, 0:LANES], 64), v[:, 2 * LANES : WIDE]))
        east_out[1] = jnp.where(first, rows[0], rows[1])

    @pl.when(y_edge)
    def _():
        nbw[...] = jnp.zeros((96, LANES), F32)
        nbw[:, 0:8] = nb[...]
        cell = lax.broadcasted_iota(I32, (2, ROWS), 1)
        ntab[...] = jnp.zeros((LEVELS, LANES), F32)
        ntab[0:2, 0:ROWS] = (ni[...] - (gx * 8 + third(cell)) + 1).astype(F32)
        ntab[2:4, 0:ROWS] = nw[...]
        acc = jnp.zeros((LEVELS, LANES), F32)
        for b in range(2):
            for f in range(3):
                k = 3 * b + f
                acc = jnp.where((lane >> 3) == k, roll(north_parents(b, f), 8 * k), acc)
        north_out[0] = acc
        north_out[1] = ntab[...]

    def to(dx, dy, src, dst, send, recv):
        return pltpu.make_async_remote_copy(
            src_ref=src,
            dst_ref=dst,
            send_sem=send,
            recv_sem=recv,
            device_id=(gx + dx, gy + dy),
            device_id_type=MESH,
        )

    sends = []
    for s, dy in enumerate((-1, 1)):
        sends.append((0, dy, has(0, dy), [to(0, dy, packed, from_y.at[1 - s], y_send.at[s], y_recv.at[1 - s])]))
    for a, dx in enumerate((-1, 1)):
        for s, dy in enumerate((-1, 1)):
            sends.append(
                (
                    dx,
                    dy,
                    has(dx, dy),
                    [to(dx, dy, packed.at[a], from_d.at[1 - a, 1 - s], d_send.at[2 * a + s], d_recv.at[2 * (1 - a) + 1 - s])],
                )
            )
    east_sends = []
    for s, dy in enumerate((-1, 1)):
        east_sends.append(
            (dy, jnp.logical_and(x_edge, has(0, dy)), to(0, dy, east_out, east_in.at[1 - s], ea_send.at[s], ea_recv.at[1 - s]))
        )
    x_sends = []
    north_sends = []
    for a, dx in enumerate((-1, 1)):
        group = []
        for f in range(3):
            n = X_ROWS[f]
            if dx < 0:
                src, dst = ext.at[f, HALO : HALO + n], ext.at[f, HALO + ROWS : HALO + ROWS + n]
            else:
                src, dst = ext.at[f, HALO + ROWS - n : HALO + ROWS], ext.at[f, HALO - n : HALO]
            group.append(to(dx, 0, src, dst, x_send.at[3 * a + f], x_recv.at[3 * (1 - a) + f]))
        x_sends.append((dx, 0, has(dx, 0), group))
        north_sends.append(
            (dx, jnp.logical_and(y_edge, has(dx, 0)), to(dx, 0, north_out, north_in.at[1 - a], na_send.at[a], na_recv.at[1 - a]))
        )

    count_x = 1 + has_x[-1].astype(I32) + has_x[1].astype(I32)
    count_y = 1 + has_y[-1].astype(I32) + has_y[1].astype(I32)
    pl.semaphore_wait(barrier, count_x * count_y - 1)

    for _, _, there, group in sends:

        @pl.when(there)
        def _(group=group):
            for c in group:
                c.start()

    for _, there, c in east_sends + north_sends:

        @pl.when(there)
        def _(c=c):
            c.start()

    for _, _, there, group in x_sends:

        @pl.when(there)
        def _(group=group):
            for c in group:
                c.start()

    level = lax.broadcasted_iota(I32, (LEVELS, LANES), 0)
    half = jnp.zeros((LEVELS, LANES), F32)
    visc = jnp.zeros((LEVELS, LANES), F32)
    for l in range(LEVELS):
        half = jnp.where(level == l, 0.5 * ks[l], half)
        visc = jnp.where(level == l, qs[l], visc)
    half_w = jnp.concatenate([half] * 3, axis=1)
    visc_w = jnp.concatenate([visc] * 3, axis=1)

    def in_first(r):
        x = gx * ROWS + r - HALO
        return jnp.where(jnp.logical_and(x >= 3 * shift_x, x < total_x + 3 * shift_x), 1.0, 0.0).astype(F32)

    def in_second(r):
        x = gx * ROWS + r - HALO
        return jnp.where(jnp.logical_and(x >= 0, x < total_x), 1.0, 0.0).astype(F32)

    def store_mid(f, r, v):
        mid[f, r] = v

    def store_out(f, r, v):
        out[f, r - HALO] = v

    def substep_1(lo, hi):
        advance(lambda f, r: ext[f, r], store_mid, lo, hi, half_w, lambda r: half_w * in_first(r), visc_w, 1)

    def substep_2(lo, hi):
        advance(lambda f, r: mid[f, r], store_out, lo, hi, half_w, lambda r: half_w * in_second(r), visc_w, 1)

    substep_1(9, 23)
    substep_2(11, 21)

    def blend(parents, base, upper, weight, by):
        c0 = (1.0 - upper) * (1.0 - weight)
        c1 = (1.0 - upper) * weight + upper * (1.0 - weight)
        c2 = upper * weight
        values = []
        for v in parents:
            v = pick_shift(v, by, 1)
            values.append(c0 * take(v, base - 1) + c1 * take(v, base) + c2 * take(v, base + 1))
        return values

    def outward(c):
        return jnp.where(side_x > 0, (2.0 * c + 1.0) / 6.0, (5.0 - 2.0 * c) / 6.0).astype(F32)

    @pl.when(x_edge)
    def _():
        upper, weight = east_rows()
        upper = pick_shift(upper, by_y, 3)
        weight = pick_shift(weight, by_y, 3)
        for j in range(3):
            cut = slice(LANES * j, LANES * j + LANES)
            base = third(lane + LANES * j)
            for f in range(3):
                inner, outer = blend([east_parents(b, f) for b in range(2)], base, upper[:, cut], weight[:, cut], by_y)
                for c in range(3):
                    a = outward(c)
                    strip[c, f, :, cut] = inner * (1.0 - a) + outer * a

    for a, (dx, _, there, group) in enumerate(x_sends):

        @pl.when(has(-dx, 0))
        def _(group=group):
            for c in group:
                c.wait_recv()

    for side, first_strip, first_own, zero in ((0, 1, 4, 0), (1, 28, 25, 31)):

        @pl.when(west if side == 0 else east)
        def _(first_strip=first_strip, first_own=first_own, zero=zero):
            for f in range(3):
                ext[f, zero] = jnp.zeros((LEVELS, WIDE), F32)
                for c in range(3):
                    ext[f, first_strip + c] = jnp.where(out_x, strip[c, f], 0.0)
                    ext[f, first_own + c] = jnp.where(out_x, ext[f, first_own + c], 0.0)

    for r in list(range(HALO)) + list(range(HALO + ROWS, SPAN)):
        for f in range(3):
            gxt[f, r] = edge_block(ext[f, r, :, 0:LANES], ext[f, r, :, 2 * LANES : WIDE])

    substep_1(2, 9)
    substep_1(23, 30)

    def lay_rows(dst, source, width):
        for side, first_own, beyond in ((0, 4, (2, 3)), (1, 25, (28, 29))):

            @pl.when(west if side == 0 else east)
            def _(first_own=first_own, beyond=beyond):
                for f in range(3):
                    for r in beyond:
                        dst[f, r] = jnp.zeros((LEVELS, width), F32)
                    for c in range(3):
                        dst[f, first_own + c] = jnp.where(out_x, dst[f, first_own + c], source[c, f])

    lay_rows(mid, strip, WIDE)
    substep_2(4, 11)
    substep_2(21, 28)

    @pl.when(y_edge)
    def _():
        for a, (dx, there, c) in enumerate(north_sends):

            @pl.when(has(-dx, 0))
            def _(c=c):
                c.wait_recv()

        lower_in = jnp.where(has_x[-1], north_in[0], 0.0)
        upper_in = jnp.where(has_x[1], north_in[1], 0.0)
        lower_tab = jnp.where(has_x[-1], north_in[0, 1], 0.0)
        upper_tab = jnp.where(has_x[1], north_in[1, 1], 0.0)
        lower_band, upper_band = lower_in[0], upper_in[0]
        own = ntab[...]
        tab = jnp.where(
            lane >= 112,
            roll(lower_tab, 128 - ROWS),
            jnp.where((lane >= ROWS) & (lane < 2 * ROWS), roll(upper_tab, ROWS), own),
        )
        tab = pick_shift(tab, by_x, 3)
        parents = []
        for b in range(2):
            for f in range(3):
                k = 3 * b + f
                v = jnp.where((lane >= 8) & (lane < 16), roll(upper_band, 8 - 8 * k), north_parents(b, f))
                parents.append(jnp.where(lane >= 120, roll(lower_band, -8 - 8 * k), v))
        place = lane & 7
        step = jnp.where(place < 4, place, place - 5).astype(F32)
        a = jnp.where(place < 4, (2.0 * step + 1.0) / 6.0, (5.0 - 2.0 * step) / 6.0)
        real = (place != 3) & (place != 4)
        for h in range(2):
            x = slot + (16 * h - HALO)
            base = third(x)
            tab_x = take(tab, x)
            upper = jnp.broadcast_to(jnp.where(side_y == 0, tab_x[0:1], tab_x[1:2]), (LEVELS, LANES))
            weight = jnp.broadcast_to(jnp.where(side_y == 0, tab_x[2:3], tab_x[3:4]), (LEVELS, LANES))
            whole = x + gx * ROWS - 3 * by_x
            fits = real & (whole >= 0) & (whole < total_x)
            values = blend(parents, base, upper, weight, by_x)
            for f in range(3):
                ns[h, f] = jnp.where(fits, values[f] * (1.0 - a) + values[3 + f] * a, 0.0)

    for s, (_, dy, _, group) in enumerate(sends):

        @pl.when(has(-sends[s][0], -dy) if sends[s][0] else has(0, -dy))
        def _(group=group):
            for c in group:
                c.wait_recv()

    low = (lane & 7) < 4
    halo_lanes = ((lane >= 64) & (lane < 68)) | (lane >= 124)
    cells = edge_cells() + gy * WIDE
    keep_north = jnp.logical_and(low, north)
    keep_south = jnp.logical_and(jnp.logical_not(low), south)
    ns_lanes = jnp.logical_or(keep_north, keep_south)
    joined = {}
    for f in range(3):
        for h in range(2):
            v = jnp.where(low, from_y[1, h, f], from_y[0, h, f])
            d = roll(jnp.where(low, from_d[h, 1, f], from_d[h, 0, f]), 64)
            v = jnp.where((slot < HALO) if h == 0 else (slot >= 16 - HALO), d, v)
            joined[h, f] = v
    for f in range(3):
        for h in range(2):
            packed_ns = jnp.where(out_y, ns[h, f], 0.0)
            joined[h, f] = jnp.where(ns_lanes, packed_ns, joined[h, f])
    for r in range(SPAN):
        h, i = divmod(r, 16)
        for f in range(3):
            gxt[f, r] = jnp.where(halo_lanes, roll(joined[h, f], -8 * i), gxt[f, r])

    @pl.when(x_edge)
    def _():
        for s, (dy, _, c) in enumerate(east_sends):

            @pl.when(has(0, -dy))
            def _(c=c):
                c.wait_recv()

        lower_in = jnp.where(has_y[-1], east_in[0], 0.0)
        upper_in = jnp.where(has_y[1], east_in[1], 0.0)
        lower_band, lower_tab = lower_in[0], lower_in[1]
        upper_band, upper_tab = upper_in[0], upper_in[1]
        upper, weight = east_rows()
        tabs = []
        for k, v in enumerate((upper, weight)):
            v = edge_block(v[:, 0:LANES], v[:, 2 * LANES : WIDE])
            lo_row = jnp.broadcast_to(lower_tab[k : k + 1], (LEVELS, LANES))
            up_row = jnp.broadcast_to(upper_tab[k : k + 1], (LEVELS, LANES))
            v = jnp.where((lane >= 64) & (lane < 96), up_row, v)
            v = jnp.where(lane >= 112, lo_row, v)
            tabs.append(pick_shift(v, by_y, 3))
        base = jnp.where(lane < 32, third(lane), jnp.where(lane < 96, third(lane + (WIDE - 64)) - 32, third(lane - LANES)))
        inside = jnp.logical_and(
            jnp.logical_or(jnp.logical_not(north), lane < 64) | (lane >= 96),
            jnp.logical_or(jnp.logical_not(south), lane < 96),
        )
        for f in range(3):
            parents = []
            for b in range(2):
                k = 3 * b + f
                own = east_parents(b, f)
                v = jnp.where((lane >= 64) & (lane < 96), roll(own, -32), own)
                v = jnp.where((lane >= 96) & (lane < 100), roll(upper_band, 96 - 8 * k), v)
                parents.append(jnp.where(lane >= 124, roll(lower_band, -8 * k), v))
            inner, outer = blend(parents, base, tabs[0], tabs[1], by_y)
            for c in range(3):
                a = outward(c)
                strip_g[c, f] = inner * (1.0 - a) + outer * a
        for side, first_strip, first_own, zero in ((0, 1, 4, 0), (1, 28, 25, 31)):

            @pl.when(west if side == 0 else east)
            def _(first_strip=first_strip, first_own=first_own, zero=zero):
                for f in range(3):
                    gxt[f, zero] = jnp.zeros((LEVELS, LANES), F32)
                    for c in range(3):
                        gxt[f, first_strip + c] = jnp.where(
                            inside, jnp.where(out_x, strip_g[c, f], 0.0), gxt[f, first_strip + c]
                        )
                        gxt[f, first_own + c] = jnp.where(out_x, gxt[f, first_own + c], 0.0)

    my_first = jnp.logical_and(cells >= 3 * shift_y, cells < total_y + 3 * shift_y)
    my_second = jnp.logical_and(cells >= 0, cells < total_y)

    @pl.when(y_edge)
    def _():
        for r in range(SPAN):
            for f in range(3):
                gxt[f, r] = jnp.where(my_first, gxt[f, r], 0.0)

    half_1 = jnp.where(my_first, half, 0.0)
    half_2 = jnp.where(my_second, half, 0.0)

    def store_midg(f, r, v):
        midg[f, r] = v

    def store_edge(f, r, v):
        r = r - HALO
        head = slice(0, LANES)
        tail = slice(2 * LANES, WIDE)
        out[f, r, :, head] = jnp.where(lane < 16, v, out[f, r, :, head])
        out[f, r, :, tail] = jnp.where(lane >= 112, roll(v, 64), out[f, r, :, tail])

    advance(lambda f, r: gxt[f, r], store_midg, 2, 30, half, lambda r: half_1 * in_first(r), visc, None)
    lay_rows(midg, strip_g, LANES)

    @pl.when(y_edge)
    def _():
        mine = jnp.where(north, jnp.where((lane >= 61) & (lane < 64), 1, 0), jnp.where(lane < 3, 1, 0)) > 0
        lay = jnp.logical_and(mine, jnp.logical_not(out_y))
        for r in range(2, 30):
            h, i = divmod(r, 16)
            for f in range(3):
                v = ns[h, f]
                v = jnp.where(north, roll(v, -8 * i - 3), roll(v, -8 * i + 3))
                v = jnp.where(lay, v, midg[f, r])
                midg[f, r] = jnp.where(my_second, v, 0.0)

    advance(lambda f, r: midg[f, r], store_edge, 4, 28, half, lambda r: half_2 * in_second(r), visc, None)

    for _, _, there, group in sends + x_sends:

        @pl.when(there)
        def _(group=group):
            for c in group:
                c.wait_send()

    for _, there, c in east_sends + north_sends:

        @pl.when(there)
        def _(c=c):
            c.wait_send()


def write_kernel(ready, out, sem):
    copies = [
        pltpu.make_async_copy(ready.at[f, :, l, :], out.at[f, l], sem.at[f * LEVELS + l])
        for f in range(3)
        for l in range(LEVELS)
    ]
    for c in copies:
        c.start()
    for c in copies:
        c.wait()


def body(
    sizes,
    fields,
    east_band,
    north_band,
    east_index,
    north_index,
    east_weight,
    north_weight,
    nest_moves,
    courant,
    diffuse,
):
    vmem = pltpu.VMEM
    dma = pltpu.SemaphoreType.DMA
    tile = (LEVELS, LANES)
    ready = pl.pallas_call(
        functools.partial(exchange_kernel, sizes),
        out_shape=jax.ShapeDtypeStruct((3, ROWS, LEVELS, WIDE), F32),
        in_specs=[pl.BlockSpec(memory_space=pl.ANY)] * 10,
        out_specs=pl.BlockSpec(memory_space=pltpu.VMEM),
        scratch_shapes=[
            vmem((3, SPAN, LEVELS, WIDE), F32),
            vmem((3, SPAN) + tile, F32),
            vmem((3, SPAN, LEVELS, WIDE), F32),
            vmem((3, SPAN) + tile, F32),
            vmem((2, 3) + tile, F32),
            vmem((2, 2, 3) + tile, F32),
            vmem((2, 2, 3) + tile, F32),
            vmem((2,) + tile, F32),
            vmem((2, 2) + tile, F32),
            vmem((2,) + tile, F32),
            vmem((2, 2) + tile, F32),
            vmem((3, 3, LEVELS, WIDE), F32),
            vmem((3, 3) + tile, F32),
            vmem((2, 3) + tile, F32),
            vmem((96, LANES), F32),
            vmem((2, WIDE), I32),
            vmem((2, WIDE), F32),
            vmem((96, 8), F32),
            vmem((96, LANES), F32),
            vmem((2, ROWS), I32),
            vmem((2, ROWS), F32),
            vmem(tile, F32),
            pltpu.SMEM((2, 2), I32),
            pltpu.SMEM((LEVELS,), F32),
            pltpu.SMEM((LEVELS,), F32),
            dma((24,)),
            dma((9,)),
            dma((6,)),
            dma((6,)),
            dma((2,)),
            dma((2,)),
            dma((4,)),
            dma((4,)),
            dma((2,)),
            dma((2,)),
            dma((2,)),
            dma((2,)),
        ],
        compiler_params=pltpu.CompilerParams(
            collective_id=0, has_side_effects=True, vmem_limit_bytes=VMEM_A
        ),
    )(
        fields,
        east_band.reshape(96, LANES),
        north_band.reshape(96, 8),
        east_index,
        north_index,
        east_weight,
        north_weight,
        nest_moves,
        courant,
        diffuse,
    )
    return pl.pallas_call(
        write_kernel,
        out_shape=jax.ShapeDtypeStruct(fields.shape, F32),
        in_specs=[pl.BlockSpec(memory_space=pltpu.VMEM)],
        out_specs=pl.BlockSpec(memory_space=pl.ANY),
        scratch_shapes=[dma((24,))],
        compiler_params=pltpu.CompilerParams(vmem_limit_bytes=VMEM_B),
    )(ready)


VMEM_A = 56 * 1024 * 1024
VMEM_B = 8 * 1024 * 1024


def solution(mesh):
    sizes = (mesh.shape["gx"], mesh.shape["gy"])
    return jax.shard_map(
        functools.partial(body, sizes),
        mesh=mesh,
        in_specs=(
            P(None, None, "gx", "gy"),
            P(None, None, None, None, "gy"),
            P(None, None, None, None, "gx"),
            P(None, "gy"),
            P(None, "gx"),
            P(None, "gy"),
            P(None, "gx"),
            P(),
            P(),
            P(),
        ),
        out_specs=P(None, None, "gx", "gy"),
        check_vma=False,
    )
```

```python
import functools

import jax
import jax.numpy as jnp
from jax import lax
from jax.experimental import pallas as pl
from jax.experimental.pallas import tpu as pltpu
from jax.sharding import PartitionSpec as P

MESH = pl.DeviceIdType.MESH
F32 = jnp.float32
I32 = jnp.int32
HALO = 4
ROWS = 24
SPAN = ROWS + 2 * HALO
WIDE = 384
LANES = 128
LEVELS = 8
X_ROWS = (4, 3, 2)
TILE = (LEVELS, LANES)


def third(v):
    return (((v + 48) * 43691) >> 17) - 16


def roll(v, by):
    by = by % v.shape[1]
    return pltpu.roll(v, by, 1) if by else v


def roll_rows(v, by):
    return pltpu.roll(v, by % v.shape[0], 0)


def iota(axis=1, shape=TILE):
    return lax.broadcasted_iota(I32, shape, axis)


def take(v, at):
    return jnp.take_along_axis(v, at & (LANES - 1), axis=1)


def pick_shift(v, by, step):
    return jnp.where(by > 0, roll(v, step), jnp.where(by < 0, roll(v, -step), v))


def slots():
    lane = iota()
    return jnp.where((lane & 7) < 4, ((lane + 64) & 127) >> 3, ((lane + 4) & 127) >> 3)


def advance(load, store, lo, hi, kk, kk_row, visc):
    def first(r, p_below, p_here, p_above):
        k = kk_row(r)
        u = load(1, r) - k * (p_above - p_below)
        v = load(2, r) - k * (roll(p_here, -1) - roll(p_here, 1))
        return u, v

    p = [load(0, lo - 2 + i) for i in range(4)]
    ub, vb = first(lo - 1, p[0], p[1], p[2])
    u0, v0 = first(lo, p[1], p[2], p[3])
    p0, p1 = p[2], p[3]
    for r in range(lo, hi):
        p2 = load(0, r + 2)
        ua, va = first(r + 1, p0, p1, p2)
        un, us, vn, vs = roll(u0, -1), roll(u0, 1), roll(v0, -1), roll(v0, 1)
        store(0, r, p0 - kk * ((ua - ub) + (vn - vs)))
        store(1, r, u0 + visc * (((ua + ub) + (un + us)) - 4.0 * u0))
        store(2, r, v0 + visc * (((va + vb) + (vn + vs)) - 4.0 * v0))
        p0, p1, ub, u0, vb, v0 = p1, p2, u0, ua, v0, va


def edge_substep(fields, kk_in, kk, visc):
    p, u, v = fields
    u = u - kk_in * (roll_rows(p, -1) - roll_rows(p, 1))
    v = v - kk_in * (roll(p, -1) - roll(p, 1))
    ue, uw = roll_rows(u, -1), roll_rows(u, 1)
    vn, vs = roll(v, -1), roll(v, 1)
    p = p - kk * ((ue - uw) + (vn - vs))
    u2 = u + visc * (((ue + uw) + (roll(u, -1) + roll(u, 1))) - 4.0 * u)
    v2 = v + visc * (((roll_rows(v, -1) + roll_rows(v, 1)) + (vn + vs)) - 4.0 * v)
    return p, u2, v2


def exchange_kernel(
    sizes,
    fields,
    east_band,
    north_band,
    east_index,
    north_index,
    east_weight,
    north_weight,
    moves,
    courant,
    diffuse,
    nat,
    ext,
    mid,
    gl,
    gr,
    to_y,
    from_y,
    from_d,
    east_out,
    east_in,
    north_out,
    north_in,
    strip,
    stage,
    sg,
    ns,
    ns_stage,
    nsa,
    eb,
    ei,
    ew,
    nb,
    nbw,
    ni,
    nw,
    ntab,
    mv,
    ks,
    qs,
    in_sem,
    small_sem,
    x_send,
    x_recv,
    y_send,
    y_recv,
    d_send,
    d_recv,
    ea_send,
    ea_recv,
    na_send,
    na_recv,
    ready,
):
    nx, ny = sizes
    gx = lax.axis_index("gx")
    gy = lax.axis_index("gy")
    total_x = nx * ROWS
    total_y = ny * WIDE
    upper_mid = ny // 2
    lower_mid = upper_mid - 1
    west, east = gx == 0, gx == nx - 1
    south, north = gy == 0, gy == ny - 1
    x_edge = jnp.logical_or(west, east)
    y_edge = jnp.logical_or(south, north)
    has_x = {-1: gx > 0, 1: gx < nx - 1}
    has_y = {-1: gy > 0, 1: gy < ny - 1}
    at_lower = gy == lower_mid
    at_upper = gy == upper_mid
    at_mid = jnp.logical_or(at_lower, at_upper)

    def both(a, b):
        return jnp.logical_and(a, b)

    def has(dx, dy):
        if dx and dy:
            return both(has_x[dx], has_y[dy])
        return has_x[dx] if dx else has_y[dy]

    def over(dy):
        return at_lower if dy > 0 else at_upper

    around = [(dx, dy) for dy in (-1, 1, 0) for dx in (-1, 0, 1) if dx or dy]
    barrier = pltpu.get_barrier_semaphore()
    for dx, dy in around:
        if dy:
            to_mid = (gy + dy == lower_mid) if dy > 0 else (gy + dy == upper_mid)
            greet = both(has(dx, dy), jnp.logical_or(over(dy), jnp.logical_not(to_mid)))
        else:
            greet = both(has(dx, dy), jnp.logical_not(at_mid))

        @pl.when(greet)
        def _(dx=dx, dy=dy):
            pl.semaphore_signal(barrier, inc=1, device_id=(gx + dx, gy + dy), device_id_type=MESH)

    loads = [
        pltpu.make_async_copy(
            fields.at[f, l, :, LANES * j : LANES * j + LANES], ext.at[j, f, 0:ROWS, l, :], in_sem.at[3 * j + f]
        )
        for j in (0, 2, 1)
        for f in range(3)
        for l in range(LEVELS)
    ]
    smalls = [
        pltpu.make_async_copy(s, d, small_sem.at[k])
        for k, (s, d) in enumerate(
            (
                (moves, mv),
                (courant, ks),
                (diffuse, qs),
                (east_band, eb),
                (east_index, ei),
                (east_weight, ew),
                (north_band, nb),
                (north_index, ni),
                (north_weight, nw),
            )
        )
    ]
    for c in loads + smalls:
        c.start()

    def wait_load(j, f):
        block = ext.at[j, f, 0:ROWS]
        pltpu.make_async_copy(block, block, in_sem.at[3 * j + f]).wait()

    for j in (0, 2):
        for f in range(3):
            wait_load(j, f)

    lane = iota()
    part = lane & 15
    ext_rows = ext.reshape(9 * SPAN * LEVELS, LANES)

    def edge_windows(t):
        for f in range(3):
            low, high = None, None
            for l in range(LEVELS):
                at = (f * SPAN + 8 * t) * LEVELS + l
                head = ext_rows[pl.ds(at, 8, stride=LEVELS), :]
                tail = ext_rows[pl.ds(at + 6 * SPAN * LEVELS, 8, stride=LEVELS), :]
                v = roll(jnp.where(lane < 64, head, tail), 16 * l + 4)
                low = v if low is None else jnp.where((lane >> 4) == l, v, low)
                high = v if high is None else jnp.where((((lane + 8) >> 4) & 7) == l, v, high)
            gl[f, 8 * t : 8 * t + 8] = low
            gr[f, 8 * t : 8 * t + 8] = high

    for t in range(3):
        edge_windows(t)
        for d, (source, shift) in enumerate(((gl, -4), (gr, 0))):
            v = roll(source[0, 8 * t : 8 * t + 8], shift)
            for f in range(1, 3):
                v = jnp.where((part >> 2) == f, roll(source[f, 8 * t : 8 * t + 8], 4 * f + shift), v)
            to_y[d, t] = v
    for c in smalls:
        c.wait()

    shift_x = mv[0, 0]
    shift_y = mv[0, 1]
    side_x = jnp.where(west, 0, 1)
    side_y = jnp.where(south, 0, 1)
    out_x = shift_x == 2 * side_x - 1
    out_y = shift_y == 2 * side_y - 1
    by_y = jnp.where(out_x, shift_y, 0)
    by_x = jnp.where(out_y, shift_x, 0)

    def east_rows():
        cell = iota(1, (1, WIDE))
        index = jnp.where(side_x == 0, ei[0:1, :], ei[1:2, :])
        upper = (index - (gy * LANES + third(cell)) + 1).astype(F32)
        weight = jnp.where(side_x == 0, ew[0:1, :], ew[1:2, :])
        wide = (LEVELS, WIDE)
        return jnp.broadcast_to(upper, wide), jnp.broadcast_to(weight, wide)

    def east_parents(b, f):
        return eb[pl.ds(side_x * 48 + f * 16 + b, LEVELS, stride=2), :]

    def north_parents(b, f):
        return nbw[pl.ds(side_y * 48 + f * 16 + b, LEVELS, stride=2), :]

    @pl.when(x_edge)
    def _():
        acc = jnp.zeros(TILE, F32)
        for b in range(2):
            for f in range(3):
                k = 3 * b + f
                near = (((lane - 8 * k + 4) & 127) >> 3) == 0
                acc = jnp.where(near, roll(east_parents(b, f), 8 * k), acc)
        east_out[0] = acc
        rows = [jnp.where(lane < 64, v[:, 0:LANES], v[:, 2 * LANES : WIDE]) for v in east_rows()]
        east_out[1] = jnp.where(iota(0) == 0, rows[0], rows[1])

    @pl.when(y_edge)
    def _():
        nbw[...] = jnp.zeros((96, LANES), F32)
        nbw[:, 0:8] = nb[...]
        cell = iota(1, (2, ROWS))
        ntab[...] = jnp.zeros(TILE, F32)
        ntab[0:2, 0:ROWS] = (ni[...] - (gx * 8 + third(cell)) + 1).astype(F32)
        ntab[2:4, 0:ROWS] = nw[...]
        acc = jnp.zeros(TILE, F32)
        for b in range(2):
            for f in range(3):
                k = 3 * b + f
                acc = jnp.where((lane >> 3) == k, roll(north_parents(b, f), 8 * k), acc)
        north_out[0] = acc
        north_out[1] = ntab[...]

    def to(dx, dy, src, dst, send, recv):
        return pltpu.make_async_remote_copy(
            src_ref=src,
            dst_ref=dst,
            send_sem=send,
            recv_sem=recv,
            device_id=(gx + dx, gy + dy),
            device_id_type=MESH,
        )

    y_sends = {}
    for s, dy in enumerate((-1, 1)):
        group = [(has(0, dy), to(0, dy, to_y.at[s], from_y.at[1 - s], y_send.at[s], y_recv.at[1 - s]), has(0, -dy))]
        for a, dx in enumerate((-1, 1)):
            c = to(dx, dy, to_y.at[s, 2 * a], from_d.at[1 - a, 1 - s], d_send.at[2 * a + s], d_recv.at[2 * (1 - a) + 1 - s])
            group.append((has(dx, dy), c, has(-dx, -dy)))
        c = to(0, dy, east_out, east_in.at[1 - s], ea_send.at[s], ea_recv.at[1 - s])
        group.append((both(x_edge, has(0, dy)), c, both(x_edge, has(0, -dy))))
        y_sends[dy] = group
    x_sends = []
    north_sends = []
    for a, dx in enumerate((-1, 1)):
        for f in range(3):
            n = X_ROWS[f]
            if dx < 0:
                src, dst = ext.at[:, f, 0:n], ext.at[:, f, ROWS : ROWS + n]
            else:
                src, dst = ext.at[:, f, ROWS - n : ROWS], ext.at[:, f, SPAN - n : SPAN]
            c = to(dx, 0, src, dst, x_send.at[3 * a + f], x_recv.at[3 * (1 - a) + f])
            x_sends.append((has(dx, 0), c, has(-dx, 0)))
        c = to(dx, 0, north_out, north_in.at[1 - a], na_send.at[a], na_recv.at[1 - a])
        north_sends.append((both(y_edge, has(dx, 0)), c, both(y_edge, has(-dx, 0))))

    def start(group, extra=None):
        for there, c, _ in group:

            @pl.when(there if extra is None else both(there, extra))
            def _(c=c):
                c.start()

    def wait_recv(group):
        for _, c, there in group:

            @pl.when(there)
            def _(c=c):
                c.wait_recv()

    count_x = 1 + has_x[-1].astype(I32) + has_x[1].astype(I32)
    count_y = 1 + has_y[-1].astype(I32) + has_y[1].astype(I32)

    for f in range(3):
        wait_load(1, f)

    @pl.when(at_upper)
    def _():
        pl.semaphore_wait(barrier, count_x)
        start(y_sends[-1])

    @pl.when(jnp.logical_not(at_mid))
    def _():
        pl.semaphore_wait(barrier, count_x * count_y - 1)

        @pl.when(gy == lower_mid - 1)
        def _():
            pl.semaphore_signal(ready, inc=1, device_id=(gx, gy + 1), device_id_type=MESH)

        @pl.when(gy == upper_mid + 1)
        def _():
            pl.semaphore_signal(ready, inc=1, device_id=(gx, gy - 1), device_id_type=MESH)

        start(y_sends[-1])
        start(y_sends[1])
        start(north_sends)
        start(x_sends)

    def spread(values, level, scale):
        v = jnp.zeros(TILE, F32)
        for l in range(LEVELS):
            v = jnp.where(level == l, scale * values[l], v)
        return v

    level = iota(0)
    half = spread(ks, level, 0.5)
    visc = spread(qs, level, 1.0)
    half_w = jnp.concatenate([half] * 3, axis=1)
    visc_w = jnp.concatenate([visc] * 3, axis=1)
    nat_rows = nat.reshape(9 * ROWS * LEVELS, LANES)

    def in_first(r):
        x = gx * ROWS + r
        return jnp.where(both(x >= 3 * shift_x, x < total_x + 3 * shift_x), 1.0, 0.0).astype(F32)

    def in_second(r):
        x = gx * ROWS + r
        return jnp.where(both(x >= 0, x < total_x), 1.0, 0.0).astype(F32)

    def load_ext(f, r):
        return jnp.concatenate([ext[j, f, r % SPAN] for j in range(3)], axis=1)

    def load_mid(f, r):
        return mid[f, r % SPAN]

    def store_mid(f, r, v):
        mid[f, r % SPAN] = v

    def store_nat(f, r, v):
        for j in range(3):
            at = (3 * j + f) * LEVELS * ROWS + r
            nat_rows[pl.ds(at, LEVELS, stride=ROWS), :] = v[:, LANES * j : LANES * j + LANES]

    def substep_1(lo, hi, kk_row):
        advance(load_ext, store_mid, lo, hi, half_w, kk_row, visc_w)

    def substep_2(lo, hi, kk_row):
        advance(load_mid, store_nat, lo, hi, half_w, kk_row, visc_w)

    def everywhere(r):
        return half_w

    substep_1(5, 19, everywhere)
    substep_2(7, 17, everywhere)

    @pl.when(at_mid)
    def _():
        pl.semaphore_wait(ready, 1)
        start(x_sends)
        start(y_sends[-1], at_lower)
        start(y_sends[1], at_upper)
        start(north_sends)

    @pl.when(at_lower)
    def _():
        pl.semaphore_wait(barrier, count_x)
        start(y_sends[1])

    def blend(parents, base, upper, weight, by):
        c0 = (1.0 - upper) * (1.0 - weight)
        c1 = (1.0 - upper) * weight + upper * (1.0 - weight)
        c2 = upper * weight
        values = []
        for v in parents:
            v = pick_shift(v, by, 1)
            values.append(c0 * take(v, base - 1) + c1 * take(v, base) + c2 * take(v, base + 1))
        return values

    def outward(c):
        return jnp.where(side_x > 0, (2.0 * c + 1.0) / 6.0, (5.0 - 2.0 * c) / 6.0).astype(F32)

    @pl.when(x_edge)
    def _():
        upper, weight = east_rows()
        upper = pick_shift(upper, by_y, 3)
        weight = pick_shift(weight, by_y, 3)
        for j in range(3):
            cut = slice(LANES * j, LANES * j + LANES)
            base = third(lane + LANES * j)
            for f in range(3):
                inner, outer = blend([east_parents(b, f) for b in range(2)], base, upper[:, cut], weight[:, cut], by_y)
                for c in range(3):
                    a = outward(c)
                    strip[c, f, :, cut] = inner * (1.0 - a) + outer * a

    tall = (SPAN, LANES)
    row = iota(0, tall)
    row = jnp.where(row < SPAN - HALO, row, row - SPAN) + gx * ROWS
    part_t = iota(1, tall) & 15
    in_x1 = (row >= 3 * shift_x) & (row < total_x + 3 * shift_x)
    in_x2 = (row >= 0) & (row < total_x)
    sides = []
    for window, origin in (((lane >> 4), -HALO), (((lane + 8) >> 4) & 7, WIDE - 12)):
        k = spread(ks, window, 0.5)
        q = spread(qs, window, 1.0)
        k = jnp.concatenate([k] * 4, axis=0)
        q = jnp.concatenate([q] * 4, axis=0)
        y = (part_t if origin < 0 else ((part_t + 8) & 15)) + (origin + gy * WIDE)
        in_y = (y >= 0) & (y < total_y)
        first = in_x1 & (y >= 3 * shift_y) & (y < total_y + 3 * shift_y)
        second = in_x2 & in_y
        sides.append((k, q, first, second, jnp.where(first, k, 0.0), jnp.where(second, k, 0.0), in_y))

    wait_recv(x_sends)

    sides_x = ((west, 29, 0, 28, (30, 31)), (east, 24, 21, 27, (24, 25)))
    for there, beyond, own, zero, _ in sides_x:

        @pl.when(there)
        def _(beyond=beyond, own=own, zero=zero):
            for f in range(3):
                for j in range(3):
                    cut = slice(LANES * j, LANES * j + LANES)
                    ext[j, f, zero] = jnp.zeros(TILE, F32)
                    for c in range(3):
                        ext[j, f, beyond + c] = jnp.where(out_x, strip[c, f, :, cut], 0.0)
                        ext[j, f, own + c] = jnp.where(out_x, ext[j, f, own + c], 0.0)

    edge_windows(3)

    def first_rows(r):
        return half_w * in_first(r)

    def second_rows(r):
        return half_w * in_second(r)

    substep_1(-2, 5, first_rows)
    substep_1(19, 26, first_rows)
    for there, _, own, _, outside in sides_x:

        @pl.when(there)
        def _(own=own, outside=outside):
            for f in range(3):
                for r in outside:
                    mid[f, r] = jnp.zeros((LEVELS, WIDE), F32)
                for c in range(3):
                    mid[f, own + c] = jnp.where(out_x, mid[f, own + c], strip[c, f])

    substep_2(0, 7, second_rows)
    substep_2(17, 24, second_rows)

    @pl.when(y_edge)
    def _():
        wait_recv(north_sends)
        lower_band = jnp.where(has_x[-1], north_in[0, 0], 0.0)
        upper_band = jnp.where(has_x[1], north_in[1, 0], 0.0)
        lower_tab = jnp.where(has_x[-1], north_in[0, 1], 0.0)
        upper_tab = jnp.where(has_x[1], north_in[1, 1], 0.0)
        tab = jnp.where(
            lane >= 112,
            roll(lower_tab, 128 - ROWS),
            jnp.where((lane >= ROWS) & (lane < 2 * ROWS), roll(upper_tab, ROWS), ntab[...]),
        )
        tab = pick_shift(tab, by_x, 3)
        parents = []
        for b in range(2):
            for f in range(3):
                k = 3 * b + f
                v = jnp.where((lane >= 8) & (lane < 16), roll(upper_band, 8 - 8 * k), north_parents(b, f))
                parents.append(jnp.where(lane >= 120, roll(lower_band, -8 - 8 * k), v))
        place = lane & 7
        slot = slots()
        step = jnp.where(place < 4, place, place - 5).astype(F32)
        a = jnp.where(place < 4, (2.0 * step + 1.0) / 6.0, (5.0 - 2.0 * step) / 6.0)
        real = (place != 3) & (place != 4)
        for h in range(2):
            x = slot + (16 * h - HALO)
            base = third(x)
            tab_x = take(tab, x)
            upper = jnp.broadcast_to(jnp.where(side_y == 0, tab_x[0:1], tab_x[1:2]), TILE)
            weight = jnp.broadcast_to(jnp.where(side_y == 0, tab_x[2:3], tab_x[3:4]), TILE)
            whole = x + gx * ROWS - 3 * by_x
            fits = real & (whole >= 0) & (whole < total_x)
            values = blend(parents, base, upper, weight, by_x)
            for f in range(3):
                v = jnp.where(fits, values[f] * (1.0 - a) + values[3 + f] * a, 0.0)
                ns[h, f] = jnp.where(north, roll(v, -64), roll(v, -124))
        for r in range(SPAN):
            h, i = divmod(r, 16)
            for f in range(3):
                ns_stage[f, (r - HALO) % SPAN] = roll(ns[h, f], -8 * i)
        staged = ns_stage.reshape(3 * SPAN * LEVELS, LANES)
        for t in range(4):
            v = jnp.zeros(TILE, F32)
            for f in range(3):
                for l in range(LEVELS):
                    rows = staged[pl.ds((f * SPAN + 8 * t) * LEVELS + l, 8, stride=LEVELS), :]
                    v = jnp.where((lane >> 2) == 4 * l + f, roll(rows, 16 * l + 4 * f), v)
            nsa[t] = v

    wait_recv(y_sends[-1])
    wait_recv(y_sends[1])

    @pl.when(x_edge)
    def _():
        lower_band = jnp.where(has_y[-1], east_in[0, 0], 0.0)
        upper_band = jnp.where(has_y[1], east_in[1, 0], 0.0)
        lower_tab = jnp.where(has_y[-1], east_in[0, 1], 0.0)
        upper_tab = jnp.where(has_y[1], east_in[1, 1], 0.0)
        tabs = east_rows()
        for s in range(2):
            near = []
            for k in range(2):
                if s == 0:
                    v = jnp.where(lane >= 112, jnp.broadcast_to(lower_tab[k : k + 1], TILE), tabs[k][:, 0:LANES])
                else:
                    v = jnp.where(lane < 16, jnp.broadcast_to(upper_tab[k : k + 1], TILE), tabs[k][:, 2 * LANES : WIDE])
                near.append(pick_shift(v, by_y, 3))
            cell = jnp.where(lane < 64, lane, lane - LANES) + (WIDE if s else 0)
            base = third(cell)
            for f in range(3):
                parents = []
                for b in range(2):
                    k = 3 * b + f
                    own = east_parents(b, f)
                    if s == 0:
                        v = jnp.where(lane >= 124, roll(lower_band, -8 * k), own)
                    else:
                        v = jnp.where(lane < 4, roll(upper_band, -8 * k), own)
                    parents.append(v)
                inner, outer = blend(parents, base, near[0], near[1], by_y)
                for c in range(3):
                    a = outward(c)
                    v = inner * (1.0 - a) + outer * a
                    stage[s, f, c] = v
                    stage[s, f, 5 + c] = v
                for c in (3, 4):
                    stage[s, f, c] = jnp.zeros(TILE, F32)
        staged = stage.reshape(2 * 3 * 8 * LEVELS, LANES)
        for s in range(2):
            for f in range(3):
                acc = None
                for l in range(LEVELS):
                    v = roll(staged[pl.ds((s * 3 + f) * 8 * LEVELS + l, 8, stride=LEVELS), :], 16 * l + 4)
                    window = (lane >> 4) if s == 0 else (((lane + 8) >> 4) & 7)
                    acc = v if acc is None else jnp.where(window == l, v, acc)
                sg[s, f] = acc

    sub = iota(0)
    outer_side = both(x_edge, True)
    beyond_rows = jnp.where(west, 1, 0) * (sub >= 4).astype(I32) + jnp.where(east, 1, 0) * (sub < 4).astype(I32) > 0
    own_low = both(both(west, jnp.logical_not(out_x)), outer_side)
    own_high = both(both(east, jnp.logical_not(out_x)), outer_side)
    results = []
    for s, source in enumerate((gl, gr)):
        k, q, first, second, k1, k2, in_y = sides[s]
        absent = south if s == 0 else north
        take_strip = both(absent, out_y)
        lay_strip = both(absent, jnp.logical_not(out_y))
        head = jnp.where(sub < 4, from_d[1, s], from_d[0, s])
        arrived = jnp.concatenate([from_y[s, 0], from_y[s, 1], from_y[s, 2], head], axis=0)
        packed = jnp.concatenate([nsa[t] for t in range(4)], axis=0)
        arrived = jnp.where(absent, packed, arrived)
        halo = (part_t < 4) if s == 0 else ((part_t >= 4) & (part_t < 8))
        state = []
        for f in range(3):
            v = jnp.where(halo, roll(arrived, -4 * f + 4 * s), source[f])
            tip = jnp.where(beyond_rows & in_y[0:8], sg[s, f], v[24:32])
            v = jnp.concatenate([v[0:24], tip], axis=0)
            state.append(jnp.where(first, v, 0.0))
        state = edge_substep(state, k1, k, q)
        if s == 0:
            own_strip = (part_t >= 4) & (part_t < 7)
        else:
            own_strip = (part_t >= 1) & (part_t < 4)
        own_strip = own_strip & lay_strip
        laid = []
        for f in range(3):
            v = state[f]
            low = jnp.where((sub < 3) & own_low, sg[s, f], v[0:8])
            high = jnp.where((sub >= 5) & own_high, sg[s, f], v[16:24])
            v = jnp.concatenate([low, v[8:16], high, v[24:32]], axis=0)
            v = jnp.where(own_strip, roll(packed, -4 * f + (3 if s == 0 else 1)), v)
            laid.append(jnp.where(second, v, 0.0))
        results.append(edge_substep(laid, k2, k, q))

    part_r = iota(1, (ROWS, LANES)) & 15
    lane_r = iota(1, (ROWS, LANES))
    for f in range(3):
        v = jnp.where((part_r >= 4) & (part_r < 12), results[0][f][0:ROWS], results[1][f][0:ROWS])
        for l in range(LEVELS):
            m = roll(v, -16 * l - 4)
            nat[0, f, l] = jnp.where(lane_r < 8, m, nat[0, f, l])
            nat[2, f, l] = jnp.where(lane_r >= 120, m, nat[2, f, l])

    for there, c, _ in y_sends[-1] + y_sends[1] + x_sends + north_sends:

        @pl.when(there)
        def _(c=c):
            c.wait_send()


def write_kernel(ready, out, sem):
    copies = [
        pltpu.make_async_copy(ready.at[j, f], out.at[f, :, :, LANES * j : LANES * j + LANES], sem.at[3 * j + f])
        for j in range(3)
        for f in range(3)
    ]
    for c in copies:
        c.start()
    for c in copies:
        c.wait()


def body(
    sizes,
    fields,
    east_band,
    north_band,
    east_index,
    north_index,
    east_weight,
    north_weight,
    nest_moves,
    courant,
    diffuse,
):
    vmem = pltpu.VMEM
    dma = pltpu.SemaphoreType.DMA
    ready = pl.pallas_call(
        functools.partial(exchange_kernel, sizes),
        out_shape=vmem((3, 3, LEVELS, ROWS, LANES), F32),
        in_specs=[pl.BlockSpec(memory_space=pl.ANY)] * 10,
        out_specs=pl.BlockSpec(memory_space=pltpu.VMEM),
        scratch_shapes=[
            vmem((3, 3, SPAN) + TILE, F32),
            vmem((3, SPAN, LEVELS, WIDE), F32),
            vmem((3, SPAN, LANES), F32),
            vmem((3, SPAN, LANES), F32),
            vmem((2, 3) + TILE, F32),
            vmem((2, 3) + TILE, F32),
            vmem((2, 2) + TILE, F32),
            vmem((2,) + TILE, F32),
            vmem((2, 2) + TILE, F32),
            vmem((2,) + TILE, F32),
            vmem((2, 2) + TILE, F32),
            vmem((3, 3, LEVELS, WIDE), F32),
            vmem((2, 3, 8) + TILE, F32),
            vmem((2, 3) + TILE, F32),
            vmem((2, 3) + TILE, F32),
            vmem((3, SPAN) + TILE, F32),
            vmem((4,) + TILE, F32),
            vmem((96, LANES), F32),
            vmem((2, WIDE), I32),
            vmem((2, WIDE), F32),
            vmem((96, 8), F32),
            vmem((96, LANES), F32),
            vmem((2, ROWS), I32),
            vmem((2, ROWS), F32),
            vmem(TILE, F32),
            pltpu.SMEM((2, 2), I32),
            pltpu.SMEM((LEVELS,), F32),
            pltpu.SMEM((LEVELS,), F32),
            dma((9,)),
            dma((9,)),
            dma((6,)),
            dma((6,)),
            dma((2,)),
            dma((2,)),
            dma((4,)),
            dma((4,)),
            dma((2,)),
            dma((2,)),
            dma((2,)),
            dma((2,)),
            pltpu.SemaphoreType.REGULAR,
        ],
        compiler_params=pltpu.CompilerParams(
            collective_id=0, has_side_effects=True, vmem_limit_bytes=VMEM_A
        ),
    )(
        fields,
        east_band.reshape(96, LANES),
        north_band.reshape(96, 8),
        east_index,
        north_index,
        east_weight,
        north_weight,
        nest_moves,
        courant,
        diffuse,
    )
    return pl.pallas_call(
        write_kernel,
        out_shape=jax.ShapeDtypeStruct(fields.shape, F32),
        in_specs=[pl.BlockSpec(memory_space=pltpu.VMEM)],
        out_specs=pl.BlockSpec(memory_space=pl.ANY),
        scratch_shapes=[dma((9,))],
        compiler_params=pltpu.CompilerParams(vmem_limit_bytes=VMEM_B),
    )(ready)


VMEM_A = 56 * 1024 * 1024
VMEM_B = 8 * 1024 * 1024


def solution(mesh):
    sizes = (mesh.shape["gx"], mesh.shape["gy"])
    return jax.shard_map(
        functools.partial(body, sizes),
        mesh=mesh,
        in_specs=(
            P(None, None, "gx", "gy"),
            P(None, None, None, None, "gy"),
            P(None, None, None, None, "gx"),
            P(None, "gy"),
            P(None, "gx"),
            P(None, "gy"),
            P(None, "gx"),
            P(),
            P(),
            P(),
        ),
        out_specs=P(None, None, "gx", "gy"),
        check_vma=False,
    )
```

```python
import functools

import jax
import jax.numpy as jnp
from jax import lax
from jax.experimental import pallas as pl
from jax.experimental.pallas import tpu as pltpu
from jax.sharding import PartitionSpec as P

MESH = pl.DeviceIdType.MESH
F32 = jnp.float32
I32 = jnp.int32
HALO = 4
ROWS = 24
SPAN = ROWS + 2 * HALO
WIDE = 384
LANES = 128
LEVELS = 8
X_ROWS = (4, 3, 2)
TILE = (LEVELS, LANES)


def third(v):
    return (((v + 48) * 43691) >> 17) - 16


def roll(v, by):
    by = by % v.shape[1]
    return pltpu.roll(v, by, 1) if by else v


def roll_rows(v, by):
    return pltpu.roll(v, by % v.shape[0], 0)


def iota(axis=1, shape=TILE):
    return lax.broadcasted_iota(I32, shape, axis)


def take(v, at):
    return jnp.take_along_axis(v, at & (LANES - 1), axis=1)


def pick_shift(v, by, step):
    return jnp.where(by > 0, roll(v, step), jnp.where(by < 0, roll(v, -step), v))


def slots():
    lane = iota()
    return jnp.where((lane & 7) < 4, ((lane + 64) & 127) >> 3, ((lane + 4) & 127) >> 3)


def advance(load, store, lo, count, kk, kk_row, visc):
    def first(r, p_below, p_here, p_above):
        k = kk_row(r)
        u = load(1, r) - k * (p_above - p_below)
        v = load(2, r) - k * (roll(p_here, -1) - roll(p_here, 1))
        return u, v

    p = [load(0, lo - 2 + i) for i in range(4)]
    ub, vb = first(lo - 1, p[0], p[1], p[2])
    u0, v0 = first(lo, p[1], p[2], p[3])
    p0, p1 = p[2], p[3]
    for step in range(count):
        r = lo + step
        p2 = load(0, r + 2)
        ua, va = first(r + 1, p0, p1, p2)
        un, us, vn, vs = roll(u0, -1), roll(u0, 1), roll(v0, -1), roll(v0, 1)
        store(0, r, p0 - kk * ((ua - ub) + (vn - vs)))
        store(1, r, u0 + visc * (((ua + ub) + (un + us)) - 4.0 * u0))
        store(2, r, v0 + visc * (((va + vb) + (vn + vs)) - 4.0 * v0))
        p0, p1, ub, u0, vb, v0 = p1, p2, u0, ua, v0, va


def edge_substep(fields, kk_in, kk, visc, keep):
    p, u, v = fields
    u = u - kk_in * (roll_rows(p, -1) - roll_rows(p, 1))
    v = v - kk_in * (roll(p, -1) - roll(p, 1))
    ue, uw = roll_rows(u, -1)[0:keep], roll_rows(u, 1)[0:keep]
    ve, vw = roll_rows(v, -1)[0:keep], roll_rows(v, 1)[0:keep]
    p, u, v, kk, visc = p[0:keep], u[0:keep], v[0:keep], kk[0:keep], visc[0:keep]
    vn, vs = roll(v, -1), roll(v, 1)
    p = p - kk * ((ue - uw) + (vn - vs))
    u2 = u + visc * (((ue + uw) + (roll(u, -1) + roll(u, 1))) - 4.0 * u)
    v2 = v + visc * (((ve + vw) + (vn + vs)) - 4.0 * v)
    return p, u2, v2


def exchange_kernel(
    sizes,
    fields,
    east_band,
    north_band,
    east_index,
    north_index,
    east_weight,
    north_weight,
    moves,
    courant,
    diffuse,
    nat,
    ext,
    mid,
    g,
    to_y,
    from_y,
    from_d,
    east_out,
    east_in,
    north_out,
    north_in,
    strip,
    stage,
    sg,
    ns,
    ns_stage,
    nso,
    hop,
    mask,
    factor,
    done,
    eb,
    ei,
    ew,
    nb,
    nbw,
    ni,
    nw,
    ntab,
    mv,
    ks,
    qs,
    in_sem,
    small_sem,
    x_send,
    x_recv,
    y_send,
    y_recv,
    d_send,
    d_recv,
    ea_send,
    ea_recv,
    na_send,
    na_recv,
    ready,
    h_send,
    h_recv,
):
    nx, ny = sizes
    gx = lax.axis_index("gx")
    gy = lax.axis_index("gy")
    total_x = nx * ROWS
    total_y = ny * WIDE
    upper_mid = ny // 2
    lower_mid = upper_mid - 1
    west, east = gx == 0, gx == nx - 1
    south, north = gy == 0, gy == ny - 1
    x_edge = jnp.logical_or(west, east)
    y_edge = jnp.logical_or(south, north)
    has_x = {-1: gx > 0, 1: gx < nx - 1}
    has_y = {-1: gy > 0, 1: gy < ny - 1}
    at_lower = gy == lower_mid
    at_upper = gy == upper_mid
    at_mid = jnp.logical_or(at_lower, at_upper)

    def both(a, b):
        return jnp.logical_and(a, b)

    def has(dx, dy):
        if dx and dy:
            return both(has_x[dx], has_y[dy])
        return has_x[dx] if dx else has_y[dy]

    def over(dy):
        return at_lower if dy > 0 else at_upper

    odd = lax.rem(gx, 2) == 1
    even = jnp.logical_not(odd)
    is_far = {-1: even, 1: odd}
    has_far = jnp.where(odd, has_x[1].astype(I32), has_x[-1].astype(I32))

    barrier = pltpu.get_barrier_semaphore()

    def greet(dx, dy, there):
        @pl.when(both(has(dx, dy), there))
        def _():
            pl.semaphore_signal(barrier, inc=1, device_id=(gx + dx, gy + dy), device_id_type=MESH)

    for dy in (1, -1):
        for dx in (-1, 1, 0):
            greet(dx, dy, both(over(dy), is_far[dx]) if dx and dy < 0 else over(dy))
    for dy in (1, -1):
        to_mid = (gy + dy == lower_mid) if dy > 0 else (gy + dy == upper_mid)
        for dx in (-1, 1, 0):
            greet(dx, dy, jnp.logical_not(jnp.logical_or(over(dy), to_mid)))
    for dx in (-1, 1):
        greet(dx, 0, jnp.logical_not(at_mid))

    loads = [
        pltpu.make_async_copy(
            fields.at[f, l, :, LANES * j : LANES * j + LANES], ext.at[j, f, 0:ROWS, l, :], in_sem.at[3 * j + f]
        )
        for j in (0, 2, 1)
        for f in range(3)
        for l in range(LEVELS)
    ]
    smalls = [
        pltpu.make_async_copy(s, d, small_sem.at[k])
        for k, (s, d) in enumerate(
            (
                (moves, mv),
                (courant, ks),
                (diffuse, qs),
                (east_band, eb),
                (east_index, ei),
                (east_weight, ew),
                (north_band, nb),
                (north_index, ni),
                (north_weight, nw),
            )
        )
    ]
    for c in loads + smalls:
        c.start()

    def wait_load(j, f):
        block = ext.at[j, f, 0:ROWS]
        pltpu.make_async_copy(block, block, in_sem.at[3 * j + f]).wait()

    for j in (0, 2):
        for f in range(3):
            wait_load(j, f)

    lane = iota()
    part = lane & 15
    ext_rows = ext.reshape(9 * SPAN * LEVELS, LANES)

    def edge_windows(t):
        for f in range(3):
            low, high = None, None
            for l in range(LEVELS):
                at = (f * SPAN + 8 * t) * LEVELS + l
                head = ext_rows[pl.ds(at, 8, stride=LEVELS), :]
                tail = ext_rows[pl.ds(at + 6 * SPAN * LEVELS, 8, stride=LEVELS), :]
                v = roll(jnp.where(lane < 64, head, tail), 16 * l + 4)
                low = v if low is None else jnp.where((lane >> 4) == l, v, low)
                high = v if high is None else jnp.where((((lane + 8) >> 4) & 7) == l, v, high)
            g[0, f, 8 * t : 8 * t + 8] = low
            g[1, f, 8 * t : 8 * t + 8] = high

    for t in range(3):
        edge_windows(t)
        for d in range(2):
            v = g[d, 0, 8 * t : 8 * t + 8]
            for f in range(1, 3):
                v = jnp.where((part >> 2) == f + 1 - d, roll(g[d, f, 8 * t : 8 * t + 8], 4 * f), v)
            to_y[d, t] = v
    for c in smalls:
        c.wait()

    shift_x = mv[0, 0]
    shift_y = mv[0, 1]
    side_x = jnp.where(west, 0, 1)
    side_y = jnp.where(south, 0, 1)
    out_x = shift_x == 2 * side_x - 1
    out_y = shift_y == 2 * side_y - 1
    by_y = jnp.where(out_x, shift_y, 0)
    by_x = jnp.where(out_y, shift_x, 0)

    def east_rows():
        cell = iota(1, (1, WIDE))
        index = jnp.where(side_x == 0, ei[0:1, :], ei[1:2, :])
        upper = (index - (gy * LANES + third(cell)) + 1).astype(F32)
        weight = jnp.where(side_x == 0, ew[0:1, :], ew[1:2, :])
        wide = (LEVELS, WIDE)
        return jnp.broadcast_to(upper, wide), jnp.broadcast_to(weight, wide)

    def east_parents(b, f):
        return eb[pl.ds(side_x * 48 + f * 16 + b, LEVELS, stride=2), :]

    def north_parents(b, f):
        return nbw[pl.ds(side_y * 48 + f * 16 + b, LEVELS, stride=2), :]

    @pl.when(x_edge)
    def _():
        acc = jnp.zeros(TILE, F32)
        for b in range(2):
            for f in range(3):
                k = 3 * b + f
                near = (((lane - 8 * k + 4) & 127) >> 3) == 0
                acc = jnp.where(near, roll(east_parents(b, f), 8 * k), acc)
        east_out[0] = acc
        rows = [jnp.where(lane < 64, v[:, 0:LANES], v[:, 2 * LANES : WIDE]) for v in east_rows()]
        east_out[1] = jnp.where(iota(0) == 0, rows[0], rows[1])

    @pl.when(y_edge)
    def _():
        nbw[...] = jnp.zeros((96, LANES), F32)
        nbw[:, 0:8] = nb[...]
        cell = iota(1, (2, ROWS))
        ntab[...] = jnp.zeros(TILE, F32)
        ntab[0:2, 0:ROWS] = (ni[...] - (gx * 8 + third(cell)) + 1).astype(F32)
        ntab[2:4, 0:ROWS] = nw[...]
        acc = jnp.zeros(TILE, F32)
        for b in range(2):
            for f in range(3):
                k = 3 * b + f
                acc = jnp.where((lane >> 3) == k, roll(north_parents(b, f), 8 * k), acc)
        north_out[0] = acc
        north_out[1] = ntab[...]

    def to(dx, dy, src, dst, send, recv):
        return pltpu.make_async_remote_copy(
            src_ref=src,
            dst_ref=dst,
            send_sem=send,
            recv_sem=recv,
            device_id=(gx + dx, gy + dy),
            device_id_type=MESH,
        )

    y_sends = {}
    for s, dy in enumerate((-1, 1)):
        group = []
        for a, dx in enumerate((-1, 1)):
            c = to(dx, dy, to_y.at[s, 2 * a], from_d.at[1 - a, 1 - s], d_send.at[2 * a + s], d_recv.at[2 * (1 - a) + 1 - s])
            there = has(dx, dy)
            if dy > 0:
                there = both(there, jnp.logical_or(is_far[dx], jnp.logical_not(at_lower)))
            group.append((there, c, has(-dx, -dy)))
        c = to(0, dy, to_y.at[s], from_y.at[1 - s], y_send.at[s], y_recv.at[1 - s])
        group.append((has(0, dy), c, has(0, -dy)))
        c = to(0, dy, east_out, east_in.at[1 - s], ea_send.at[s], ea_recv.at[1 - s])
        group.append((both(x_edge, has(0, dy)), c, both(x_edge, has(0, -dy))))
        y_sends[dy] = group
    x_sends = []
    north_sends = []
    for a, dx in enumerate((-1, 1)):
        for f in range(3):
            n = X_ROWS[f]
            if dx < 0:
                src, dst = ext.at[:, f, 0:n], ext.at[:, f, ROWS : ROWS + n]
            else:
                src, dst = ext.at[:, f, ROWS - n : ROWS], ext.at[:, f, SPAN - n : SPAN]
            c = to(dx, 0, src, dst, x_send.at[3 * a + f], x_recv.at[3 * (1 - a) + f])
            x_sends.append((has(dx, 0), c, has(-dx, 0)))
        c = to(dx, 0, north_out, north_in.at[1 - a], na_send.at[a], na_recv.at[1 - a])
        north_sends.append((both(y_edge, has(dx, 0)), c, both(y_edge, has(-dx, 0))))

    side = jnp.where(at_upper, 1, 0)
    east_one = odd.astype(I32)
    mate = 1 - 2 * east_one
    has_mate = jnp.where(odd, has_x[-1].astype(I32), has_x[1].astype(I32)) > 0
    first_hop = to(mate, 0, to_y.at[1, 2 * (1 - east_one)], hop, h_send.at[0], h_recv)
    last_hop = to(0, 1, hop, from_d.at[1 - east_one, 0], h_send.at[1], d_recv.at[2 * (1 - east_one)])

    def start(group, extra=None):
        for there, c, _ in group:

            @pl.when(there if extra is None else both(there, extra))
            def _(c=c):
                c.start()

    def wait_recv(group):
        for _, c, there in group:

            @pl.when(there)
            def _(c=c):
                c.wait_recv()

    count_x = 1 + has_x[-1].astype(I32) + has_x[1].astype(I32)
    count_y = 1 + has_y[-1].astype(I32) + has_y[1].astype(I32)

    for f in range(3):
        wait_load(1, f)

    @pl.when(at_upper)
    def _():
        pl.semaphore_wait(barrier, count_x)
        start(y_sends[-1])

    @pl.when(jnp.logical_not(at_mid))
    def _():
        pl.semaphore_wait(barrier, count_x * count_y - 1)

        @pl.when(gy == lower_mid - 1)
        def _():
            pl.semaphore_signal(ready, inc=1, device_id=(gx, gy + 1), device_id_type=MESH)

        @pl.when(gy == upper_mid + 1)
        def _():
            pl.semaphore_signal(ready, inc=1, device_id=(gx, gy - 1), device_id_type=MESH)

        start(y_sends[-1])
        start(y_sends[1])
        start(north_sends)
        start(x_sends)

    def spread(values, level, scale):
        v = jnp.zeros(TILE, F32)
        for l in range(LEVELS):
            v = jnp.where(level == l, scale * values[l], v)
        return v

    level = iota(0)
    half = spread(ks, level, 0.5)
    visc = spread(qs, level, 1.0)
    half_w = jnp.concatenate([half] * 3, axis=1)
    visc_w = jnp.concatenate([visc] * 3, axis=1)
    nat_rows = nat.reshape(9 * ROWS * LEVELS, LANES)

    def in_first(r):
        x = gx * ROWS + r
        return jnp.where(both(x >= 3 * shift_x, x < total_x + 3 * shift_x), 1.0, 0.0).astype(F32)

    def in_second(r):
        x = gx * ROWS + r
        return jnp.where(both(x >= 0, x < total_x), 1.0, 0.0).astype(F32)

    def load_ext(f, r):
        return jnp.concatenate([ext[j, f, r & (SPAN - 1)] for j in range(3)], axis=1)

    def load_mid(f, r):
        return mid[f, r & (SPAN - 1)]

    def store_mid(f, r, v):
        mid[f, r & (SPAN - 1)] = v

    def store_nat(f, r, v):
        for j in range(3):
            at = (3 * j + f) * LEVELS * ROWS + r
            nat_rows[pl.ds(at, LEVELS, stride=ROWS), :] = v[:, LANES * j : LANES * j + LANES]

    def substep_1(lo, count, kk_row):
        advance(load_ext, store_mid, lo, count, half_w, kk_row, visc_w)

    def substep_2(lo, count, kk_row):
        advance(load_mid, store_nat, lo, count, half_w, kk_row, visc_w)

    def everywhere(r):
        return half_w

    substep_1(5, 14, everywhere)
    substep_2(7, 10, everywhere)

    @pl.when(at_mid)
    def _():
        pl.semaphore_wait(ready, 1)

        @pl.when(both(at_lower, has_mate))
        def _():
            first_hop.start()

        start(x_sends)
        start(y_sends[-1], at_lower)
        start(y_sends[1], at_upper)
        start(north_sends)

    @pl.when(at_lower)
    def _():
        pl.semaphore_wait(barrier, 1 + has_far)
        start(y_sends[1])

        @pl.when(has_mate)
        def _():
            first_hop.wait_recv()
            last_hop.start()

    def blend(parents, base, upper, weight, by):
        c0 = (1.0 - upper) * (1.0 - weight)
        c1 = (1.0 - upper) * weight + upper * (1.0 - weight)
        c2 = upper * weight
        values = []
        for v in parents:
            v = pick_shift(v, by, 1)
            values.append(c0 * take(v, base - 1) + c1 * take(v, base) + c2 * take(v, base + 1))
        return values

    def outward(c):
        return jnp.where(side_x > 0, (2.0 * c + 1.0) / 6.0, (5.0 - 2.0 * c) / 6.0).astype(F32)

    @pl.when(x_edge)
    def _():
        upper, weight = east_rows()
        upper = pick_shift(upper, by_y, 3)
        weight = pick_shift(weight, by_y, 3)
        for j in range(3):
            cut = slice(LANES * j, LANES * j + LANES)
            base = third(lane + LANES * j)
            for f in range(3):
                inner, outer = blend([east_parents(b, f) for b in range(2)], base, upper[:, cut], weight[:, cut], by_y)
                for c in range(3):
                    a = outward(c)
                    strip[c, f, :, cut] = inner * (1.0 - a) + outer * a

    tall = (SPAN, LANES)
    row = iota(0, tall)
    row = jnp.where(row < SPAN - HALO, row, row - SPAN) + gx * ROWS
    part_t = iota(1, tall) & 15
    in_x1 = (row >= 3 * shift_x) & (row < total_x + 3 * shift_x)
    in_x2 = (row >= 0) & (row < total_x)
    for s, (window, origin) in enumerate((((lane >> 4), -HALO), (((lane + 8) >> 4) & 7, WIDE - 12))):
        factor[s, 0] = spread(ks, window, 0.5)
        factor[s, 1] = spread(qs, window, 1.0)
        y = (part_t if origin < 0 else ((part_t + 8) & 15)) + (origin + gy * WIDE)
        in_y = (y >= 0) & (y < total_y)
        mask[s, 0] = jnp.where(in_x1 & (y >= 3 * shift_y) & (y < total_y + 3 * shift_y), 1.0, 0.0)
        mask[s, 1] = jnp.where(in_x2 & in_y, 1.0, 0.0)
        mask[s, 2] = jnp.where(in_y, 1.0, 0.0)

    sides_x = ((west, 29, 0, 28, (30, 31)), (east, 24, 21, 27, (24, 25)))
    for there, beyond, own, zero, _ in sides_x:

        @pl.when(there)
        def _(beyond=beyond, own=own, zero=zero):
            for f in range(3):
                for j in range(3):
                    cut = slice(LANES * j, LANES * j + LANES)
                    ext[j, f, zero] = jnp.zeros(TILE, F32)
                    for c in range(3):
                        ext[j, f, beyond + c] = jnp.where(out_x, strip[c, f, :, cut], 0.0)
                        ext[j, f, own + c] = jnp.where(out_x, ext[j, f, own + c], 0.0)

    def first_rows(r):
        return half_w * in_first(r)

    def second_rows(r):
        return half_w * in_second(r)

    for turn in range(2):
        westward = odd if turn == 0 else even

        @pl.when(westward)
        def _():
            wait_recv(x_sends[3:6])

        @pl.when(jnp.logical_not(westward))
        def _():
            wait_recv(x_sends[0:3])

        if turn == 1:
            edge_windows(3)
        substep_1(jnp.where(westward, -2, 19), 7, first_rows)
        for there, _, own, _, outside in sides_x:

            @pl.when(there)
            def _(own=own, outside=outside):
                for f in range(3):
                    for r in outside:
                        mid[f, r] = jnp.zeros((LEVELS, WIDE), F32)
                    for c in range(3):
                        mid[f, own + c] = jnp.where(out_x, mid[f, own + c], strip[c, f])

        substep_2(jnp.where(westward, 0, 17), 7, second_rows)

    @pl.when(y_edge)
    def _():
        wait_recv(north_sends)
        lower_band = jnp.where(has_x[-1], north_in[0, 0], 0.0)
        upper_band = jnp.where(has_x[1], north_in[1, 0], 0.0)
        lower_tab = jnp.where(has_x[-1], north_in[0, 1], 0.0)
        upper_tab = jnp.where(has_x[1], north_in[1, 1], 0.0)
        tab = jnp.where(
            lane >= 112,
            roll(lower_tab, 128 - ROWS),
            jnp.where((lane >= ROWS) & (lane < 2 * ROWS), roll(upper_tab, ROWS), ntab[...]),
        )
        tab = pick_shift(tab, by_x, 3)
        parents = []
        for b in range(2):
            for f in range(3):
                k = 3 * b + f
                v = jnp.where((lane >= 8) & (lane < 16), roll(upper_band, 8 - 8 * k), north_parents(b, f))
                parents.append(jnp.where(lane >= 120, roll(lower_band, -8 - 8 * k), v))
        place = lane & 7
        slot = slots()
        step = jnp.where(place < 4, place, place - 5).astype(F32)
        a = jnp.where(place < 4, (2.0 * step + 1.0) / 6.0, (5.0 - 2.0 * step) / 6.0)
        real = (place != 3) & (place != 4)
        for h in range(2):
            x = slot + (16 * h - HALO)
            base = third(x)
            tab_x = take(tab, x)
            upper = jnp.broadcast_to(jnp.where(side_y == 0, tab_x[0:1], tab_x[1:2]), TILE)
            weight = jnp.broadcast_to(jnp.where(side_y == 0, tab_x[2:3], tab_x[3:4]), TILE)
            whole = x + gx * ROWS - 3 * by_x
            fits = real & (whole >= 0) & (whole < total_x)
            values = blend(parents, base, upper, weight, by_x)
            for f in range(3):
                v = jnp.where(fits, values[f] * (1.0 - a) + values[3 + f] * a, 0.0)
                ns[h, f] = jnp.where(north, roll(v, -60), roll(v, -124))
        for r in range(SPAN):
            h, i = divmod(r, 16)
            for f in range(3):
                ns_stage[f, (r - HALO) % SPAN] = roll(ns[h, f], -8 * i)
        staged = ns_stage.reshape(3 * SPAN * LEVELS, LANES)
        late = jnp.where(north, 1, 0)
        for t in range(4):
            v = jnp.zeros(TILE, F32)
            for f in range(3):
                for l in range(LEVELS):
                    rows = staged[pl.ds((f * SPAN + 8 * t) * LEVELS + l, 8, stride=LEVELS), :]
                    v = jnp.where((lane >> 2) == 4 * l + f + late, roll(rows, 16 * l + 4 * f), v)
            for there, s in ((south, 0), (north, 1)):

                @pl.when(there)
                def _(s=s, t=t, v=v):
                    if t < 3:
                        from_y[s, t] = v
                    else:
                        from_d[0, s] = v
                        from_d[1, s] = v

            for f in range(3):
                nso[f, 8 * t : 8 * t + 8] = jnp.where(north, roll(v, -4 * f - 3), roll(v, -4 * f + 3))

    def east_edge_strip(s):
        band = jnp.where(jnp.where(s == 0, has_y[-1], has_y[1]), east_in[s, 0], 0.0)
        far_tab = jnp.where(jnp.where(s == 0, has_y[-1], has_y[1]), east_in[s, 1], 0.0)
        beyond = ((lane + 64 * s) & 127) >= 64
        near = []
        for k, v in enumerate(east_rows()):
            v = jnp.where(s == 0, v[:, 0:LANES], v[:, 2 * LANES : WIDE])
            v = jnp.where(beyond, jnp.broadcast_to(far_tab[k : k + 1], TILE), v)
            near.append(pick_shift(v, by_y, 3))
        base = third(jnp.where(lane < 64, lane, lane - LANES) + WIDE * s)
        for f in range(3):
            parents = []
            for b in range(2):
                k = 3 * b + f
                parents.append(jnp.where(beyond, roll(band, -8 * k), east_parents(b, f)))
            inner, outer = blend(parents, base, near[0], near[1], by_y)
            for c in range(3):
                a = outward(c)
                v = inner * (1.0 - a) + outer * a
                stage[f, c] = v
                stage[f, 5 + c] = v
            for c in (3, 4):
                stage[f, c] = jnp.zeros(TILE, F32)
        staged = stage.reshape(3 * 8 * LEVELS, LANES)
        window = ((lane + 8 * s) >> 4) & 7
        for f in range(3):
            acc = None
            for l in range(LEVELS):
                v = roll(staged[pl.ds(f * 8 * LEVELS + l, 8, stride=LEVELS), :], 16 * l + 4)
                acc = v if acc is None else jnp.where(window == l, v, acc)
            sg[f] = acc

    sub = iota(0)
    beyond_rows = (jnp.where(west, 1, 0) * (sub >= 4).astype(I32) + jnp.where(east, 1, 0) * (sub < 4).astype(I32)) > 0
    own_low = both(west, jnp.logical_not(out_x))
    own_high = both(east, jnp.logical_not(out_x))

    def edge_side(s):
        @pl.when(x_edge)
        def _():
            east_edge_strip(s)

        k = jnp.concatenate([factor[s, 0]] * 4, axis=0)
        q = jnp.concatenate([factor[s, 1]] * 4, axis=0)
        first = mask[s, 0] > 0.5
        second = mask[s, 1] > 0.5
        in_y = mask[s, 2, 0:8] > 0.5
        lay_strip = both(jnp.where(s == 0, south, north), jnp.logical_not(out_y))
        head = jnp.where(sub < 4, from_d[1, s], from_d[0, s])
        arrived = jnp.concatenate([from_y[s, 0], from_y[s, 1], from_y[s, 2], head], axis=0)
        halo = ((part_t - 4 * s) & 15) < 4
        own_strip = (((part_t - 4 + 3 * s) & 15) < 3) & lay_strip
        state = []
        for f in range(3):
            v = jnp.where(halo, roll(arrived, -4 * f), g[s, f])
            tip = jnp.where(beyond_rows & in_y, sg[f], v[24:32])
            v = jnp.concatenate([v[0:24], tip], axis=0)
            state.append(jnp.where(first, v, 0.0))
        state = edge_substep(state, jnp.where(first, k, 0.0), k, q, SPAN)
        laid = []
        for f in range(3):
            v = state[f]
            low = jnp.where((sub < 3) & own_low, sg[f], v[0:8])
            high = jnp.where((sub >= 5) & own_high, sg[f], v[16:24])
            v = jnp.concatenate([low, v[8:16], high, v[24:32]], axis=0)
            v = jnp.where(own_strip, nso[f], v)
            laid.append(jnp.where(second, v, 0.0))
        return edge_substep(laid, jnp.where(second, k, 0.0), k, q, ROWS)

    @pl.when(at_upper)
    def _():
        wait_recv(y_sends[-1])

    @pl.when(jnp.logical_not(at_upper))
    def _():
        wait_recv(y_sends[1])

    for f, v in enumerate(edge_side(side)):
        done[f] = v

    @pl.when(at_upper)
    def _():
        wait_recv(y_sends[1])

    @pl.when(jnp.logical_not(at_upper))
    def _():
        wait_recv(y_sends[-1])

    lane_r = iota(1, (ROWS, LANES))
    ahead = ((((lane_r & 15) + 12) & 15) < 8).astype(I32)
    fresh = ahead == side
    for f, v in enumerate(edge_side(1 - side)):
        v = jnp.where(fresh, v, done[f])
        for l in range(LEVELS):
            m = roll(v, -16 * l - 4)
            nat[0, f, l] = jnp.where(lane_r < 8, m, nat[0, f, l])
            nat[2, f, l] = jnp.where(lane_r >= 120, m, nat[2, f, l])

    @pl.when(both(at_lower, has_mate))
    def _():
        first_hop.wait_send()
        last_hop.wait_send()

    for there, c, _ in y_sends[-1] + y_sends[1] + x_sends + north_sends:

        @pl.when(there)
        def _(c=c):
            c.wait_send()


def write_kernel(ready, out, sem):
    copies = [
        pltpu.make_async_copy(ready.at[j, f], out.at[f, :, :, LANES * j : LANES * j + LANES], sem.at[3 * j + f])
        for j in range(3)
        for f in range(3)
    ]
    for c in copies:
        c.start()
    for c in copies:
        c.wait()


def body(
    sizes,
    fields,
    east_band,
    north_band,
    east_index,
    north_index,
    east_weight,
    north_weight,
    nest_moves,
    courant,
    diffuse,
):
    vmem = pltpu.VMEM
    dma = pltpu.SemaphoreType.DMA
    ready = pl.pallas_call(
        functools.partial(exchange_kernel, sizes),
        out_shape=vmem((3, 3, LEVELS, ROWS, LANES), F32),
        in_specs=[pl.BlockSpec(memory_space=pl.ANY)] * 10,
        out_specs=pl.BlockSpec(memory_space=pltpu.VMEM),
        scratch_shapes=[
            vmem((3, 3, SPAN) + TILE, F32),
            vmem((3, SPAN, LEVELS, WIDE), F32),
            vmem((2, 3, SPAN, LANES), F32),
            vmem((2, 3) + TILE, F32),
            vmem((2, 3) + TILE, F32),
            vmem((2, 2) + TILE, F32),
            vmem((2,) + TILE, F32),
            vmem((2, 2) + TILE, F32),
            vmem((2,) + TILE, F32),
            vmem((2, 2) + TILE, F32),
            vmem((3, 3, LEVELS, WIDE), F32),
            vmem((3, 8) + TILE, F32),
            vmem((3,) + TILE, F32),
            vmem((2, 3) + TILE, F32),
            vmem((3, SPAN) + TILE, F32),
            vmem((3, SPAN, LANES), F32),
            vmem(TILE, F32),
            vmem((2, 3, SPAN, LANES), F32),
            vmem((2, 2) + TILE, F32),
            vmem((3, ROWS, LANES), F32),
            vmem((96, LANES), F32),
            vmem((2, WIDE), I32),
            vmem((2, WIDE), F32),
            vmem((96, 8), F32),
            vmem((96, LANES), F32),
            vmem((2, ROWS), I32),
            vmem((2, ROWS), F32),
            vmem(TILE, F32),
            pltpu.SMEM((2, 2), I32),
            pltpu.SMEM((LEVELS,), F32),
            pltpu.SMEM((LEVELS,), F32),
            dma((9,)),
            dma((9,)),
            dma((6,)),
            dma((6,)),
            dma((2,)),
            dma((2,)),
            dma((4,)),
            dma((4,)),
            dma((2,)),
            dma((2,)),
            dma((2,)),
            dma((2,)),
            pltpu.SemaphoreType.REGULAR,
            dma((2,)),
            dma,
        ],
        compiler_params=pltpu.CompilerParams(
            collective_id=0, has_side_effects=True, vmem_limit_bytes=VMEM_A
        ),
    )(
        fields,
        east_band.reshape(96, LANES),
        north_band.reshape(96, 8),
        east_index,
        north_index,
        east_weight,
        north_weight,
        nest_moves,
        courant,
        diffuse,
    )
    return pl.pallas_call(
        write_kernel,
        out_shape=jax.ShapeDtypeStruct(fields.shape, F32),
        in_specs=[pl.BlockSpec(memory_space=pltpu.VMEM)],
        out_specs=pl.BlockSpec(memory_space=pl.ANY),
        scratch_shapes=[dma((9,))],
        compiler_params=pltpu.CompilerParams(vmem_limit_bytes=VMEM_B),
    )(ready)


VMEM_A = 56 * 1024 * 1024
VMEM_B = 8 * 1024 * 1024


def solution(mesh):
    sizes = (mesh.shape["gx"], mesh.shape["gy"])
    return jax.shard_map(
        functools.partial(body, sizes),
        mesh=mesh,
        in_specs=(
            P(None, None, "gx", "gy"),
            P(None, None, None, None, "gy"),
            P(None, None, None, None, "gx"),
            P(None, "gy"),
            P(None, "gx"),
            P(None, "gy"),
            P(None, "gx"),
            P(),
            P(),
            P(),
        ),
        out_specs=P(None, None, "gx", "gy"),
        check_vma=False,
    )
```

```python
import functools

import jax
import jax.numpy as jnp
from jax import lax
from jax.experimental import pallas as pl
from jax.experimental.pallas import tpu as pltpu
from jax.sharding import PartitionSpec as P

MESH = pl.DeviceIdType.MESH
F32 = jnp.float32
I32 = jnp.int32
HALO = 4
ROWS = 24
SPAN = ROWS + 2 * HALO
WIDE = 384
LANES = 128
LEVELS = 8
X_ROWS = (4, 3, 2)
RUN = 8
TILE = (LEVELS, LANES)


def third(v):
    return (((v + 48) * 43691) >> 17) - 16


def roll(v, by):
    by = by % v.shape[1]
    return pltpu.roll(v, by, 1) if by else v


def roll_rows(v, by):
    return pltpu.roll(v, by % v.shape[0], 0)


def iota(axis=1, shape=TILE):
    return lax.broadcasted_iota(I32, shape, axis)


def take(v, at):
    return jnp.take_along_axis(v, at & (LANES - 1), axis=1)


def pick_shift(v, by, step):
    return jnp.where(by > 0, roll(v, step), jnp.where(by < 0, roll(v, -step), v))


def slots():
    lane = iota()
    return jnp.where((lane & 7) < 4, ((lane + 64) & 127) >> 3, ((lane + 4) & 127) >> 3)


def advance(load, store, lo, count, kk, kk_row, visc):
    def first(r, p_below, p_here, p_above):
        k = kk_row(r)
        u = load(1, r) - k * (p_above - p_below)
        v = load(2, r) - k * (roll(p_here, -1) - roll(p_here, 1))
        return u, v

    p = [load(0, lo - 2 + i) for i in range(4)]
    ub, vb = first(lo - 1, p[0], p[1], p[2])
    u0, v0 = first(lo, p[1], p[2], p[3])
    p0, p1 = p[2], p[3]
    for step in range(count):
        r = lo + step
        p2 = load(0, r + 2)
        ua, va = first(r + 1, p0, p1, p2)
        un, us, vn, vs = roll(u0, -1), roll(u0, 1), roll(v0, -1), roll(v0, 1)
        store(0, r, p0 - kk * ((ua - ub) + (vn - vs)))
        store(1, r, u0 + visc * (((ua + ub) + (un + us)) - 4.0 * u0))
        store(2, r, v0 + visc * (((va + vb) + (vn + vs)) - 4.0 * v0))
        p0, p1, ub, u0, vb, v0 = p1, p2, u0, ua, v0, va


def edge_substep(fields, kk_in, kk, visc, keep):
    p, u, v = fields
    u = u - kk_in * (roll_rows(p, -1) - roll_rows(p, 1))
    v = v - kk_in * (roll(p, -1) - roll(p, 1))
    ue, uw = roll_rows(u, -1)[0:keep], roll_rows(u, 1)[0:keep]
    ve, vw = roll_rows(v, -1)[0:keep], roll_rows(v, 1)[0:keep]
    p, u, v, kk, visc = p[0:keep], u[0:keep], v[0:keep], kk[0:keep], visc[0:keep]
    vn, vs = roll(v, -1), roll(v, 1)
    p = p - kk * ((ue - uw) + (vn - vs))
    u2 = u + visc * (((ue + uw) + (roll(u, -1) + roll(u, 1))) - 4.0 * u)
    v2 = v + visc * (((ve + vw) + (vn + vs)) - 4.0 * v)
    return p, u2, v2


def exchange_kernel(
    sizes,
    fields,
    east_band,
    north_band,
    east_index,
    north_index,
    east_weight,
    north_weight,
    moves,
    courant,
    diffuse,
    nat,
    ext,
    mid,
    g,
    to_y,
    from_y,
    from_d,
    east_out,
    east_in,
    north_out,
    north_in,
    strip,
    stage,
    sg,
    ns,
    ns_stage,
    nso,
    hop,
    mask,
    factor,
    done,
    eb,
    ei,
    ew,
    nb,
    nbw,
    ni,
    nw,
    ntab,
    mv,
    ks,
    qs,
    in_sem,
    small_sem,
    x_send,
    x_recv,
    y_send,
    y_recv,
    d_send,
    d_recv,
    ea_send,
    ea_recv,
    na_send,
    na_recv,
    ready,
    h_send,
    h_recv,
):
    nx, ny = sizes
    gx = lax.axis_index("gx")
    gy = lax.axis_index("gy")
    total_x = nx * ROWS
    total_y = ny * WIDE
    upper_mid = ny // 2
    lower_mid = upper_mid - 1
    west, east = gx == 0, gx == nx - 1
    south, north = gy == 0, gy == ny - 1
    x_edge = jnp.logical_or(west, east)
    y_edge = jnp.logical_or(south, north)
    has_x = {-1: gx > 0, 1: gx < nx - 1}
    has_y = {-1: gy > 0, 1: gy < ny - 1}
    at_lower = gy == lower_mid
    at_upper = gy == upper_mid
    at_mid = jnp.logical_or(at_lower, at_upper)

    def both(a, b):
        return jnp.logical_and(a, b)

    def has(dx, dy):
        if dx and dy:
            return both(has_x[dx], has_y[dy])
        return has_x[dx] if dx else has_y[dy]

    def over(dy):
        return at_lower if dy > 0 else at_upper

    odd = lax.rem(gx, 2) == 1
    even = jnp.logical_not(odd)
    is_far = {-1: even, 1: odd}
    has_far = jnp.where(odd, has_x[1].astype(I32), has_x[-1].astype(I32))

    seam_west = both(lax.rem(gx, RUN) == 0, gx > 0)
    seam_east = both(lax.rem(gx, RUN) == RUN - 1, gx < nx - 1)

    barrier = pltpu.get_barrier_semaphore()

    def greet(dx, dy, there):
        @pl.when(both(has(dx, dy), there))
        def _():
            pl.semaphore_signal(barrier, inc=1, device_id=(gx + dx, gy + dy), device_id_type=MESH)

    for dy in (1, -1):
        for dx in (-1, 1, 0):
            there = over(dy)
            if dx and dy < 0:
                there = both(there, is_far[dx])
            if dx > 0 and dy < 0:
                there = both(there, jnp.logical_not(seam_east))
            greet(dx, dy, there)
    for dy in (1, -1):
        to_mid = (gy + dy == lower_mid) if dy > 0 else (gy + dy == upper_mid)
        for dx in (-1, 1, 0):
            greet(dx, dy, jnp.logical_not(jnp.logical_or(over(dy), to_mid)))
    for dx in (-1, 1):
        greet(dx, 0, jnp.logical_not(at_mid))

    loads = [
        pltpu.make_async_copy(
            fields.at[f, l, :, LANES * j : LANES * j + LANES], ext.at[j, f, 0:ROWS, l, :], in_sem.at[3 * j + f]
        )
        for j in (0, 2, 1)
        for f in range(3)
        for l in range(LEVELS)
    ]
    smalls = [
        pltpu.make_async_copy(s, d, small_sem.at[k])
        for k, (s, d) in enumerate(
            (
                (moves, mv),
                (courant, ks),
                (diffuse, qs),
                (east_band, eb),
                (east_index, ei),
                (east_weight, ew),
                (north_band, nb),
                (north_index, ni),
                (north_weight, nw),
            )
        )
    ]
    for c in loads + smalls:
        c.start()

    def wait_load(j, f):
        block = ext.at[j, f, 0:ROWS]
        pltpu.make_async_copy(block, block, in_sem.at[3 * j + f]).wait()

    for j in (0, 2):
        for f in range(3):
            wait_load(j, f)

    lane = iota()
    part = lane & 15
    ext_rows = ext.reshape(9 * SPAN * LEVELS, LANES)

    def edge_windows(t):
        for f in range(3):
            low, high = None, None
            for l in range(LEVELS):
                at = (f * SPAN + 8 * t) * LEVELS + l
                head = ext_rows[pl.ds(at, 8, stride=LEVELS), :]
                tail = ext_rows[pl.ds(at + 6 * SPAN * LEVELS, 8, stride=LEVELS), :]
                v = roll(jnp.where(lane < 64, head, tail), 16 * l + 4)
                low = v if low is None else jnp.where((lane >> 4) == l, v, low)
                high = v if high is None else jnp.where((((lane + 8) >> 4) & 7) == l, v, high)
            g[0, f, 8 * t : 8 * t + 8] = low
            g[1, f, 8 * t : 8 * t + 8] = high

    for t in range(3):
        edge_windows(t)
        for d in range(2):
            v = g[d, 0, 8 * t : 8 * t + 8]
            for f in range(1, 3):
                v = jnp.where((part >> 2) == f + 1 - d, roll(g[d, f, 8 * t : 8 * t + 8], 4 * f), v)
            to_y[d, t] = v
    for c in smalls:
        c.wait()

    shift_x = mv[0, 0]
    shift_y = mv[0, 1]
    side_x = jnp.where(west, 0, 1)
    side_y = jnp.where(south, 0, 1)
    out_x = shift_x == 2 * side_x - 1
    out_y = shift_y == 2 * side_y - 1
    by_y = jnp.where(out_x, shift_y, 0)
    by_x = jnp.where(out_y, shift_x, 0)

    def east_rows():
        cell = iota(1, (1, WIDE))
        index = jnp.where(side_x == 0, ei[0:1, :], ei[1:2, :])
        upper = (index - (gy * LANES + third(cell)) + 1).astype(F32)
        weight = jnp.where(side_x == 0, ew[0:1, :], ew[1:2, :])
        wide = (LEVELS, WIDE)
        return jnp.broadcast_to(upper, wide), jnp.broadcast_to(weight, wide)

    def east_parents(b, f):
        return eb[pl.ds(side_x * 48 + f * 16 + b, LEVELS, stride=2), :]

    def north_parents(b, f):
        return nbw[pl.ds(side_y * 48 + f * 16 + b, LEVELS, stride=2), :]

    @pl.when(x_edge)
    def _():
        acc = jnp.zeros(TILE, F32)
        for b in range(2):
            for f in range(3):
                k = 3 * b + f
                near = (((lane - 8 * k + 4) & 127) >> 3) == 0
                acc = jnp.where(near, roll(east_parents(b, f), 8 * k), acc)
        east_out[0] = acc
        rows = [jnp.where(lane < 64, v[:, 0:LANES], v[:, 2 * LANES : WIDE]) for v in east_rows()]
        east_out[1] = jnp.where(iota(0) == 0, rows[0], rows[1])

    @pl.when(y_edge)
    def _():
        nbw[...] = jnp.zeros((96, LANES), F32)
        nbw[:, 0:8] = nb[...]
        cell = iota(1, (2, ROWS))
        ntab[...] = jnp.zeros(TILE, F32)
        ntab[0:2, 0:ROWS] = (ni[...] - (gx * 8 + third(cell)) + 1).astype(F32)
        ntab[2:4, 0:ROWS] = nw[...]
        acc = jnp.zeros(TILE, F32)
        for b in range(2):
            for f in range(3):
                k = 3 * b + f
                acc = jnp.where((lane >> 3) == k, roll(north_parents(b, f), 8 * k), acc)
        north_out[0] = acc
        north_out[1] = ntab[...]

    def to(dx, dy, src, dst, send, recv):
        return pltpu.make_async_remote_copy(
            src_ref=src,
            dst_ref=dst,
            send_sem=send,
            recv_sem=recv,
            device_id=(gx + dx, gy + dy),
            device_id_type=MESH,
        )

    y_sends = {}
    for s, dy in enumerate((-1, 1)):
        group = []
        for a, dx in enumerate((-1, 1)):
            c = to(dx, dy, to_y.at[s, 2 * a], from_d.at[1 - a, 1 - s], d_send.at[2 * a + s], d_recv.at[2 * (1 - a) + 1 - s])
            there = has(dx, dy)
            if dy > 0:
                near = jnp.logical_not(is_far[dx])
                near = jnp.logical_or(near, seam_west) if dx < 0 else near
                there = both(there, jnp.logical_not(both(near, at_lower)))
            group.append((there, c, has(-dx, -dy)))
        c = to(0, dy, to_y.at[s], from_y.at[1 - s], y_send.at[s], y_recv.at[1 - s])
        group.append((has(0, dy), c, has(0, -dy)))
        c = to(0, dy, east_out, east_in.at[1 - s], ea_send.at[s], ea_recv.at[1 - s])
        group.append((both(x_edge, has(0, dy)), c, both(x_edge, has(0, -dy))))
        y_sends[dy] = group
    x_sends = []
    north_sends = []
    for a, dx in enumerate((-1, 1)):
        for f in range(3):
            n = X_ROWS[f]
            if dx < 0:
                src, dst = ext.at[:, f, 0:n], ext.at[:, f, ROWS : ROWS + n]
            else:
                src, dst = ext.at[:, f, ROWS - n : ROWS], ext.at[:, f, SPAN - n : SPAN]
            c = to(dx, 0, src, dst, x_send.at[3 * a + f], x_recv.at[3 * (1 - a) + f])
            x_sends.append((has(dx, 0), c, has(-dx, 0)))
        c = to(dx, 0, north_out, north_in.at[1 - a], na_send.at[a], na_recv.at[1 - a])
        north_sends.append((both(y_edge, has(dx, 0)), c, both(y_edge, has(-dx, 0))))

    side = jnp.where(at_upper, 1, 0)
    east_one = odd.astype(I32)
    mate = 1 - 2 * east_one
    has_mate = jnp.where(odd, has_x[-1].astype(I32), has_x[1].astype(I32)) > 0
    first_hop = to(mate, 0, to_y.at[1, 2 * (1 - east_one)], hop.at[0], h_send.at[0], h_recv.at[0])
    last_hop = to(0, 1, hop.at[0], from_d.at[1 - east_one, 0], h_send.at[1], d_recv.at[2 * (1 - east_one)])
    first_seam_hop = to(-1, 0, to_y.at[1, 0], hop.at[1], h_send.at[2], h_recv.at[1])
    last_seam_hop = to(0, 1, hop.at[1], from_d.at[1, 0], h_send.at[3], d_recv.at[2])

    def start(group, extra=None):
        for there, c, _ in group:

            @pl.when(there if extra is None else both(there, extra))
            def _(c=c):
                c.start()

    def wait_recv(group):
        for _, c, there in group:

            @pl.when(there)
            def _(c=c):
                c.wait_recv()

    count_x = 1 + has_x[-1].astype(I32) + has_x[1].astype(I32)
    count_y = 1 + has_y[-1].astype(I32) + has_y[1].astype(I32)

    for f in range(3):
        wait_load(1, f)

    @pl.when(at_upper)
    def _():
        pl.semaphore_wait(barrier, count_x)
        start(y_sends[-1])

    @pl.when(jnp.logical_not(at_mid))
    def _():
        pl.semaphore_wait(barrier, count_x * count_y - 1)

        @pl.when(gy == lower_mid - 1)
        def _():
            pl.semaphore_signal(ready, inc=1, device_id=(gx, gy + 1), device_id_type=MESH)

        @pl.when(gy == upper_mid + 1)
        def _():
            pl.semaphore_signal(ready, inc=1, device_id=(gx, gy - 1), device_id_type=MESH)

        start(y_sends[-1])
        start(y_sends[1])
        start(north_sends)
        start(x_sends)

    def spread(values, level, scale):
        v = jnp.zeros(TILE, F32)
        for l in range(LEVELS):
            v = jnp.where(level == l, scale * values[l], v)
        return v

    level = iota(0)
    half = spread(ks, level, 0.5)
    visc = spread(qs, level, 1.0)
    half_w = jnp.concatenate([half] * 3, axis=1)
    visc_w = jnp.concatenate([visc] * 3, axis=1)
    nat_rows = nat.reshape(9 * ROWS * LEVELS, LANES)

    def in_first(r):
        x = gx * ROWS + r
        return jnp.where(both(x >= 3 * shift_x, x < total_x + 3 * shift_x), 1.0, 0.0).astype(F32)

    def in_second(r):
        x = gx * ROWS + r
        return jnp.where(both(x >= 0, x < total_x), 1.0, 0.0).astype(F32)

    def load_ext(f, r):
        return jnp.concatenate([ext[j, f, r & (SPAN - 1)] for j in range(3)], axis=1)

    def load_mid(f, r):
        return mid[f, r & (SPAN - 1)]

    def store_mid(f, r, v):
        mid[f, r & (SPAN - 1)] = v

    def store_nat(f, r, v):
        for j in range(3):
            at = (3 * j + f) * LEVELS * ROWS + r
            nat_rows[pl.ds(at, LEVELS, stride=ROWS), :] = v[:, LANES * j : LANES * j + LANES]

    def substep_1(lo, count, kk_row):
        advance(load_ext, store_mid, lo, count, half_w, kk_row, visc_w)

    def substep_2(lo, count, kk_row):
        advance(load_mid, store_nat, lo, count, half_w, kk_row, visc_w)

    def everywhere(r):
        return half_w

    substep_1(5, 14, everywhere)
    substep_2(7, 10, everywhere)

    @pl.when(at_mid)
    def _():
        pl.semaphore_wait(ready, 1)

        @pl.when(both(at_lower, has_mate))
        def _():
            first_hop.start()

        @pl.when(both(at_lower, seam_west))
        def _():
            first_seam_hop.start()

        start(x_sends)
        start(y_sends[-1], at_lower)
        start(y_sends[1], at_upper)
        start(north_sends)

    @pl.when(at_lower)
    def _():
        pl.semaphore_wait(barrier, 1 + has_far - seam_west.astype(I32))
        start(y_sends[1])

        @pl.when(has_mate)
        def _():
            first_hop.wait_recv()
            last_hop.start()

        @pl.when(seam_east)
        def _():
            first_seam_hop.wait_recv()
            last_seam_hop.start()

    def blend(parents, base, upper, weight, by):
        c0 = (1.0 - upper) * (1.0 - weight)
        c1 = (1.0 - upper) * weight + upper * (1.0 - weight)
        c2 = upper * weight
        values = []
        for v in parents:
            v = pick_shift(v, by, 1)
            values.append(c0 * take(v, base - 1) + c1 * take(v, base) + c2 * take(v, base + 1))
        return values

    def outward(c):
        return jnp.where(side_x > 0, (2.0 * c + 1.0) / 6.0, (5.0 - 2.0 * c) / 6.0).astype(F32)

    @pl.when(x_edge)
    def _():
        upper, weight = east_rows()
        upper = pick_shift(upper, by_y, 3)
        weight = pick_shift(weight, by_y, 3)
        for j in range(3):
            cut = slice(LANES * j, LANES * j + LANES)
            base = third(lane + LANES * j)
            for f in range(3):
                inner, outer = blend([east_parents(b, f) for b in range(2)], base, upper[:, cut], weight[:, cut], by_y)
                for c in range(3):
                    a = outward(c)
                    strip[c, f, :, cut] = inner * (1.0 - a) + outer * a

    tall = (SPAN, LANES)
    row = iota(0, tall)
    row = jnp.where(row < SPAN - HALO, row, row - SPAN) + gx * ROWS
    part_t = iota(1, tall) & 15
    in_x1 = (row >= 3 * shift_x) & (row < total_x + 3 * shift_x)
    in_x2 = (row >= 0) & (row < total_x)
    for s, (window, origin) in enumerate((((lane >> 4), -HALO), (((lane + 8) >> 4) & 7, WIDE - 12))):
        factor[s, 0] = spread(ks, window, 0.5)
        factor[s, 1] = spread(qs, window, 1.0)
        y = (part_t if origin < 0 else ((part_t + 8) & 15)) + (origin + gy * WIDE)
        in_y = (y >= 0) & (y < total_y)
        mask[s, 0] = jnp.where(in_x1 & (y >= 3 * shift_y) & (y < total_y + 3 * shift_y), 1.0, 0.0)
        mask[s, 1] = jnp.where(in_x2 & in_y, 1.0, 0.0)
        mask[s, 2] = jnp.where(in_y, 1.0, 0.0)

    sides_x = ((west, 29, 0, 28, (30, 31)), (east, 24, 21, 27, (24, 25)))
    for there, beyond, own, zero, _ in sides_x:

        @pl.when(there)
        def _(beyond=beyond, own=own, zero=zero):
            for f in range(3):
                for j in range(3):
                    cut = slice(LANES * j, LANES * j + LANES)
                    ext[j, f, zero] = jnp.zeros(TILE, F32)
                    for c in range(3):
                        ext[j, f, beyond + c] = jnp.where(out_x, strip[c, f, :, cut], 0.0)
                        ext[j, f, own + c] = jnp.where(out_x, ext[j, f, own + c], 0.0)

    def first_rows(r):
        return half_w * in_first(r)

    def second_rows(r):
        return half_w * in_second(r)

    for turn in range(2):
        westward = odd if turn == 0 else even

        @pl.when(westward)
        def _():
            wait_recv(x_sends[3:6])

        @pl.when(jnp.logical_not(westward))
        def _():
            wait_recv(x_sends[0:3])

        if turn == 1:
            edge_windows(3)
        substep_1(jnp.where(westward, -2, 19), 7, first_rows)
        for there, _, own, _, outside in sides_x:

            @pl.when(there)
            def _(own=own, outside=outside):
                for f in range(3):
                    for r in outside:
                        mid[f, r] = jnp.zeros((LEVELS, WIDE), F32)
                    for c in range(3):
                        mid[f, own + c] = jnp.where(out_x, mid[f, own + c], strip[c, f])

        substep_2(jnp.where(westward, 0, 17), 7, second_rows)

    @pl.when(y_edge)
    def _():
        wait_recv(north_sends)
        lower_band = jnp.where(has_x[-1], north_in[0, 0], 0.0)
        upper_band = jnp.where(has_x[1], north_in[1, 0], 0.0)
        lower_tab = jnp.where(has_x[-1], north_in[0, 1], 0.0)
        upper_tab = jnp.where(has_x[1], north_in[1, 1], 0.0)
        tab = jnp.where(
            lane >= 112,
            roll(lower_tab, 128 - ROWS),
            jnp.where((lane >= ROWS) & (lane < 2 * ROWS), roll(upper_tab, ROWS), ntab[...]),
        )
        tab = pick_shift(tab, by_x, 3)
        parents = []
        for b in range(2):
            for f in range(3):
                k = 3 * b + f
                v = jnp.where((lane >= 8) & (lane < 16), roll(upper_band, 8 - 8 * k), north_parents(b, f))
                parents.append(jnp.where(lane >= 120, roll(lower_band, -8 - 8 * k), v))
        place = lane & 7
        slot = slots()
        step = jnp.where(place < 4, place, place - 5).astype(F32)
        a = jnp.where(place < 4, (2.0 * step + 1.0) / 6.0, (5.0 - 2.0 * step) / 6.0)
        real = (place != 3) & (place != 4)
        for h in range(2):
            x = slot + (16 * h - HALO)
            base = third(x)
            tab_x = take(tab, x)
            upper = jnp.broadcast_to(jnp.where(side_y == 0, tab_x[0:1], tab_x[1:2]), TILE)
            weight = jnp.broadcast_to(jnp.where(side_y == 0, tab_x[2:3], tab_x[3:4]), TILE)
            whole = x + gx * ROWS - 3 * by_x
            fits = real & (whole >= 0) & (whole < total_x)
            values = blend(parents, base, upper, weight, by_x)
            for f in range(3):
                v = jnp.where(fits, values[f] * (1.0 - a) + values[3 + f] * a, 0.0)
                ns[h, f] = jnp.where(north, roll(v, -60), roll(v, -124))
        for r in range(SPAN):
            h, i = divmod(r, 16)
            for f in range(3):
                ns_stage[f, (r - HALO) % SPAN] = roll(ns[h, f], -8 * i)
        staged = ns_stage.reshape(3 * SPAN * LEVELS, LANES)
        late = jnp.where(north, 1, 0)
        for t in range(4):
            v = jnp.zeros(TILE, F32)
            for f in range(3):
                for l in range(LEVELS):
                    rows = staged[pl.ds((f * SPAN + 8 * t) * LEVELS + l, 8, stride=LEVELS), :]
                    v = jnp.where((lane >> 2) == 4 * l + f + late, roll(rows, 16 * l + 4 * f), v)
            for there, s in ((south, 0), (north, 1)):

                @pl.when(there)
                def _(s=s, t=t, v=v):
                    if t < 3:
                        from_y[s, t] = v
                    else:
                        from_d[0, s] = v
                        from_d[1, s] = v

            for f in range(3):
                nso[f, 8 * t : 8 * t + 8] = jnp.where(north, roll(v, -4 * f - 3), roll(v, -4 * f + 3))

    def east_edge_strip(s):
        band = jnp.where(jnp.where(s == 0, has_y[-1], has_y[1]), east_in[s, 0], 0.0)
        far_tab = jnp.where(jnp.where(s == 0, has_y[-1], has_y[1]), east_in[s, 1], 0.0)
        beyond = ((lane + 64 * s) & 127) >= 64
        near = []
        for k, v in enumerate(east_rows()):
            v = jnp.where(s == 0, v[:, 0:LANES], v[:, 2 * LANES : WIDE])
            v = jnp.where(beyond, jnp.broadcast_to(far_tab[k : k + 1], TILE), v)
            near.append(pick_shift(v, by_y, 3))
        base = third(jnp.where(lane < 64, lane, lane - LANES) + WIDE * s)
        for f in range(3):
            parents = []
            for b in range(2):
                k = 3 * b + f
                parents.append(jnp.where(beyond, roll(band, -8 * k), east_parents(b, f)))
            inner, outer = blend(parents, base, near[0], near[1], by_y)
            for c in range(3):
                a = outward(c)
                v = inner * (1.0 - a) + outer * a
                stage[f, c] = v
                stage[f, 5 + c] = v
            for c in (3, 4):
                stage[f, c] = jnp.zeros(TILE, F32)
        staged = stage.reshape(3 * 8 * LEVELS, LANES)
        window = ((lane + 8 * s) >> 4) & 7
        for f in range(3):
            acc = None
            for l in range(LEVELS):
                v = roll(staged[pl.ds(f * 8 * LEVELS + l, 8, stride=LEVELS), :], 16 * l + 4)
                acc = v if acc is None else jnp.where(window == l, v, acc)
            sg[f] = acc

    sub = iota(0)
    beyond_rows = (jnp.where(west, 1, 0) * (sub >= 4).astype(I32) + jnp.where(east, 1, 0) * (sub < 4).astype(I32)) > 0
    own_low = both(west, jnp.logical_not(out_x))
    own_high = both(east, jnp.logical_not(out_x))

    def edge_side(s):
        @pl.when(x_edge)
        def _():
            east_edge_strip(s)

        k = jnp.concatenate([factor[s, 0]] * 4, axis=0)
        q = jnp.concatenate([factor[s, 1]] * 4, axis=0)
        first = mask[s, 0] > 0.5
        second = mask[s, 1] > 0.5
        in_y = mask[s, 2, 0:8] > 0.5
        lay_strip = both(jnp.where(s == 0, south, north), jnp.logical_not(out_y))
        head = jnp.where(sub < 4, from_d[1, s], from_d[0, s])
        arrived = jnp.concatenate([from_y[s, 0], from_y[s, 1], from_y[s, 2], head], axis=0)
        halo = ((part_t - 4 * s) & 15) < 4
        own_strip = (((part_t - 4 + 3 * s) & 15) < 3) & lay_strip
        state = []
        for f in range(3):
            v = jnp.where(halo, roll(arrived, -4 * f), g[s, f])
            tip = jnp.where(beyond_rows & in_y, sg[f], v[24:32])
            v = jnp.concatenate([v[0:24], tip], axis=0)
            state.append(jnp.where(first, v, 0.0))
        state = edge_substep(state, jnp.where(first, k, 0.0), k, q, SPAN)
        laid = []
        for f in range(3):
            v = state[f]
            low = jnp.where((sub < 3) & own_low, sg[f], v[0:8])
            high = jnp.where((sub >= 5) & own_high, sg[f], v[16:24])
            v = jnp.concatenate([low, v[8:16], high, v[24:32]], axis=0)
            v = jnp.where(own_strip, nso[f], v)
            laid.append(jnp.where(second, v, 0.0))
        return edge_substep(laid, jnp.where(second, k, 0.0), k, q, ROWS)

    @pl.when(at_upper)
    def _():
        wait_recv(y_sends[-1])

    @pl.when(jnp.logical_not(at_upper))
    def _():
        wait_recv(y_sends[1])

    for f, v in enumerate(edge_side(side)):
        done[f] = v

    for there, c, _ in y_sends[-1] + y_sends[1] + x_sends + north_sends:

        @pl.when(there)
        def _(c=c):
            c.wait_send()

    @pl.when(both(at_lower, has_mate))
    def _():
        first_hop.wait_send()
        last_hop.wait_send()

    @pl.when(both(at_lower, seam_west))
    def _():
        first_seam_hop.wait_send()

    @pl.when(both(at_lower, seam_east))
    def _():
        last_seam_hop.wait_send()

    @pl.when(at_upper)
    def _():
        wait_recv(y_sends[1])

    @pl.when(jnp.logical_not(at_upper))
    def _():
        wait_recv(y_sends[-1])

    lane_r = iota(1, (ROWS, LANES))
    ahead = ((((lane_r & 15) + 12) & 15) < 8).astype(I32)
    fresh = ahead == side
    for f, v in enumerate(edge_side(1 - side)):
        v = jnp.where(fresh, v, done[f])
        for l in range(LEVELS):
            m = roll(v, -16 * l - 4)
            nat[0, f, l] = jnp.where(lane_r < 8, m, nat[0, f, l])
            nat[2, f, l] = jnp.where(lane_r >= 120, m, nat[2, f, l])


def write_kernel(ready, out, sem):
    copies = [
        pltpu.make_async_copy(ready.at[j, f], out.at[f, :, :, LANES * j : LANES * j + LANES], sem.at[3 * j + f])
        for j in range(3)
        for f in range(3)
    ]
    for c in copies:
        c.start()
    for c in copies:
        c.wait()


def body(
    sizes,
    fields,
    east_band,
    north_band,
    east_index,
    north_index,
    east_weight,
    north_weight,
    nest_moves,
    courant,
    diffuse,
):
    vmem = pltpu.VMEM
    dma = pltpu.SemaphoreType.DMA
    ready = pl.pallas_call(
        functools.partial(exchange_kernel, sizes),
        out_shape=vmem((3, 3, LEVELS, ROWS, LANES), F32),
        in_specs=[pl.BlockSpec(memory_space=pl.ANY)] * 10,
        out_specs=pl.BlockSpec(memory_space=pltpu.VMEM),
        scratch_shapes=[
            vmem((3, 3, SPAN) + TILE, F32),
            vmem((3, SPAN, LEVELS, WIDE), F32),
            vmem((2, 3, SPAN, LANES), F32),
            vmem((2, 3) + TILE, F32),
            vmem((2, 3) + TILE, F32),
            vmem((2, 2) + TILE, F32),
            vmem((2,) + TILE, F32),
            vmem((2, 2) + TILE, F32),
            vmem((2,) + TILE, F32),
            vmem((2, 2) + TILE, F32),
            vmem((3, 3, LEVELS, WIDE), F32),
            vmem((3, 8) + TILE, F32),
            vmem((3,) + TILE, F32),
            vmem((2, 3) + TILE, F32),
            vmem((3, SPAN) + TILE, F32),
            vmem((3, SPAN, LANES), F32),
            vmem((2,) + TILE, F32),
            vmem((2, 3, SPAN, LANES), F32),
            vmem((2, 2) + TILE, F32),
            vmem((3, ROWS, LANES), F32),
            vmem((96, LANES), F32),
            vmem((2, WIDE), I32),
            vmem((2, WIDE), F32),
            vmem((96, 8), F32),
            vmem((96, LANES), F32),
            vmem((2, ROWS), I32),
            vmem((2, ROWS), F32),
            vmem(TILE, F32),
            pltpu.SMEM((2, 2), I32),
            pltpu.SMEM((LEVELS,), F32),
            pltpu.SMEM((LEVELS,), F32),
            dma((9,)),
            dma((9,)),
            dma((6,)),
            dma((6,)),
            dma((2,)),
            dma((2,)),
            dma((4,)),
            dma((4,)),
            dma((2,)),
            dma((2,)),
            dma((2,)),
            dma((2,)),
            pltpu.SemaphoreType.REGULAR,
            dma((4,)),
            dma((2,)),
        ],
        compiler_params=pltpu.CompilerParams(
            collective_id=0, has_side_effects=True, vmem_limit_bytes=VMEM_A
        ),
    )(
        fields,
        east_band.reshape(96, LANES),
        north_band.reshape(96, 8),
        east_index,
        north_index,
        east_weight,
        north_weight,
        nest_moves,
        courant,
        diffuse,
    )
    return pl.pallas_call(
        write_kernel,
        out_shape=jax.ShapeDtypeStruct(fields.shape, F32),
        in_specs=[pl.BlockSpec(memory_space=pltpu.VMEM)],
        out_specs=pl.BlockSpec(memory_space=pl.ANY),
        scratch_shapes=[dma((9,))],
        compiler_params=pltpu.CompilerParams(vmem_limit_bytes=VMEM_B),
    )(ready)


VMEM_A = 56 * 1024 * 1024
VMEM_B = 8 * 1024 * 1024


def solution(mesh):
    sizes = (mesh.shape["gx"], mesh.shape["gy"])
    return jax.shard_map(
        functools.partial(body, sizes),
        mesh=mesh,
        in_specs=(
            P(None, None, "gx", "gy"),
            P(None, None, None, None, "gy"),
            P(None, None, None, None, "gx"),
            P(None, "gy"),
            P(None, "gx"),
            P(None, "gy"),
            P(None, "gx"),
            P(),
            P(),
            P(),
        ),
        out_specs=P(None, None, "gx", "gy"),
        check_vma=False,
    )
```

```python
import functools

import jax
import jax.numpy as jnp
from jax import lax
from jax.experimental import pallas as pl
from jax.experimental.pallas import tpu as pltpu
from jax.sharding import PartitionSpec as P

MESH = pl.DeviceIdType.MESH
F32 = jnp.float32
I32 = jnp.int32
HALO = 4
ROWS = 24
SPAN = ROWS + 2 * HALO
WIDE = 384
LANES = 128
LEVELS = 8
X_ROWS = (4, 3, 2)
RUN = 8
TILE = (LEVELS, LANES)


def third(v):
    return (((v + 48) * 43691) >> 17) - 16


def roll(v, by):
    by = by % v.shape[1]
    return pltpu.roll(v, by, 1) if by else v


def roll_rows(v, by):
    return pltpu.roll(v, by % v.shape[0], 0)


def iota(axis=1, shape=TILE):
    return lax.broadcasted_iota(I32, shape, axis)


def take(v, at):
    return jnp.take_along_axis(v, at & (LANES - 1), axis=1)


def pick_shift(v, by, step):
    return jnp.where(by > 0, roll(v, step), jnp.where(by < 0, roll(v, -step), v))


def slots():
    lane = iota()
    return jnp.where((lane & 7) < 4, ((lane + 64) & 127) >> 3, ((lane + 4) & 127) >> 3)


def advance(load, store, lo, count, kk, kk_row, visc):
    def first(r, p_below, p_here, p_above):
        k = kk_row(r)
        u = load(1, r) - k * (p_above - p_below)
        v = load(2, r) - k * (roll(p_here, -1) - roll(p_here, 1))
        return u, v

    p = [load(0, lo - 2 + i) for i in range(4)]
    ub, vb = first(lo - 1, p[0], p[1], p[2])
    u0, v0 = first(lo, p[1], p[2], p[3])
    p0, p1 = p[2], p[3]
    for step in range(count):
        r = lo + step
        p2 = load(0, r + 2)
        ua, va = first(r + 1, p0, p1, p2)
        un, us, vn, vs = roll(u0, -1), roll(u0, 1), roll(v0, -1), roll(v0, 1)
        store(0, r, p0 - kk * ((ua - ub) + (vn - vs)))
        store(1, r, u0 + visc * (((ua + ub) + (un + us)) - 4.0 * u0))
        store(2, r, v0 + visc * (((va + vb) + (vn + vs)) - 4.0 * v0))
        p0, p1, ub, u0, vb, v0 = p1, p2, u0, ua, v0, va


def edge_substep(fields, kk_in, kk, visc, keep):
    p, u, v = fields
    u = u - kk_in * (roll_rows(p, -1) - roll_rows(p, 1))
    v = v - kk_in * (roll(p, -1) - roll(p, 1))
    ue, uw = roll_rows(u, -1)[0:keep], roll_rows(u, 1)[0:keep]
    ve, vw = roll_rows(v, -1)[0:keep], roll_rows(v, 1)[0:keep]
    p, u, v, kk, visc = p[0:keep], u[0:keep], v[0:keep], kk[0:keep], visc[0:keep]
    vn, vs = roll(v, -1), roll(v, 1)
    p = p - kk * ((ue - uw) + (vn - vs))
    u2 = u + visc * (((ue + uw) + (roll(u, -1) + roll(u, 1))) - 4.0 * u)
    v2 = v + visc * (((ve + vw) + (vn + vs)) - 4.0 * v)
    return p, u2, v2


def exchange_kernel(
    sizes,
    fields,
    east_band,
    north_band,
    east_index,
    north_index,
    east_weight,
    north_weight,
    moves,
    courant,
    diffuse,
    nat,
    ext,
    mid,
    g,
    to_y,
    from_y,
    from_d,
    east_out,
    east_in,
    north_out,
    north_in,
    strip,
    stage,
    sg,
    ns,
    ns_stage,
    nso,
    hop,
    mask,
    factor,
    done,
    eb,
    ei,
    ew,
    nb,
    nbw,
    ni,
    nw,
    ntab,
    mv,
    ks,
    qs,
    sent,
    received,
    ready,
):
    nx, ny = sizes
    gx = lax.axis_index("gx")
    gy = lax.axis_index("gy")
    total_x = nx * ROWS
    total_y = ny * WIDE
    upper_mid = ny // 2
    lower_mid = upper_mid - 1
    west, east = gx == 0, gx == nx - 1
    south, north = gy == 0, gy == ny - 1
    x_edge = jnp.logical_or(west, east)
    y_edge = jnp.logical_or(south, north)
    has_x = {-1: gx > 0, 1: gx < nx - 1}
    has_y = {-1: gy > 0, 1: gy < ny - 1}
    at_lower = gy == lower_mid
    at_upper = gy == upper_mid
    at_mid = jnp.logical_or(at_lower, at_upper)

    def both(a, b):
        return jnp.logical_and(a, b)

    def has(dx, dy):
        if dx and dy:
            return both(has_x[dx], has_y[dy])
        return has_x[dx] if dx else has_y[dy]

    def over(dy):
        return at_lower if dy > 0 else at_upper

    odd = lax.rem(gx, 2) == 1
    even = jnp.logical_not(odd)
    is_far = {-1: even, 1: odd}
    has_far = jnp.where(odd, has_x[1].astype(I32), has_x[-1].astype(I32))

    seam_west = both(lax.rem(gx, RUN) == 0, gx > 0)
    seam_east = both(lax.rem(gx, RUN) == RUN - 1, gx < nx - 1)

    barrier = pltpu.get_barrier_semaphore()

    def greet(dx, dy, there):
        @pl.when(both(has(dx, dy), there))
        def _():
            pl.semaphore_signal(barrier, inc=1, device_id=(gx + dx, gy + dy), device_id_type=MESH)

    for dy in (1, -1):
        for dx in (-1, 1, 0):
            there = over(dy)
            if dx and dy < 0:
                there = both(there, is_far[dx])
            if dx > 0 and dy < 0:
                there = both(there, jnp.logical_not(seam_east))
            greet(dx, dy, there)
    for dy in (1, -1):
        to_mid = (gy + dy == lower_mid) if dy > 0 else (gy + dy == upper_mid)
        for dx in (-1, 1, 0):
            greet(dx, dy, jnp.logical_not(jnp.logical_or(over(dy), to_mid)))
    for dx in (-1, 1):
        greet(dx, 0, jnp.logical_not(at_mid))

    loads = [
        pltpu.make_async_copy(
            fields.at[f, l, :, LANES * j : LANES * j + LANES], ext.at[j, f, 0:ROWS, l, :], sent.at[j & 1]
        )
        for j in (0, 2, 1)
        for f in range(3)
        for l in range(LEVELS)
    ]
    smalls = [
        pltpu.make_async_copy(s, d, sent.at[2 + k])
        for k, (s, d) in enumerate(
            ((moves, mv), (courant, ks), (diffuse, qs), (east_band, eb), (east_index, ei), (east_weight, ew))
        )
    ]
    norths = [
        pltpu.make_async_copy(s, d, sent.at[2 + k])
        for k, (s, d) in enumerate(((north_band, nb), (north_index, ni), (north_weight, nw)))
    ]
    for c in loads + smalls:
        c.start()

    def wait_bytes(block, sem):
        pltpu.make_async_copy(block, block, sem).wait()

    wait_bytes(ext.at[0:2, :, 0:ROWS], sent.at[0])

    lane = iota()
    part = lane & 15
    ext_rows = ext.reshape(9 * SPAN * LEVELS, LANES)

    def edge_windows(t):
        for f in range(3):
            low, high = None, None
            for l in range(LEVELS):
                at = (f * SPAN + 8 * t) * LEVELS + l
                head = ext_rows[pl.ds(at, 8, stride=LEVELS), :]
                tail = ext_rows[pl.ds(at + 6 * SPAN * LEVELS, 8, stride=LEVELS), :]
                v = roll(jnp.where(lane < 64, head, tail), 16 * l + 4)
                low = v if low is None else jnp.where((lane >> 4) == l, v, low)
                high = v if high is None else jnp.where((((lane + 8) >> 4) & 7) == l, v, high)
            g[0, f, 8 * t : 8 * t + 8] = low
            g[1, f, 8 * t : 8 * t + 8] = high

    for t in range(3):
        edge_windows(t)
        for d in range(2):
            v = g[d, 0, 8 * t : 8 * t + 8]
            for f in range(1, 3):
                v = jnp.where((part >> 2) == f + 1 - d, roll(g[d, f, 8 * t : 8 * t + 8], 4 * f), v)
            to_y[d, t] = v
    for c in smalls:
        c.wait()

    shift_x = mv[0, 0]
    shift_y = mv[0, 1]
    side_x = jnp.where(west, 0, 1)
    side_y = jnp.where(south, 0, 1)
    out_x = shift_x == 2 * side_x - 1
    out_y = shift_y == 2 * side_y - 1
    by_y = jnp.where(out_x, shift_y, 0)
    by_x = jnp.where(out_y, shift_x, 0)

    def east_rows():
        cell = iota(1, (1, WIDE))
        index = jnp.where(side_x == 0, ei[0:1, :], ei[1:2, :])
        upper = (index - (gy * LANES + third(cell)) + 1).astype(F32)
        weight = jnp.where(side_x == 0, ew[0:1, :], ew[1:2, :])
        wide = (LEVELS, WIDE)
        return jnp.broadcast_to(upper, wide), jnp.broadcast_to(weight, wide)

    def east_parents(b, f):
        return eb[pl.ds(side_x * 48 + f * 16 + b, LEVELS, stride=2), :]

    def north_parents(b, f):
        return nbw[pl.ds(side_y * 48 + f * 16 + b, LEVELS, stride=2), :]

    @pl.when(x_edge)
    def _():
        acc = jnp.zeros(TILE, F32)
        for b in range(2):
            for f in range(3):
                k = 3 * b + f
                near = (((lane - 8 * k + 4) & 127) >> 3) == 0
                acc = jnp.where(near, roll(east_parents(b, f), 8 * k), acc)
        east_out[0] = acc
        rows = [jnp.where(lane < 64, v[:, 0:LANES], v[:, 2 * LANES : WIDE]) for v in east_rows()]
        east_out[1] = jnp.where(iota(0) == 0, rows[0], rows[1])

    @pl.when(y_edge)
    def _():
        for c in norths:
            c.start()
        for c in norths:
            c.wait()
        nbw[...] = jnp.zeros((96, LANES), F32)
        nbw[:, 0:8] = nb[...]
        cell = iota(1, (2, ROWS))
        ntab[...] = jnp.zeros(TILE, F32)
        ntab[0:2, 0:ROWS] = (ni[...] - (gx * 8 + third(cell)) + 1).astype(F32)
        ntab[2:4, 0:ROWS] = nw[...]
        acc = jnp.zeros(TILE, F32)
        for b in range(2):
            for f in range(3):
                k = 3 * b + f
                acc = jnp.where((lane >> 3) == k, roll(north_parents(b, f), 8 * k), acc)
        north_out[0] = acc
        north_out[1] = ntab[...]

    def to(dx, dy, src, dst, send, recv):
        return pltpu.make_async_remote_copy(
            src_ref=src,
            dst_ref=dst,
            send_sem=send,
            recv_sem=recv,
            device_id=(gx + dx, gy + dy),
            device_id_type=MESH,
        )

    y_sends = {}
    for s, dy in enumerate((-1, 1)):
        group = []
        for a, dx in enumerate((-1, 1)):
            c = to(
                dx,
                dy,
                to_y.at[s, 2 * a],
                from_d.at[1 - a, 1 - s],
                sent.at[4 + 2 * a + s],
                received.at[4 + 2 * (1 - a) + 1 - s],
            )
            there = has(dx, dy)
            if dy > 0:
                near = jnp.logical_not(is_far[dx])
                near = jnp.logical_or(near, seam_west) if dx < 0 else near
                there = both(there, jnp.logical_not(both(near, at_lower)))
            group.append((there, c, has(-dx, -dy)))
        c = to(0, dy, to_y.at[s], from_y.at[1 - s], sent.at[2 + s], received.at[2 + 1 - s])
        group.append((has(0, dy), c, has(0, -dy)))
        send, recv = sent.at[4 + 2 * side_x + s], received.at[4 + 2 * side_x + 1 - s]
        c = to(0, dy, east_out, east_in.at[1 - s], send, recv)
        group.append((both(x_edge, has(0, dy)), c, both(x_edge, has(0, -dy))))
        y_sends[dy] = group
    x_sends = []
    north_sends = []
    for a, dx in enumerate((-1, 1)):
        for f in range(3):
            n = X_ROWS[f]
            if dx < 0:
                src, dst = ext.at[:, f, 0:n], ext.at[:, f, ROWS : ROWS + n]
            else:
                src, dst = ext.at[:, f, ROWS - n : ROWS], ext.at[:, f, SPAN - n : SPAN]
            x_sends.append((has(dx, 0), to(dx, 0, src, dst, sent.at[a], received.at[1 - a]), None))
        send, recv = sent.at[4 + 2 * a + side_y], received.at[4 + 2 * (1 - a) + side_y]
        c = to(dx, 0, north_out, north_in.at[1 - a], send, recv)
        north_sends.append((both(y_edge, has(dx, 0)), c, both(y_edge, has(-dx, 0))))

    side = jnp.where(at_upper, 1, 0)
    east_one = odd.astype(I32)
    mate = 1 - 2 * east_one
    has_mate = jnp.where(odd, has_x[-1].astype(I32), has_x[1].astype(I32)) > 0
    first_hop = to(mate, 0, to_y.at[1, 2 * (1 - east_one)], hop.at[0], sent.at[8], received.at[8])
    last_hop = to(
        0, 1, hop.at[0], from_d.at[1 - east_one, 0], sent.at[4 + 2 * (1 - east_one) + 1], received.at[4 + 2 * (1 - east_one)]
    )
    first_seam_hop = to(-1, 0, to_y.at[1, 0], hop.at[1], sent.at[5], received.at[9])
    last_seam_hop = to(0, 1, hop.at[1], from_d.at[1, 0], sent.at[9], received.at[6])

    def start(group, extra=None):
        for there, c, _ in group:

            @pl.when(there if extra is None else both(there, extra))
            def _(c=c):
                c.start()

    def wait_recv(group):
        for _, c, there in group:

            @pl.when(there)
            def _(c=c):
                c.wait_recv()

    count_x = 1 + has_x[-1].astype(I32) + has_x[1].astype(I32)
    count_y = 1 + has_y[-1].astype(I32) + has_y[1].astype(I32)

    wait_bytes(ext.at[1, :, 0:ROWS], sent.at[1])

    @pl.when(at_upper)
    def _():
        pl.semaphore_wait(barrier, count_x)
        start(y_sends[-1])

    @pl.when(jnp.logical_not(at_mid))
    def _():
        pl.semaphore_wait(barrier, count_x * count_y - 1)

        @pl.when(gy == lower_mid - 1)
        def _():
            pl.semaphore_signal(ready, inc=1, device_id=(gx, gy + 1), device_id_type=MESH)

        @pl.when(gy == upper_mid + 1)
        def _():
            pl.semaphore_signal(ready, inc=1, device_id=(gx, gy - 1), device_id_type=MESH)

        start(y_sends[-1])
        start(y_sends[1])
        start(north_sends)
        start(x_sends)

    def spread(values, level, scale):
        v = jnp.zeros(TILE, F32)
        for l in range(LEVELS):
            v = jnp.where(level == l, scale * values[l], v)
        return v

    level = iota(0)
    half = spread(ks, level, 0.5)
    visc = spread(qs, level, 1.0)
    half_w = jnp.concatenate([half] * 3, axis=1)
    visc_w = jnp.concatenate([visc] * 3, axis=1)
    nat_rows = nat.reshape(9 * ROWS * LEVELS, LANES)

    def in_first(r):
        x = gx * ROWS + r
        return jnp.where(both(x >= 3 * shift_x, x < total_x + 3 * shift_x), 1.0, 0.0).astype(F32)

    def in_second(r):
        x = gx * ROWS + r
        return jnp.where(both(x >= 0, x < total_x), 1.0, 0.0).astype(F32)

    def load_ext(f, r):
        return jnp.concatenate([ext[j, f, r & (SPAN - 1)] for j in range(3)], axis=1)

    def load_mid(f, r):
        return mid[f, r & (SPAN - 1)]

    def store_mid(f, r, v):
        mid[f, r & (SPAN - 1)] = v

    def store_nat(f, r, v):
        for j in range(3):
            at = (3 * j + f) * LEVELS * ROWS + r
            nat_rows[pl.ds(at, LEVELS, stride=ROWS), :] = v[:, LANES * j : LANES * j + LANES]

    def substep_1(lo, count, kk_row):
        advance(load_ext, store_mid, lo, count, half_w, kk_row, visc_w)

    def substep_2(lo, count, kk_row):
        advance(load_mid, store_nat, lo, count, half_w, kk_row, visc_w)

    def everywhere(r):
        return half_w

    substep_1(5, 14, everywhere)
    substep_2(7, 10, everywhere)

    @pl.when(at_mid)
    def _():
        pl.semaphore_wait(ready, 1)

        @pl.when(both(at_lower, has_mate))
        def _():
            first_hop.start()

        @pl.when(both(at_lower, seam_west))
        def _():
            first_seam_hop.start()

        start(x_sends)
        start(y_sends[-1], at_lower)
        start(y_sends[1], at_upper)
        start(north_sends)

    @pl.when(at_lower)
    def _():
        pl.semaphore_wait(barrier, 1 + has_far - seam_west.astype(I32))
        start(y_sends[1])

        @pl.when(has_mate)
        def _():
            first_hop.wait_recv()
            last_hop.start()

        @pl.when(seam_east)
        def _():
            first_seam_hop.wait_recv()
            last_seam_hop.start()

    def blend(parents, base, upper, weight, by):
        c0 = (1.0 - upper) * (1.0 - weight)
        c1 = (1.0 - upper) * weight + upper * (1.0 - weight)
        c2 = upper * weight
        values = []
        for v in parents:
            v = pick_shift(v, by, 1)
            values.append(c0 * take(v, base - 1) + c1 * take(v, base) + c2 * take(v, base + 1))
        return values

    def outward(c):
        return jnp.where(side_x > 0, (2.0 * c + 1.0) / 6.0, (5.0 - 2.0 * c) / 6.0).astype(F32)

    @pl.when(x_edge)
    def _():
        upper, weight = east_rows()
        upper = pick_shift(upper, by_y, 3)
        weight = pick_shift(weight, by_y, 3)
        for j in range(3):
            cut = slice(LANES * j, LANES * j + LANES)
            base = third(lane + LANES * j)
            for f in range(3):
                inner, outer = blend([east_parents(b, f) for b in range(2)], base, upper[:, cut], weight[:, cut], by_y)
                for c in range(3):
                    a = outward(c)
                    strip[c, f, :, cut] = inner * (1.0 - a) + outer * a

    tall = (SPAN, LANES)
    row = iota(0, tall)
    row = jnp.where(row < SPAN - HALO, row, row - SPAN) + gx * ROWS
    part_t = iota(1, tall) & 15
    in_x1 = (row >= 3 * shift_x) & (row < total_x + 3 * shift_x)
    in_x2 = (row >= 0) & (row < total_x)
    for s, (window, origin) in enumerate((((lane >> 4), -HALO), (((lane + 8) >> 4) & 7, WIDE - 12))):
        factor[s, 0] = spread(ks, window, 0.5)
        factor[s, 1] = spread(qs, window, 1.0)
        y = (part_t if origin < 0 else ((part_t + 8) & 15)) + (origin + gy * WIDE)
        in_y = (y >= 0) & (y < total_y)
        mask[s, 0] = jnp.where(in_x1 & (y >= 3 * shift_y) & (y < total_y + 3 * shift_y), 1.0, 0.0)
        mask[s, 1] = jnp.where(in_x2 & in_y, 1.0, 0.0)
        mask[s, 2] = jnp.where(in_y, 1.0, 0.0)

    sides_x = ((west, 29, 0, 28, (30, 31)), (east, 24, 21, 27, (24, 25)))
    for there, beyond, own, zero, _ in sides_x:

        @pl.when(there)
        def _(beyond=beyond, own=own, zero=zero):
            for f in range(3):
                for j in range(3):
                    cut = slice(LANES * j, LANES * j + LANES)
                    ext[j, f, zero] = jnp.zeros(TILE, F32)
                    for c in range(3):
                        ext[j, f, beyond + c] = jnp.where(out_x, strip[c, f, :, cut], 0.0)
                        ext[j, f, own + c] = jnp.where(out_x, ext[j, f, own + c], 0.0)

    def first_rows(r):
        return half_w * in_first(r)

    def second_rows(r):
        return half_w * in_second(r)

    def x_wait(sem, there):
        @pl.when(there)
        def _():
            wait_bytes(ext.at[:, 0, 0 : sum(X_ROWS)], sem)

    for turn in range(2):
        westward = odd if turn == 0 else even

        @pl.when(westward)
        def _():
            x_wait(received.at[0], has(-1, 0))

        @pl.when(jnp.logical_not(westward))
        def _():
            x_wait(received.at[1], has(1, 0))

        if turn == 1:
            edge_windows(3)
        substep_1(jnp.where(westward, -2, 19), 7, first_rows)
        for there, _, own, _, outside in sides_x:

            @pl.when(there)
            def _(own=own, outside=outside):
                for f in range(3):
                    for r in outside:
                        mid[f, r] = jnp.zeros((LEVELS, WIDE), F32)
                    for c in range(3):
                        mid[f, own + c] = jnp.where(out_x, mid[f, own + c], strip[c, f])

        substep_2(jnp.where(westward, 0, 17), 7, second_rows)

    @pl.when(y_edge)
    def _():
        wait_recv(north_sends)
        lower_band = jnp.where(has_x[-1], north_in[0, 0], 0.0)
        upper_band = jnp.where(has_x[1], north_in[1, 0], 0.0)
        lower_tab = jnp.where(has_x[-1], north_in[0, 1], 0.0)
        upper_tab = jnp.where(has_x[1], north_in[1, 1], 0.0)
        tab = jnp.where(
            lane >= 112,
            roll(lower_tab, 128 - ROWS),
            jnp.where((lane >= ROWS) & (lane < 2 * ROWS), roll(upper_tab, ROWS), ntab[...]),
        )
        tab = pick_shift(tab, by_x, 3)
        parents = []
        for b in range(2):
            for f in range(3):
                k = 3 * b + f
                v = jnp.where((lane >= 8) & (lane < 16), roll(upper_band, 8 - 8 * k), north_parents(b, f))
                parents.append(jnp.where(lane >= 120, roll(lower_band, -8 - 8 * k), v))
        place = lane & 7
        slot = slots()
        step = jnp.where(place < 4, place, place - 5).astype(F32)
        a = jnp.where(place < 4, (2.0 * step + 1.0) / 6.0, (5.0 - 2.0 * step) / 6.0)
        real = (place != 3) & (place != 4)
        for h in range(2):
            x = slot + (16 * h - HALO)
            base = third(x)
            tab_x = take(tab, x)
            upper = jnp.broadcast_to(jnp.where(side_y == 0, tab_x[0:1], tab_x[1:2]), TILE)
            weight = jnp.broadcast_to(jnp.where(side_y == 0, tab_x[2:3], tab_x[3:4]), TILE)
            whole = x + gx * ROWS - 3 * by_x
            fits = real & (whole >= 0) & (whole < total_x)
            values = blend(parents, base, upper, weight, by_x)
            for f in range(3):
                v = jnp.where(fits, values[f] * (1.0 - a) + values[3 + f] * a, 0.0)
                ns[h, f] = jnp.where(north, roll(v, -60), roll(v, -124))
        for r in range(SPAN):
            h, i = divmod(r, 16)
            for f in range(3):
                ns_stage[f, (r - HALO) % SPAN] = roll(ns[h, f], -8 * i)
        staged = ns_stage.reshape(3 * SPAN * LEVELS, LANES)
        late = jnp.where(north, 1, 0)
        for t in range(4):
            v = jnp.zeros(TILE, F32)
            for f in range(3):
                for l in range(LEVELS):
                    rows = staged[pl.ds((f * SPAN + 8 * t) * LEVELS + l, 8, stride=LEVELS), :]
                    v = jnp.where((lane >> 2) == 4 * l + f + late, roll(rows, 16 * l + 4 * f), v)
            for there, s in ((south, 0), (north, 1)):

                @pl.when(there)
                def _(s=s, t=t, v=v):
                    if t < 3:
                        from_y[s, t] = v
                    else:
                        from_d[0, s] = v
                        from_d[1, s] = v

            for f in range(3):
                nso[f, 8 * t : 8 * t + 8] = jnp.where(north, roll(v, -4 * f - 3), roll(v, -4 * f + 3))

    def east_edge_strip(s):
        band = jnp.where(jnp.where(s == 0, has_y[-1], has_y[1]), east_in[s, 0], 0.0)
        far_tab = jnp.where(jnp.where(s == 0, has_y[-1], has_y[1]), east_in[s, 1], 0.0)
        beyond = ((lane + 64 * s) & 127) >= 64
        near = []
        for k, v in enumerate(east_rows()):
            v = jnp.where(s == 0, v[:, 0:LANES], v[:, 2 * LANES : WIDE])
            v = jnp.where(beyond, jnp.broadcast_to(far_tab[k : k + 1], TILE), v)
            near.append(pick_shift(v, by_y, 3))
        base = third(jnp.where(lane < 64, lane, lane - LANES) + WIDE * s)
        for f in range(3):
            parents = []
            for b in range(2):
                k = 3 * b + f
                parents.append(jnp.where(beyond, roll(band, -8 * k), east_parents(b, f)))
            inner, outer = blend(parents, base, near[0], near[1], by_y)
            for c in range(3):
                a = outward(c)
                v = inner * (1.0 - a) + outer * a
                stage[f, c] = v
                stage[f, 5 + c] = v
            for c in (3, 4):
                stage[f, c] = jnp.zeros(TILE, F32)
        staged = stage.reshape(3 * 8 * LEVELS, LANES)
        window = ((lane + 8 * s) >> 4) & 7
        for f in range(3):
            acc = None
            for l in range(LEVELS):
                v = roll(staged[pl.ds(f * 8 * LEVELS + l, 8, stride=LEVELS), :], 16 * l + 4)
                acc = v if acc is None else jnp.where(window == l, v, acc)
            sg[f] = acc

    sub = iota(0)
    beyond_rows = (jnp.where(west, 1, 0) * (sub >= 4).astype(I32) + jnp.where(east, 1, 0) * (sub < 4).astype(I32)) > 0
    own_low = both(west, jnp.logical_not(out_x))
    own_high = both(east, jnp.logical_not(out_x))

    def edge_side(s):
        @pl.when(x_edge)
        def _():
            east_edge_strip(s)

        k = jnp.concatenate([factor[s, 0]] * 4, axis=0)
        q = jnp.concatenate([factor[s, 1]] * 4, axis=0)
        first = mask[s, 0] > 0.5
        second = mask[s, 1] > 0.5
        in_y = mask[s, 2, 0:8] > 0.5
        lay_strip = both(jnp.where(s == 0, south, north), jnp.logical_not(out_y))
        head = jnp.where(sub < 4, from_d[1, s], from_d[0, s])
        arrived = jnp.concatenate([from_y[s, 0], from_y[s, 1], from_y[s, 2], head], axis=0)
        halo = ((part_t - 4 * s) & 15) < 4
        own_strip = (((part_t - 4 + 3 * s) & 15) < 3) & lay_strip
        state = []
        for f in range(3):
            v = jnp.where(halo, roll(arrived, -4 * f), g[s, f])
            tip = jnp.where(beyond_rows & in_y, sg[f], v[24:32])
            v = jnp.concatenate([v[0:24], tip], axis=0)
            state.append(jnp.where(first, v, 0.0))
        state = edge_substep(state, jnp.where(first, k, 0.0), k, q, SPAN)
        laid = []
        for f in range(3):
            v = state[f]
            low = jnp.where((sub < 3) & own_low, sg[f], v[0:8])
            high = jnp.where((sub >= 5) & own_high, sg[f], v[16:24])
            v = jnp.concatenate([low, v[8:16], high, v[24:32]], axis=0)
            v = jnp.where(own_strip, nso[f], v)
            laid.append(jnp.where(second, v, 0.0))
        return edge_substep(laid, jnp.where(second, k, 0.0), k, q, ROWS)

    @pl.when(at_upper)
    def _():
        wait_recv(y_sends[-1])

    @pl.when(jnp.logical_not(at_upper))
    def _():
        wait_recv(y_sends[1])

    for f, v in enumerate(edge_side(side)):
        done[f] = v

    for a, dx in enumerate((-1, 1)):
        x_wait(sent.at[a], has(dx, 0))
    for there, c, _ in y_sends[-1] + y_sends[1] + north_sends:

        @pl.when(there)
        def _(c=c):
            c.wait_send()

    @pl.when(both(at_lower, has_mate))
    def _():
        first_hop.wait_send()
        last_hop.wait_send()

    @pl.when(both(at_lower, seam_west))
    def _():
        first_seam_hop.wait_send()

    @pl.when(both(at_lower, seam_east))
    def _():
        last_seam_hop.wait_send()

    @pl.when(at_upper)
    def _():
        wait_recv(y_sends[1])

    @pl.when(jnp.logical_not(at_upper))
    def _():
        wait_recv(y_sends[-1])

    lane_r = iota(1, (ROWS, LANES))
    ahead = ((((lane_r & 15) + 12) & 15) < 8).astype(I32)
    fresh = ahead == side
    for f, v in enumerate(edge_side(1 - side)):
        v = jnp.where(fresh, v, done[f])
        for l in range(LEVELS):
            m = roll(v, -16 * l - 4)
            nat[0, f, l] = jnp.where(lane_r < 8, m, nat[0, f, l])
            nat[2, f, l] = jnp.where(lane_r >= 120, m, nat[2, f, l])


def write_kernel(ready, out, sem):
    for j in range(3):
        pltpu.make_async_copy(ready.at[j], out.at[:, :, :, LANES * j : LANES * j + LANES], sem).start()
    pltpu.make_async_copy(ready, ready, sem).wait()


def body(
    sizes,
    fields,
    east_band,
    north_band,
    east_index,
    north_index,
    east_weight,
    north_weight,
    nest_moves,
    courant,
    diffuse,
):
    vmem = pltpu.VMEM
    dma = pltpu.SemaphoreType.DMA
    ready = pl.pallas_call(
        functools.partial(exchange_kernel, sizes),
        out_shape=vmem((3, 3, LEVELS, ROWS, LANES), F32),
        in_specs=[pl.BlockSpec(memory_space=pl.ANY)] * 10,
        out_specs=pl.BlockSpec(memory_space=pltpu.VMEM),
        scratch_shapes=[
            vmem((3, 3, SPAN) + TILE, F32),
            vmem((3, SPAN, LEVELS, WIDE), F32),
            vmem((2, 3, SPAN, LANES), F32),
            vmem((2, 3) + TILE, F32),
            vmem((2, 3) + TILE, F32),
            vmem((2, 2) + TILE, F32),
            vmem((2,) + TILE, F32),
            vmem((2, 2) + TILE, F32),
            vmem((2,) + TILE, F32),
            vmem((2, 2) + TILE, F32),
            vmem((3, 3, LEVELS, WIDE), F32),
            vmem((3, 8) + TILE, F32),
            vmem((3,) + TILE, F32),
            vmem((2, 3) + TILE, F32),
            vmem((3, SPAN) + TILE, F32),
            vmem((3, SPAN, LANES), F32),
            vmem((2,) + TILE, F32),
            vmem((2, 3, SPAN, LANES), F32),
            vmem((2, 2) + TILE, F32),
            vmem((3, ROWS, LANES), F32),
            vmem((96, LANES), F32),
            vmem((2, WIDE), I32),
            vmem((2, WIDE), F32),
            vmem((96, 8), F32),
            vmem((96, LANES), F32),
            vmem((2, ROWS), I32),
            vmem((2, ROWS), F32),
            vmem(TILE, F32),
            pltpu.SMEM((2, 2), I32),
            pltpu.SMEM((LEVELS,), F32),
            pltpu.SMEM((LEVELS,), F32),
            dma((10,)),
            dma((10,)),
            pltpu.SemaphoreType.REGULAR,
        ],
        compiler_params=pltpu.CompilerParams(
            collective_id=0, has_side_effects=True, vmem_limit_bytes=VMEM_A
        ),
    )(
        fields,
        east_band.reshape(96, LANES),
        north_band.reshape(96, 8),
        east_index,
        north_index,
        east_weight,
        north_weight,
        nest_moves,
        courant,
        diffuse,
    )
    return pl.pallas_call(
        write_kernel,
        out_shape=jax.ShapeDtypeStruct(fields.shape, F32),
        in_specs=[pl.BlockSpec(memory_space=pltpu.VMEM)],
        out_specs=pl.BlockSpec(memory_space=pl.ANY),
        scratch_shapes=[dma],
        compiler_params=pltpu.CompilerParams(vmem_limit_bytes=VMEM_B),
    )(ready)


VMEM_A = 56 * 1024 * 1024
VMEM_B = 8 * 1024 * 1024


def solution(mesh):
    sizes = (mesh.shape["gx"], mesh.shape["gy"])
    return jax.shard_map(
        functools.partial(body, sizes),
        mesh=mesh,
        in_specs=(
            P(None, None, "gx", "gy"),
            P(None, None, None, None, "gy"),
            P(None, None, None, None, "gx"),
            P(None, "gy"),
            P(None, "gx"),
            P(None, "gy"),
            P(None, "gx"),
            P(),
            P(),
            P(),
        ),
        out_specs=P(None, None, "gx", "gy"),
        check_vma=False,
    )
```

```python
import functools

import jax
import jax.numpy as jnp
from jax import lax
from jax.experimental import pallas as pl
from jax.experimental.pallas import tpu as pltpu
from jax.sharding import PartitionSpec as P

MESH = pl.DeviceIdType.MESH
F32 = jnp.float32
I32 = jnp.int32
HALO = 4
ROWS = 24
SPAN = ROWS + 2 * HALO
WIDE = 384
LANES = 128
LEVELS = 8
X_ROWS = (4, 3, 2)
RUN = 8
TILE = (LEVELS, LANES)


def third(v):
    return (((v + 48) * 43691) >> 17) - 16


def roll(v, by):
    by = by % v.shape[1]
    return pltpu.roll(v, by, 1) if by else v


def roll_rows(v, by):
    return pltpu.roll(v, by % v.shape[0], 0)


def iota(axis=1, shape=TILE):
    return lax.broadcasted_iota(I32, shape, axis)


def take(v, at):
    return jnp.take_along_axis(v, at & (LANES - 1), axis=1)


def pick_shift(v, by, step):
    return jnp.where(by > 0, roll(v, step), jnp.where(by < 0, roll(v, -step), v))


def slots():
    lane = iota()
    return jnp.where((lane & 7) < 4, ((lane + 64) & 127) >> 3, ((lane + 4) & 127) >> 3)


def advance(load, store, lo, count, kk, kk_row, visc):
    def first(r, p_below, p_here, p_above):
        k = kk_row(r)
        u = load(1, r) - k * (p_above - p_below)
        v = load(2, r) - k * (roll(p_here, -1) - roll(p_here, 1))
        return u, v

    p = [load(0, lo - 2 + i) for i in range(4)]
    ub, vb = first(lo - 1, p[0], p[1], p[2])
    u0, v0 = first(lo, p[1], p[2], p[3])
    p0, p1 = p[2], p[3]
    for step in range(count):
        r = lo + step
        p2 = load(0, r + 2)
        ua, va = first(r + 1, p0, p1, p2)
        un, us, vn, vs = roll(u0, -1), roll(u0, 1), roll(v0, -1), roll(v0, 1)
        store(0, r, p0 - kk * ((ua - ub) + (vn - vs)))
        store(1, r, u0 + visc * (((ua + ub) + (un + us)) - 4.0 * u0))
        store(2, r, v0 + visc * (((va + vb) + (vn + vs)) - 4.0 * v0))
        p0, p1, ub, u0, vb, v0 = p1, p2, u0, ua, v0, va


def edge_substep(p, u, v, k_in, kk, visc, keep):
    def across(w):
        return roll_rows(w, -1), roll_rows(w, 1)

    def first(i, rows):
        east, west = across(p[i])
        u1 = u[i][0:rows] - k_in[i][0:rows] * (east - west)[0:rows]
        v1 = v[i][0:rows] - k_in[i][0:rows] * (p[i + 1][0:rows] - p[i - 1][0:rows])
        return u1, v1

    u0, v0 = first(0, SPAN)
    un, vn = first(1, keep)
    us, vs = first(-1, keep)
    (ue, uw), (ve, vw) = ([w[0:keep] for w in across(x)] for x in (u0, v0))
    u0, v0, kk, visc = u0[0:keep], v0[0:keep], kk[0:keep], visc[0:keep]
    return (
        p[0][0:keep] - kk * ((ue - uw) + (vn - vs)),
        u0 + visc * (((ue + uw) + (un + us)) - 4.0 * u0),
        v0 + visc * (((ve + vw) + (vn + vs)) - 4.0 * v0),
    )


def exchange_kernel(
    sizes,
    fields,
    east_band,
    north_band,
    east_index,
    north_index,
    east_weight,
    north_weight,
    moves,
    courant,
    diffuse,
    nat,
    ext,
    mid,
    g,
    to_y,
    from_y,
    from_d,
    east_out,
    east_in,
    north_out,
    north_in,
    strip,
    stage,
    sg,
    ns,
    ns_stage,
    nso,
    hop,
    pre,
    mask,
    factor,
    done,
    eb,
    ei,
    ew,
    nb,
    nbw,
    ni,
    nw,
    ntab,
    mv,
    ks,
    qs,
    sent,
    received,
    ready,
):
    nx, ny = sizes
    gx = lax.axis_index("gx")
    gy = lax.axis_index("gy")
    total_x = nx * ROWS
    total_y = ny * WIDE
    upper_mid = ny // 2
    lower_mid = upper_mid - 1
    west, east = gx == 0, gx == nx - 1
    south, north = gy == 0, gy == ny - 1
    x_edge = jnp.logical_or(west, east)
    y_edge = jnp.logical_or(south, north)
    has_x = {-1: gx > 0, 1: gx < nx - 1}
    has_y = {-1: gy > 0, 1: gy < ny - 1}
    at_lower = gy == lower_mid
    at_upper = gy == upper_mid
    at_mid = jnp.logical_or(at_lower, at_upper)
    under_lower = gy == lower_mid - 1
    above_upper = gy == upper_mid + 1
    at_next = jnp.logical_or(under_lower, above_upper)

    def both(a, b):
        return jnp.logical_and(a, b)

    def has(dx, dy):
        if dx and dy:
            return both(has_x[dx], has_y[dy])
        return has_x[dx] if dx else has_y[dy]

    def over(dy):
        return at_lower if dy > 0 else at_upper

    odd = lax.rem(gx, 2) == 1
    even = jnp.logical_not(odd)

    seam_west = both(lax.rem(gx, RUN) == 0, gx > 0)
    seam_east = both(lax.rem(gx, RUN) == RUN - 1, gx < nx - 1)

    last_column = lax.rem(gx, RUN) == RUN - 1
    beside_last = lax.rem(gx, RUN) == RUN - 2

    barrier = pltpu.get_barrier_semaphore()

    def greet(dx, dy, there):
        @pl.when(both(has(dx, dy), there))
        def _():
            pl.semaphore_signal(barrier, inc=1, device_id=(gx + dx, gy + dy), device_id_type=MESH)

    for dy in (1, -1):
        for dx in (-1, 1, 0):
            there = over(dy)
            if dx > 0 and dy < 0:
                there = both(there, jnp.logical_not(jnp.logical_or(seam_east, beside_last)))
            greet(dx, dy, there)
    for dy in (1, -1):
        ahead = (gy + dy == lower_mid - 1) if dy > 0 else (gy + dy == upper_mid + 1)
        to_mid = (under_lower if dy > 0 else above_upper) | ahead
        for dx in (-1, 1, 0):
            greet(dx, dy, jnp.logical_not(jnp.logical_or(over(dy), to_mid)))
    for dx in (-1, 1):
        greet(dx, 0, jnp.logical_not(at_mid))

    loads = [
        pltpu.make_async_copy(
            fields.at[f, l, :, LANES * j : LANES * j + LANES], ext.at[j, f, 0:ROWS, l, :], sent.at[j & 1]
        )
        for j in (0, 2, 1)
        for f in range(3)
        for l in range(LEVELS)
    ]
    smalls = [
        pltpu.make_async_copy(s, d, sent.at[2 + k])
        for k, (s, d) in enumerate(
            ((moves, mv), (courant, ks), (diffuse, qs), (east_band, eb), (east_index, ei), (east_weight, ew))
        )
    ]
    norths = [
        pltpu.make_async_copy(s, d, sent.at[2 + k])
        for k, (s, d) in enumerate(((north_band, nb), (north_index, ni), (north_weight, nw)))
    ]
    for c in loads + smalls:
        c.start()

    def wait_bytes(block, sem):
        pltpu.make_async_copy(block, block, sem).wait()

    wait_bytes(ext.at[0:2, :, 0:ROWS], sent.at[0])

    lane = iota()
    part = lane & 15
    ext_rows = ext.reshape(9 * SPAN * LEVELS, LANES)

    def edge_windows(t):
        for f in range(3):
            low, high = None, None
            for l in range(LEVELS):
                at = (f * SPAN + 8 * t) * LEVELS + l
                head = ext_rows[pl.ds(at, 8, stride=LEVELS), :]
                tail = ext_rows[pl.ds(at + 6 * SPAN * LEVELS, 8, stride=LEVELS), :]
                v = roll(jnp.where(lane < 64, head, tail), 16 * l + 4)
                low = v if low is None else jnp.where((lane >> 4) == l, v, low)
                high = v if high is None else jnp.where((((lane + 8) >> 4) & 7) == l, v, high)
            g[0, f, 8 * t : 8 * t + 8] = low
            g[1, f, 8 * t : 8 * t + 8] = high

    for t in range(3):
        edge_windows(t)
        for d in range(2):
            v = g[d, 0, 8 * t : 8 * t + 8]
            for f in range(1, 3):
                v = jnp.where((part >> 2) == f + 1 - d, roll(g[d, f, 8 * t : 8 * t + 8], 4 * f), v)
            to_y[d, t] = v
    for c in smalls:
        c.wait()

    shift_x = mv[0, 0]
    shift_y = mv[0, 1]
    side_x = jnp.where(west, 0, 1)
    side_y = jnp.where(south, 0, 1)
    out_x = shift_x == 2 * side_x - 1
    out_y = shift_y == 2 * side_y - 1
    by_y = jnp.where(out_x, shift_y, 0)
    by_x = jnp.where(out_y, shift_x, 0)

    def east_rows():
        cell = iota(1, (1, WIDE))
        index = jnp.where(side_x == 0, ei[0:1, :], ei[1:2, :])
        upper = (index - (gy * LANES + third(cell)) + 1).astype(F32)
        weight = jnp.where(side_x == 0, ew[0:1, :], ew[1:2, :])
        wide = (LEVELS, WIDE)
        return jnp.broadcast_to(upper, wide), jnp.broadcast_to(weight, wide)

    def east_parents(b, f):
        return eb[pl.ds(side_x * 48 + f * 16 + b, LEVELS, stride=2), :]

    def north_parents(b, f):
        return nbw[pl.ds(side_y * 48 + f * 16 + b, LEVELS, stride=2), :]

    @pl.when(x_edge)
    def _():
        acc = jnp.zeros(TILE, F32)
        for b in range(2):
            for f in range(3):
                k = 3 * b + f
                near = (((lane - 8 * k + 4) & 127) >> 3) == 0
                acc = jnp.where(near, roll(east_parents(b, f), 8 * k), acc)
        east_out[0] = acc
        rows = [jnp.where(lane < 64, v[:, 0:LANES], v[:, 2 * LANES : WIDE]) for v in east_rows()]
        east_out[1] = jnp.where(iota(0) == 0, rows[0], rows[1])

    @pl.when(y_edge)
    def _():
        for c in norths:
            c.start()
        for c in norths:
            c.wait()
        nbw[...] = jnp.zeros((96, LANES), F32)
        nbw[:, 0:8] = nb[...]
        cell = iota(1, (2, ROWS))
        ntab[...] = jnp.zeros(TILE, F32)
        ntab[0:2, 0:ROWS] = (ni[...] - (gx * 8 + third(cell)) + 1).astype(F32)
        ntab[2:4, 0:ROWS] = nw[...]
        acc = jnp.zeros(TILE, F32)
        for b in range(2):
            for f in range(3):
                k = 3 * b + f
                acc = jnp.where((lane >> 3) == k, roll(north_parents(b, f), 8 * k), acc)
        north_out[0] = acc
        north_out[1] = ntab[...]

    def to(dx, dy, src, dst, send, recv):
        return pltpu.make_async_remote_copy(
            src_ref=src,
            dst_ref=dst,
            send_sem=send,
            recv_sem=recv,
            device_id=(gx + dx, gy + dy),
            device_id_type=MESH,
        )

    y_sends = {}
    for s, dy in enumerate((-1, 1)):
        group = []
        for a, dx in enumerate((-1, 1)):
            c = to(
                dx,
                dy,
                to_y.at[s, 2 * a],
                from_d.at[1 - a, 1 - s],
                sent.at[4 + 2 * a + s],
                received.at[4 + 2 * (1 - a) + 1 - s],
            )
            there = has(dx, dy)
            if dx < 0 and dy > 0:
                there = both(there, jnp.logical_not(both(at_lower, jnp.logical_or(seam_west, last_column))))
            group.append((there, c, has(-dx, -dy)))
        c = to(0, dy, to_y.at[s], from_y.at[1 - s], sent.at[2 + s], received.at[2 + 1 - s])
        group.append((has(0, dy), c, has(0, -dy)))
        send, recv = sent.at[4 + 2 * side_x + s], received.at[4 + 2 * side_x + 1 - s]
        c = to(0, dy, east_out, east_in.at[1 - s], send, recv)
        group.append((both(x_edge, has(0, dy)), c, both(x_edge, has(0, -dy))))
        y_sends[dy] = group
    x_sends = []
    north_sends = []
    for a, dx in enumerate((-1, 1)):
        for f in range(3):
            n = X_ROWS[f]
            if dx < 0:
                src, dst = ext.at[:, f, 0:n], ext.at[:, f, ROWS : ROWS + n]
            else:
                src, dst = ext.at[:, f, ROWS - n : ROWS], ext.at[:, f, SPAN - n : SPAN]
            x_sends.append((has(dx, 0), to(dx, 0, src, dst, sent.at[a], received.at[1 - a]), None))
        send, recv = sent.at[4 + 2 * a + side_y], received.at[4 + 2 * (1 - a) + side_y]
        c = to(dx, 0, north_out, north_in.at[1 - a], send, recv)
        north_sends.append((both(y_edge, has(dx, 0)), c, both(y_edge, has(-dx, 0))))

    side = jnp.where(at_upper, 1, 0)
    east_one = odd.astype(I32)
    mate = 1 - 2 * east_one
    first_hop = to(mate, 0, to_y.at[1, 2 * (1 - east_one)], hop.at[0], sent.at[8], received.at[8])
    last_hop = to(
        0, 1, hop.at[0], from_d.at[1 - east_one, 0], sent.at[8], received.at[4 + 2 * (1 - east_one)]
    )
    first_seam_hop = to(-1, 0, to_y.at[1, 0], hop.at[1], sent.at[5], received.at[9])
    last_seam_hop = to(0, 1, hop.at[1], from_d.at[1, 0], sent.at[9], received.at[6])

    def start(group, extra=None):
        for there, c, _ in group:

            @pl.when(there if extra is None else both(there, extra))
            def _(c=c):
                c.start()

    def wait_recv(group):
        for _, c, there in group:

            @pl.when(there)
            def _(c=c):
                c.wait_recv()

    count_x = 1 + has_x[-1].astype(I32) + has_x[1].astype(I32)
    count_y = 1 + has_y[-1].astype(I32) + has_y[1].astype(I32)

    wait_bytes(ext.at[1, :, 0:ROWS], sent.at[1])

    @pl.when(at_upper)
    def _():
        pl.semaphore_wait(barrier, count_x)
        start(y_sends[-1])
        pl.semaphore_wait(ready, 1)
        start(x_sends)
        start(y_sends[1])

    @pl.when(jnp.logical_not(at_mid))
    def _():
        pl.semaphore_wait(barrier, jnp.where(at_next, 2 * count_x, count_x * count_y) - 1)

        @pl.when(jnp.logical_or(under_lower, gy == lower_mid - 2))
        def _():
            pl.semaphore_signal(ready, inc=1, device_id=(gx, gy + 1), device_id_type=MESH)

        @pl.when(jnp.logical_or(above_upper, gy == upper_mid + 2))
        def _():
            pl.semaphore_signal(ready, inc=1, device_id=(gx, gy - 1), device_id_type=MESH)

        start(y_sends[-1], jnp.logical_not(under_lower))
        start(y_sends[1], jnp.logical_not(above_upper))
        start(north_sends)
        start(x_sends)

    def spread(values, level, scale):
        v = jnp.zeros(TILE, F32)
        for l in range(LEVELS):
            v = jnp.where(level == l, scale * values[l], v)
        return v

    level = iota(0)
    half = spread(ks, level, 0.5)
    visc = spread(qs, level, 1.0)
    half_w = jnp.concatenate([half] * 3, axis=1)
    visc_w = jnp.concatenate([visc] * 3, axis=1)
    nat_rows = nat.reshape(9 * ROWS * LEVELS, LANES)

    def in_first(r):
        x = gx * ROWS + r
        return jnp.where(both(x >= 3 * shift_x, x < total_x + 3 * shift_x), 1.0, 0.0).astype(F32)

    def in_second(r):
        x = gx * ROWS + r
        return jnp.where(both(x >= 0, x < total_x), 1.0, 0.0).astype(F32)

    def load_ext(f, r):
        return jnp.concatenate([ext[j, f, r & (SPAN - 1)] for j in range(3)], axis=1)

    def load_mid(f, r):
        return mid[f, r & (SPAN - 1)]

    def store_mid(f, r, v):
        mid[f, r & (SPAN - 1)] = v

    def store_nat(f, r, v):
        for j in range(3):
            at = (3 * j + f) * LEVELS * ROWS + r
            nat_rows[pl.ds(at, LEVELS, stride=ROWS), :] = v[:, LANES * j : LANES * j + LANES]

    def substep_1(lo, count, kk_row):
        advance(load_ext, store_mid, lo, count, half_w, kk_row, visc_w)

    def substep_2(lo, count, kk_row):
        advance(load_mid, store_nat, lo, count, half_w, kk_row, visc_w)

    def everywhere(r):
        return half_w

    substep_1(5, 14, everywhere)
    substep_2(7, 10, everywhere)

    @pl.when(at_next)
    def _():
        pl.semaphore_wait(ready, 1)
        start(y_sends[-1], under_lower)
        start(y_sends[1], above_upper)

    @pl.when(at_lower)
    def _():
        pl.semaphore_wait(ready, 1)

        @pl.when(last_column)
        def _():
            first_hop.start()

        @pl.when(seam_west)
        def _():
            first_seam_hop.start()

        start(x_sends)
        start(y_sends[-1])

    @pl.when(at_lower)
    def _():
        pl.semaphore_wait(barrier, count_x - jnp.logical_or(seam_west, last_column).astype(I32))
        start(y_sends[1])

        @pl.when(beside_last)
        def _():
            first_hop.wait_recv()
            last_hop.start()

        @pl.when(seam_east)
        def _():
            first_seam_hop.wait_recv()
            last_seam_hop.start()

    def blend(parents, base, upper, weight, by):
        c0 = (1.0 - upper) * (1.0 - weight)
        c1 = (1.0 - upper) * weight + upper * (1.0 - weight)
        c2 = upper * weight
        values = []
        for v in parents:
            v = pick_shift(v, by, 1)
            values.append(c0 * take(v, base - 1) + c1 * take(v, base) + c2 * take(v, base + 1))
        return values

    def outward(c):
        return jnp.where(side_x > 0, (2.0 * c + 1.0) / 6.0, (5.0 - 2.0 * c) / 6.0).astype(F32)

    @pl.when(x_edge)
    def _():
        upper, weight = east_rows()
        upper = pick_shift(upper, by_y, 3)
        weight = pick_shift(weight, by_y, 3)
        for j in range(3):
            cut = slice(LANES * j, LANES * j + LANES)
            base = third(lane + LANES * j)
            for f in range(3):
                inner, outer = blend([east_parents(b, f) for b in range(2)], base, upper[:, cut], weight[:, cut], by_y)
                for c in range(3):
                    a = outward(c)
                    strip[c, f, :, cut] = inner * (1.0 - a) + outer * a

    tall = (SPAN, LANES)
    row = iota(0, tall)
    row = jnp.where(row < SPAN - HALO, row, row - SPAN) + gx * ROWS
    part_t = iota(1, tall) & 15
    in_x1 = (row >= 3 * shift_x) & (row < total_x + 3 * shift_x)
    in_x2 = (row >= 0) & (row < total_x)
    for s, (window, origin) in enumerate((((lane >> 4), -HALO), (((lane + 8) >> 4) & 7, WIDE - 12))):
        factor[s, 0] = spread(ks, window, 0.5)
        factor[s, 1] = spread(qs, window, 1.0)
        y = (part_t if origin < 0 else ((part_t + 8) & 15)) + (origin + gy * WIDE)
        for i in range(-2, 3):
            z = y + i
            in_y = (z >= 0) & (z < total_y)
            mask[s, 0, i + 2] = jnp.where(in_x1 & (z >= 3 * shift_y) & (z < total_y + 3 * shift_y), 1.0, 0.0)
            mask[s, 1, i + 2] = jnp.where(in_x2 & in_y, 1.0, 0.0)
            mask[s, 2, i + 2] = jnp.where(in_y, 1.0, 0.0)

    sides_x = ((west, 29, 0, 28, (30, 31)), (east, 24, 21, 27, (24, 25)))
    for there, beyond, own, zero, _ in sides_x:

        @pl.when(there)
        def _(beyond=beyond, own=own, zero=zero):
            for f in range(3):
                for j in range(3):
                    cut = slice(LANES * j, LANES * j + LANES)
                    ext[j, f, zero] = jnp.zeros(TILE, F32)
                    for c in range(3):
                        ext[j, f, beyond + c] = jnp.where(out_x, strip[c, f, :, cut], 0.0)
                        ext[j, f, own + c] = jnp.where(out_x, ext[j, f, own + c], 0.0)

    def first_rows(r):
        return half_w * in_first(r)

    def second_rows(r):
        return half_w * in_second(r)

    def x_wait(sem, there):
        @pl.when(there)
        def _():
            wait_bytes(ext.at[:, 0, 0 : sum(X_ROWS)], sem)

    for turn in range(2):
        westward = odd if turn == 0 else even

        @pl.when(westward)
        def _():
            x_wait(received.at[0], has(-1, 0))

        @pl.when(jnp.logical_not(westward))
        def _():
            x_wait(received.at[1], has(1, 0))

        if turn == 1:
            edge_windows(3)
        substep_1(jnp.where(westward, -2, 19), 7, first_rows)
        for there, _, own, _, outside in sides_x:

            @pl.when(there)
            def _(own=own, outside=outside):
                for f in range(3):
                    for r in outside:
                        mid[f, r] = jnp.zeros((LEVELS, WIDE), F32)
                    for c in range(3):
                        mid[f, own + c] = jnp.where(out_x, mid[f, own + c], strip[c, f])

        substep_2(jnp.where(westward, 0, 17), 7, second_rows)

    @pl.when(y_edge)
    def _():
        wait_recv(north_sends)
        lower_band = jnp.where(has_x[-1], north_in[0, 0], 0.0)
        upper_band = jnp.where(has_x[1], north_in[1, 0], 0.0)
        lower_tab = jnp.where(has_x[-1], north_in[0, 1], 0.0)
        upper_tab = jnp.where(has_x[1], north_in[1, 1], 0.0)
        tab = jnp.where(
            lane >= 112,
            roll(lower_tab, 128 - ROWS),
            jnp.where((lane >= ROWS) & (lane < 2 * ROWS), roll(upper_tab, ROWS), ntab[...]),
        )
        tab = pick_shift(tab, by_x, 3)
        parents = []
        for b in range(2):
            for f in range(3):
                k = 3 * b + f
                v = jnp.where((lane >= 8) & (lane < 16), roll(upper_band, 8 - 8 * k), north_parents(b, f))
                parents.append(jnp.where(lane >= 120, roll(lower_band, -8 - 8 * k), v))
        place = lane & 7
        slot = slots()
        step = jnp.where(place < 4, place, place - 5).astype(F32)
        a = jnp.where(place < 4, (2.0 * step + 1.0) / 6.0, (5.0 - 2.0 * step) / 6.0)
        real = (place != 3) & (place != 4)
        for h in range(2):
            x = slot + (16 * h - HALO)
            base = third(x)
            tab_x = take(tab, x)
            upper = jnp.broadcast_to(jnp.where(side_y == 0, tab_x[0:1], tab_x[1:2]), TILE)
            weight = jnp.broadcast_to(jnp.where(side_y == 0, tab_x[2:3], tab_x[3:4]), TILE)
            whole = x + gx * ROWS - 3 * by_x
            fits = real & (whole >= 0) & (whole < total_x)
            values = blend(parents, base, upper, weight, by_x)
            for f in range(3):
                v = jnp.where(fits, values[f] * (1.0 - a) + values[3 + f] * a, 0.0)
                ns[h, f] = jnp.where(north, roll(v, -60), roll(v, -124))
        for r in range(SPAN):
            h, i = divmod(r, 16)
            for f in range(3):
                ns_stage[f, (r - HALO) % SPAN] = roll(ns[h, f], -8 * i)
        staged = ns_stage.reshape(3 * SPAN * LEVELS, LANES)
        late = jnp.where(north, 1, 0)
        for t in range(4):
            v = jnp.zeros(TILE, F32)
            for f in range(3):
                for l in range(LEVELS):
                    rows = staged[pl.ds((f * SPAN + 8 * t) * LEVELS + l, 8, stride=LEVELS), :]
                    v = jnp.where((lane >> 2) == 4 * l + f + late, roll(rows, 16 * l + 4 * f), v)
            for there, s in ((south, 0), (north, 1)):

                @pl.when(there)
                def _(s=s, t=t, v=v):
                    if t < 3:
                        from_y[s, t] = v
                    else:
                        from_d[0, s] = v
                        from_d[1, s] = v

            for f in range(3):
                nso[f, 8 * t : 8 * t + 8] = jnp.where(north, roll(v, -4 * f - 3), roll(v, -4 * f + 3))

    def east_edge_strip(s):
        band = jnp.where(jnp.where(s == 0, has_y[-1], has_y[1]), east_in[s, 0], 0.0)
        far_tab = jnp.where(jnp.where(s == 0, has_y[-1], has_y[1]), east_in[s, 1], 0.0)
        beyond = ((lane + 64 * s) & 127) >= 64
        near = []
        for k, v in enumerate(east_rows()):
            v = jnp.where(s == 0, v[:, 0:LANES], v[:, 2 * LANES : WIDE])
            v = jnp.where(beyond, jnp.broadcast_to(far_tab[k : k + 1], TILE), v)
            near.append(pick_shift(v, by_y, 3))
        base = third(jnp.where(lane < 64, lane, lane - LANES) + WIDE * s)
        for f in range(3):
            parents = []
            for b in range(2):
                k = 3 * b + f
                parents.append(jnp.where(beyond, roll(band, -8 * k), east_parents(b, f)))
            inner, outer = blend(parents, base, near[0], near[1], by_y)
            for c in range(3):
                a = outward(c)
                v = inner * (1.0 - a) + outer * a
                stage[f, c] = v
                stage[f, 5 + c] = v
            for c in (3, 4):
                stage[f, c] = jnp.zeros(TILE, F32)
        staged = stage.reshape(3 * 8 * LEVELS, LANES)
        window = ((lane + 8 * s) >> 4) & 7
        for f in range(3):
            acc = None
            for l in range(LEVELS):
                v = roll(staged[pl.ds(f * 8 * LEVELS + l, 8, stride=LEVELS), :], 16 * l + 4)
                acc = v if acc is None else jnp.where(window == l, v, acc)
            for i in range(-2, 3):
                sg[f, i + 2] = roll(acc, -i)

    sub = iota(0)
    beyond_rows = (jnp.where(west, 1, 0) * (sub >= 4).astype(I32) + jnp.where(east, 1, 0) * (sub < 4).astype(I32)) > 0
    own_low = both(west, jnp.logical_not(out_x))
    own_high = both(east, jnp.logical_not(out_x))

    reach = (2, 1, 1)

    def edge_before(s):
        for f in range(3):
            for i in range(-reach[f], reach[f] + 1):
                pre[f, i + 2] = roll(g[s, f], -i)

    def edge_side(s):
        @pl.when(x_edge)
        def _():
            east_edge_strip(s)

        k = jnp.concatenate([factor[s, 0]] * 4, axis=0)
        q = jnp.concatenate([factor[s, 1]] * 4, axis=0)
        lay_strip = both(jnp.where(s == 0, south, north), jnp.logical_not(out_y))
        head = jnp.where(sub < 4, from_d[1, s], from_d[0, s])
        arrived = jnp.concatenate([from_y[s, 0], from_y[s, 1], from_y[s, 2], head], axis=0)
        own_strip = (((part_t - 4 + 3 * s) & 15) < 3) & lay_strip
        state = []
        for f in range(3):
            ahead = {}
            for i in range(-reach[f], reach[f] + 1):
                v = jnp.where(((part_t + i - 4 * s) & 15) < 4, roll(arrived, -4 * f - i), pre[f, i + 2])
                tip = jnp.where(beyond_rows & (mask[s, 2, i + 2, 0:8] > 0.5), sg[f, i + 2], v[24:32])
                v = jnp.concatenate([v[0:24], tip], axis=0)
                ahead[i] = jnp.where(mask[s, 0, i + 2] > 0.5, v, 0.0)
            state.append(ahead)
        state = edge_substep(*state, {i: k * mask[s, 0, i + 2] for i in (-1, 0, 1)}, k, q, SPAN)
        second = mask[s, 1, 2] > 0.5
        laid = []
        for f in range(3):
            v = state[f]
            low = jnp.where((sub < 3) & own_low, sg[f, 2], v[0:8])
            high = jnp.where((sub >= 5) & own_high, sg[f, 2], v[16:24])
            v = jnp.concatenate([low, v[8:16], high, v[24:32]], axis=0)
            v = jnp.where(own_strip, nso[f], v)
            v = jnp.where(second, v, 0.0)
            near = v if f == 0 else v[0:ROWS]
            ahead = {0: v, 1: roll(near, -1), -1: roll(near, 1)}
            if f == 0:
                ahead[2], ahead[-2] = roll(v[0:ROWS], -2), roll(v[0:ROWS], 2)
            laid.append(ahead)
        return edge_substep(*laid, {i: k * mask[s, 1, i + 2] for i in (-1, 0, 1)}, k, q, ROWS)

    @pl.when(at_upper)
    def _():
        wait_recv(y_sends[-1])

    @pl.when(jnp.logical_not(at_upper))
    def _():
        wait_recv(y_sends[1])

    edge_before(side)
    for f, v in enumerate(edge_side(side)):
        done[f] = v
    edge_before(1 - side)

    for a, dx in enumerate((-1, 1)):
        x_wait(sent.at[a], has(dx, 0))
    for there, c, _ in y_sends[-1] + y_sends[1] + north_sends:

        @pl.when(there)
        def _(c=c):
            c.wait_send()

    @pl.when(both(at_lower, last_column))
    def _():
        first_hop.wait_send()

    @pl.when(both(at_lower, beside_last))
    def _():
        last_hop.wait_send()

    @pl.when(both(at_lower, seam_west))
    def _():
        first_seam_hop.wait_send()

    @pl.when(both(at_lower, seam_east))
    def _():
        last_seam_hop.wait_send()

    @pl.when(at_upper)
    def _():
        wait_recv(y_sends[1])

    @pl.when(jnp.logical_not(at_upper))
    def _():
        wait_recv(y_sends[-1])

    lane_r = iota(1, (ROWS, LANES))
    ahead = ((((lane_r & 15) + 12) & 15) < 8).astype(I32)
    fresh = ahead == side
    for f, v in enumerate(edge_side(1 - side)):
        v = jnp.where(fresh, v, done[f])
        for l in range(LEVELS):
            m = roll(v, -16 * l - 4)
            nat[0, f, l] = jnp.where(lane_r < 8, m, nat[0, f, l])
            nat[2, f, l] = jnp.where(lane_r >= 120, m, nat[2, f, l])


def write_kernel(ready, out, sem):
    for j in range(3):
        pltpu.make_async_copy(ready.at[j], out.at[:, :, :, LANES * j : LANES * j + LANES], sem).start()
    pltpu.make_async_copy(ready, ready, sem).wait()


def body(
    sizes,
    fields,
    east_band,
    north_band,
    east_index,
    north_index,
    east_weight,
    north_weight,
    nest_moves,
    courant,
    diffuse,
):
    vmem = pltpu.VMEM
    dma = pltpu.SemaphoreType.DMA
    ready = pl.pallas_call(
        functools.partial(exchange_kernel, sizes),
        out_shape=vmem((3, 3, LEVELS, ROWS, LANES), F32),
        in_specs=[pl.BlockSpec(memory_space=pl.ANY)] * 10,
        out_specs=pl.BlockSpec(memory_space=pltpu.VMEM),
        scratch_shapes=[
            vmem((3, 3, SPAN) + TILE, F32),
            vmem((3, SPAN, LEVELS, WIDE), F32),
            vmem((2, 3, SPAN, LANES), F32),
            vmem((2, 3) + TILE, F32),
            vmem((2, 3) + TILE, F32),
            vmem((2, 2) + TILE, F32),
            vmem((2,) + TILE, F32),
            vmem((2, 2) + TILE, F32),
            vmem((2,) + TILE, F32),
            vmem((2, 2) + TILE, F32),
            vmem((3, 3, LEVELS, WIDE), F32),
            vmem((3, 8) + TILE, F32),
            vmem((3, 5) + TILE, F32),
            vmem((2, 3) + TILE, F32),
            vmem((3, SPAN) + TILE, F32),
            vmem((3, SPAN, LANES), F32),
            vmem((2,) + TILE, F32),
            vmem((3, 5, SPAN, LANES), F32),
            vmem((2, 3, 5, SPAN, LANES), F32),
            vmem((2, 2) + TILE, F32),
            vmem((3, ROWS, LANES), F32),
            vmem((96, LANES), F32),
            vmem((2, WIDE), I32),
            vmem((2, WIDE), F32),
            vmem((96, 8), F32),
            vmem((96, LANES), F32),
            vmem((2, ROWS), I32),
            vmem((2, ROWS), F32),
            vmem(TILE, F32),
            pltpu.SMEM((2, 2), I32),
            pltpu.SMEM((LEVELS,), F32),
            pltpu.SMEM((LEVELS,), F32),
            dma((10,)),
            dma((10,)),
            pltpu.SemaphoreType.REGULAR,
        ],
        compiler_params=pltpu.CompilerParams(
            collective_id=0, has_side_effects=True, vmem_limit_bytes=VMEM_A
        ),
    )(
        fields,
        east_band.reshape(96, LANES),
        north_band.reshape(96, 8),
        east_index,
        north_index,
        east_weight,
        north_weight,
        nest_moves,
        courant,
        diffuse,
    )
    return pl.pallas_call(
        write_kernel,
        out_shape=jax.ShapeDtypeStruct(fields.shape, F32),
        in_specs=[pl.BlockSpec(memory_space=pltpu.VMEM)],
        out_specs=pl.BlockSpec(memory_space=pl.ANY),
        scratch_shapes=[dma],
        compiler_params=pltpu.CompilerParams(vmem_limit_bytes=VMEM_B),
    )(ready)


VMEM_A = 56 * 1024 * 1024
VMEM_B = 8 * 1024 * 1024


def solution(mesh):
    sizes = (mesh.shape["gx"], mesh.shape["gy"])
    return jax.shard_map(
        functools.partial(body, sizes),
        mesh=mesh,
        in_specs=(
            P(None, None, "gx", "gy"),
            P(None, None, None, None, "gy"),
            P(None, None, None, None, "gx"),
            P(None, "gy"),
            P(None, "gx"),
            P(None, "gy"),
            P(None, "gx"),
            P(),
            P(),
            P(),
        ),
        out_specs=P(None, None, "gx", "gy"),
        check_vma=False,
    )
```

```python
import functools

import jax
import jax.numpy as jnp
from jax import lax
from jax.experimental import pallas as pl
from jax.experimental.pallas import tpu as pltpu
from jax.sharding import PartitionSpec as P

MESH = pl.DeviceIdType.MESH
F32 = jnp.float32
I32 = jnp.int32
HALO = 4
ROWS = 24
SPAN = ROWS + 2 * HALO
WIDE = 384
LANES = 128
LEVELS = 8
X_ROWS = (4, 3, 2)
RUN = 8
TILE = (LEVELS, LANES)


def third(v):
    return (((v + 48) * 43691) >> 17) - 16


def roll(v, by):
    by = by % v.shape[1]
    return pltpu.roll(v, by, 1) if by else v


def roll_rows(v, by):
    return pltpu.roll(v, by % v.shape[0], 0)


def iota(axis=1, shape=TILE):
    return lax.broadcasted_iota(I32, shape, axis)


def take(v, at):
    return jnp.take_along_axis(v, at & (LANES - 1), axis=1)


def pick_shift(v, by, step):
    return jnp.where(by > 0, roll(v, step), jnp.where(by < 0, roll(v, -step), v))


def slots():
    lane = iota()
    return jnp.where((lane & 7) < 4, ((lane + 64) & 127) >> 3, ((lane + 4) & 127) >> 3)


def advance(load, store, lo, count, kk, kk_row, visc):
    def first(r, p_below, p_here, p_above):
        k = kk_row(r)
        u = load(1, r) - k * (p_above - p_below)
        v = load(2, r) - k * (roll(p_here, -1) - roll(p_here, 1))
        return u, v

    p = [load(0, lo - 2 + i) for i in range(4)]
    ub, vb = first(lo - 1, p[0], p[1], p[2])
    u0, v0 = first(lo, p[1], p[2], p[3])
    p0, p1 = p[2], p[3]
    for step in range(count):
        r = lo + step
        p2 = load(0, r + 2)
        ua, va = first(r + 1, p0, p1, p2)
        un, us, vn, vs = roll(u0, -1), roll(u0, 1), roll(v0, -1), roll(v0, 1)
        store(0, r, p0 - kk * ((ua - ub) + (vn - vs)))
        store(1, r, u0 + visc * (((ua + ub) + (un + us)) - 4.0 * u0))
        store(2, r, v0 + visc * (((va + vb) + (vn + vs)) - 4.0 * v0))
        p0, p1, ub, u0, vb, v0 = p1, p2, u0, ua, v0, va


def edge_substep(p, u, v, k_in, kk, visc, keep):
    def across(w):
        return roll_rows(w, -1), roll_rows(w, 1)

    def first(i, rows):
        east, west = across(p[i])
        u1 = u[i][0:rows] - k_in[i][0:rows] * (east - west)[0:rows]
        v1 = v[i][0:rows] - k_in[i][0:rows] * (p[i + 1][0:rows] - p[i - 1][0:rows])
        return u1, v1

    u0, v0 = first(0, SPAN)
    un, vn = first(1, keep)
    us, vs = first(-1, keep)
    (ue, uw), (ve, vw) = ([w[0:keep] for w in across(x)] for x in (u0, v0))
    u0, v0, kk, visc = u0[0:keep], v0[0:keep], kk[0:keep], visc[0:keep]
    return (
        p[0][0:keep] - kk * ((ue - uw) + (vn - vs)),
        u0 + visc * (((ue + uw) + (un + us)) - 4.0 * u0),
        v0 + visc * (((ve + vw) + (vn + vs)) - 4.0 * v0),
    )


def exchange_kernel(
    sizes,
    fields,
    east_band,
    north_band,
    east_index,
    north_index,
    east_weight,
    north_weight,
    moves,
    courant,
    diffuse,
    nat,
    ext,
    mid,
    g,
    to_y,
    from_y,
    from_d,
    east_out,
    east_in,
    north_out,
    north_in,
    strip,
    stage,
    sg,
    ns,
    ns_stage,
    nso,
    hop,
    pre,
    mask,
    factor,
    done,
    eb,
    ei,
    ew,
    nb,
    nbw,
    ni,
    nw,
    ntab,
    mv,
    ks,
    qs,
    sent,
    received,
    ready,
):
    nx, ny = sizes
    gx = lax.axis_index("gx")
    gy = lax.axis_index("gy")
    total_x = nx * ROWS
    total_y = ny * WIDE
    upper_mid = ny // 2
    lower_mid = upper_mid - 1
    west, east = gx == 0, gx == nx - 1
    south, north = gy == 0, gy == ny - 1
    x_edge = jnp.logical_or(west, east)
    y_edge = jnp.logical_or(south, north)
    has_x = {-1: gx > 0, 1: gx < nx - 1}
    has_y = {-1: gy > 0, 1: gy < ny - 1}
    at_lower = gy == lower_mid
    at_upper = gy == upper_mid
    at_mid = jnp.logical_or(at_lower, at_upper)
    under_lower = gy == lower_mid - 1
    above_upper = gy == upper_mid + 1
    at_next = jnp.logical_or(under_lower, above_upper)

    def both(a, b):
        return jnp.logical_and(a, b)

    def has(dx, dy):
        if dx and dy:
            return both(has_x[dx], has_y[dy])
        return has_x[dx] if dx else has_y[dy]

    def over(dy):
        return at_lower if dy > 0 else at_upper

    odd = lax.rem(gx, 2) == 1
    even = jnp.logical_not(odd)

    seam_west = both(lax.rem(gx, RUN) == 0, gx > 0)
    seam_east = both(lax.rem(gx, RUN) == RUN - 1, gx < nx - 1)

    last_column = lax.rem(gx, RUN) == RUN - 1
    beside_last = lax.rem(gx, RUN) == RUN - 2

    barrier = pltpu.get_barrier_semaphore()

    def greet(dx, dy, there):
        @pl.when(both(has(dx, dy), there))
        def _():
            pl.semaphore_signal(barrier, inc=1, device_id=(gx + dx, gy + dy), device_id_type=MESH)

    for dy in (1, -1):
        for dx in (-1, 1, 0):
            there = over(dy)
            if dx > 0 and dy < 0:
                there = both(there, jnp.logical_not(jnp.logical_or(seam_east, beside_last)))
            greet(dx, dy, there)
    for dy in (1, -1):
        ahead = (gy + dy == lower_mid - 1) if dy > 0 else (gy + dy == upper_mid + 1)
        to_mid = (under_lower if dy > 0 else above_upper) | ahead
        for dx in (-1, 1, 0):
            greet(dx, dy, jnp.logical_not(jnp.logical_or(over(dy), to_mid)))
    for dx in (-1, 1):
        greet(dx, 0, jnp.logical_not(at_mid))

    loads = [
        pltpu.make_async_copy(
            fields.at[f, l, :, LANES * j : LANES * j + LANES], ext.at[j, f, 0:ROWS, l, :], sent.at[j & 1]
        )
        for j in (0, 2, 1)
        for f in range(3)
        for l in range(LEVELS)
    ]
    smalls = [
        pltpu.make_async_copy(s, d, sent.at[2 + k])
        for k, (s, d) in enumerate(
            ((moves, mv), (courant, ks), (diffuse, qs), (east_band, eb), (east_index, ei), (east_weight, ew))
        )
    ]
    norths = [
        pltpu.make_async_copy(s, d, sent.at[2 + k])
        for k, (s, d) in enumerate(((north_band, nb), (north_index, ni), (north_weight, nw)))
    ]
    for c in loads + smalls:
        c.start()

    def wait_bytes(block, sem):
        pltpu.make_async_copy(block, block, sem).wait()

    wait_bytes(ext.at[0:2, :, 0:ROWS], sent.at[0])

    lane = iota()
    part = lane & 15
    ext_rows = ext.reshape(9 * SPAN * LEVELS, LANES)

    def edge_windows(t):
        for f in range(3):
            low, high = None, None
            for l in range(LEVELS):
                at = (f * SPAN + 8 * t) * LEVELS + l
                head = ext_rows[pl.ds(at, 8, stride=LEVELS), :]
                tail = ext_rows[pl.ds(at + 6 * SPAN * LEVELS, 8, stride=LEVELS), :]
                v = roll(jnp.where(lane < 64, head, tail), 16 * l + 4)
                low = v if low is None else jnp.where((lane >> 4) == l, v, low)
                high = v if high is None else jnp.where((((lane + 8) >> 4) & 7) == l, v, high)
            g[0, f, 8 * t : 8 * t + 8] = low
            g[1, f, 8 * t : 8 * t + 8] = high

    for t in range(3):
        edge_windows(t)
        for d in range(2):
            v = g[d, 0, 8 * t : 8 * t + 8]
            for f in range(1, 3):
                v = jnp.where((part >> 2) == f + 1 - d, roll(g[d, f, 8 * t : 8 * t + 8], 4 * f), v)
            to_y[d, t] = v
    for c in smalls:
        c.wait()

    shift_x = mv[0, 0]
    shift_y = mv[0, 1]
    side_x = jnp.where(west, 0, 1)
    side_y = jnp.where(south, 0, 1)
    out_x = shift_x == 2 * side_x - 1
    out_y = shift_y == 2 * side_y - 1
    by_y = jnp.where(out_x, shift_y, 0)
    by_x = jnp.where(out_y, shift_x, 0)

    def east_rows():
        cell = iota(1, (1, WIDE))
        index = jnp.where(side_x == 0, ei[0:1, :], ei[1:2, :])
        upper = (index - (gy * LANES + third(cell)) + 1).astype(F32)
        weight = jnp.where(side_x == 0, ew[0:1, :], ew[1:2, :])
        wide = (LEVELS, WIDE)
        return jnp.broadcast_to(upper, wide), jnp.broadcast_to(weight, wide)

    def east_parents(b, f):
        return eb[pl.ds(side_x * 48 + f * 16 + b, LEVELS, stride=2), :]

    def north_parents(b, f):
        return nbw[pl.ds(side_y * 48 + f * 16 + b, LEVELS, stride=2), :]

    @pl.when(x_edge)
    def _():
        acc = jnp.zeros(TILE, F32)
        for b in range(2):
            for f in range(3):
                k = 3 * b + f
                near = (((lane - 8 * k + 4) & 127) >> 3) == 0
                acc = jnp.where(near, roll(east_parents(b, f), 8 * k), acc)
        east_out[0] = acc
        rows = [jnp.where(lane < 64, v[:, 0:LANES], v[:, 2 * LANES : WIDE]) for v in east_rows()]
        east_out[1] = jnp.where(iota(0) == 0, rows[0], rows[1])

    @pl.when(y_edge)
    def _():
        for c in norths:
            c.start()
        for c in norths:
            c.wait()
        nbw[...] = jnp.zeros((96, LANES), F32)
        nbw[:, 0:8] = nb[...]
        cell = iota(1, (2, ROWS))
        ntab[...] = jnp.zeros(TILE, F32)
        ntab[0:2, 0:ROWS] = (ni[...] - (gx * 8 + third(cell)) + 1).astype(F32)
        ntab[2:4, 0:ROWS] = nw[...]
        acc = jnp.zeros(TILE, F32)
        for b in range(2):
            for f in range(3):
                k = 3 * b + f
                acc = jnp.where((lane >> 3) == k, roll(north_parents(b, f), 8 * k), acc)
        north_out[0] = acc
        north_out[1] = ntab[...]

    def to(dx, dy, src, dst, send, recv):
        return pltpu.make_async_remote_copy(
            src_ref=src,
            dst_ref=dst,
            send_sem=send,
            recv_sem=recv,
            device_id=(gx + dx, gy + dy),
            device_id_type=MESH,
        )

    y_sends = {}
    for s, dy in enumerate((-1, 1)):
        group = []
        for a, dx in enumerate((-1, 1)):
            c = to(
                dx,
                dy,
                to_y.at[s, 2 * a],
                from_d.at[1 - a, 1 - s],
                sent.at[4 + 2 * a + s],
                received.at[4 + 2 * (1 - a) + 1 - s],
            )
            there = has(dx, dy)
            if dx < 0 and dy > 0:
                there = both(there, jnp.logical_not(both(at_lower, jnp.logical_or(seam_west, last_column))))
            group.append((there, c, has(-dx, -dy)))
        c = to(0, dy, to_y.at[s], from_y.at[1 - s], sent.at[2 + s], received.at[2 + 1 - s])
        group.append((has(0, dy), c, has(0, -dy)))
        send, recv = sent.at[4 + 2 * side_x + s], received.at[4 + 2 * side_x + 1 - s]
        c = to(0, dy, east_out, east_in.at[1 - s], send, recv)
        group.append((both(x_edge, has(0, dy)), c, both(x_edge, has(0, -dy))))
        y_sends[dy] = group
    x_sends = []
    north_sends = []
    for a, dx in enumerate((-1, 1)):
        for f in range(3):
            n = X_ROWS[f]
            if dx < 0:
                src, dst = ext.at[:, f, 0:n], ext.at[:, f, ROWS : ROWS + n]
            else:
                src, dst = ext.at[:, f, ROWS - n : ROWS], ext.at[:, f, SPAN - n : SPAN]
            x_sends.append((has(dx, 0), to(dx, 0, src, dst, sent.at[a], received.at[1 - a]), None))
        send, recv = sent.at[4 + 2 * a + side_y], received.at[4 + 2 * (1 - a) + side_y]
        c = to(dx, 0, north_out, north_in.at[1 - a], send, recv)
        north_sends.append((both(y_edge, has(dx, 0)), c, both(y_edge, has(-dx, 0))))

    side = jnp.where(at_upper, 1, 0)
    east_one = odd.astype(I32)
    mate = 1 - 2 * east_one
    first_hop = to(mate, 0, to_y.at[1, 2 * (1 - east_one)], hop.at[0], sent.at[8], received.at[8])
    last_hop = to(
        0, 1, hop.at[0], from_d.at[1 - east_one, 0], sent.at[8], received.at[4 + 2 * (1 - east_one)]
    )
    first_seam_hop = to(-1, 0, to_y.at[1, 0], hop.at[1], sent.at[5], received.at[9])
    last_seam_hop = to(0, 1, hop.at[1], from_d.at[1, 0], sent.at[9], received.at[6])

    def start(group, extra=None):
        for there, c, _ in group:

            @pl.when(there if extra is None else both(there, extra))
            def _(c=c):
                c.start()

    def wait_recv(group):
        for _, c, there in group:

            @pl.when(there)
            def _(c=c):
                c.wait_recv()

    count_x = 1 + has_x[-1].astype(I32) + has_x[1].astype(I32)
    count_y = 1 + has_y[-1].astype(I32) + has_y[1].astype(I32)

    wait_bytes(ext.at[1, :, 0:ROWS], sent.at[1])

    @pl.when(at_upper)
    def _():
        pl.semaphore_wait(barrier, count_x)
        start(y_sends[-1])
        pl.semaphore_wait(ready, 1)
        start(x_sends)
        start(y_sends[1])

    @pl.when(jnp.logical_not(at_mid))
    def _():
        pl.semaphore_wait(barrier, jnp.where(at_next, 2 * count_x, count_x * count_y) - 1)

        @pl.when(jnp.logical_or(under_lower, gy == lower_mid - 2))
        def _():
            pl.semaphore_signal(ready, inc=1, device_id=(gx, gy + 1), device_id_type=MESH)

        @pl.when(jnp.logical_or(above_upper, gy == upper_mid + 2))
        def _():
            pl.semaphore_signal(ready, inc=1, device_id=(gx, gy - 1), device_id_type=MESH)

        start(y_sends[-1], jnp.logical_not(under_lower))
        start(y_sends[1], jnp.logical_not(above_upper))
        start(north_sends)
        start(x_sends)

    def spread(values, level, scale):
        v = jnp.zeros(TILE, F32)
        for l in range(LEVELS):
            v = jnp.where(level == l, scale * values[l], v)
        return v

    level = iota(0)
    half = spread(ks, level, 0.5)
    visc = spread(qs, level, 1.0)
    half_w = jnp.concatenate([half] * 3, axis=1)
    visc_w = jnp.concatenate([visc] * 3, axis=1)
    nat_rows = nat.reshape(9 * ROWS * LEVELS, LANES)

    def in_first(r):
        x = gx * ROWS + r
        return jnp.where(both(x >= 3 * shift_x, x < total_x + 3 * shift_x), 1.0, 0.0).astype(F32)

    def in_second(r):
        x = gx * ROWS + r
        return jnp.where(both(x >= 0, x < total_x), 1.0, 0.0).astype(F32)

    def load_ext(f, r):
        return jnp.concatenate([ext[j, f, r & (SPAN - 1)] for j in range(3)], axis=1)

    def load_mid(f, r):
        return mid[f, r & (SPAN - 1)]

    def store_mid(f, r, v):
        mid[f, r & (SPAN - 1)] = v

    def store_nat(f, r, v):
        for j in range(3):
            at = (3 * j + f) * LEVELS * ROWS + r
            nat_rows[pl.ds(at, LEVELS, stride=ROWS), :] = v[:, LANES * j : LANES * j + LANES]

    def substep_1(lo, count, kk_row):
        advance(load_ext, store_mid, lo, count, half_w, kk_row, visc_w)

    def substep_2(lo, count, kk_row):
        advance(load_mid, store_nat, lo, count, half_w, kk_row, visc_w)

    def everywhere(r):
        return half_w

    substep_1(5, 14, everywhere)
    substep_2(7, 10, everywhere)

    @pl.when(at_next)
    def _():
        pl.semaphore_wait(ready, 1)
        start(y_sends[-1], under_lower)
        start(y_sends[1], above_upper)

    @pl.when(at_lower)
    def _():
        pl.semaphore_wait(ready, 1)

        @pl.when(last_column)
        def _():
            first_hop.start()

        @pl.when(seam_west)
        def _():
            first_seam_hop.start()

        start(x_sends)
        start(y_sends[-1])

    @pl.when(at_lower)
    def _():
        pl.semaphore_wait(barrier, count_x - jnp.logical_or(seam_west, last_column).astype(I32))
        start(y_sends[1])

        @pl.when(beside_last)
        def _():
            first_hop.wait_recv()
            last_hop.start()

        @pl.when(seam_east)
        def _():
            first_seam_hop.wait_recv()
            last_seam_hop.start()

    def blend(parents, base, upper, weight, by):
        c0 = (1.0 - upper) * (1.0 - weight)
        c1 = (1.0 - upper) * weight + upper * (1.0 - weight)
        c2 = upper * weight
        values = []
        for v in parents:
            v = pick_shift(v, by, 1)
            values.append(c0 * take(v, base - 1) + c1 * take(v, base) + c2 * take(v, base + 1))
        return values

    def outward(c):
        return jnp.where(side_x > 0, (2.0 * c + 1.0) / 6.0, (5.0 - 2.0 * c) / 6.0).astype(F32)

    @pl.when(x_edge)
    def _():
        upper, weight = east_rows()
        upper = pick_shift(upper, by_y, 3)
        weight = pick_shift(weight, by_y, 3)
        for j in range(3):
            cut = slice(LANES * j, LANES * j + LANES)
            base = third(lane + LANES * j)
            for f in range(3):
                inner, outer = blend([east_parents(b, f) for b in range(2)], base, upper[:, cut], weight[:, cut], by_y)
                for c in range(3):
                    a = outward(c)
                    strip[c, f, :, cut] = inner * (1.0 - a) + outer * a

    tall = (SPAN, LANES)
    row = iota(0, tall)
    row = jnp.where(row < SPAN - HALO, row, row - SPAN) + gx * ROWS
    part_t = iota(1, tall) & 15
    in_x1 = (row >= 3 * shift_x) & (row < total_x + 3 * shift_x)
    in_x2 = (row >= 0) & (row < total_x)
    for s, (window, origin) in enumerate((((lane >> 4), -HALO), (((lane + 8) >> 4) & 7, WIDE - 12))):
        factor[s, 0] = spread(ks, window, 0.5)
        factor[s, 1] = spread(qs, window, 1.0)
        y = (part_t if origin < 0 else ((part_t + 8) & 15)) + (origin + gy * WIDE)
        for i in range(-2, 3):
            z = y + i
            in_y = (z >= 0) & (z < total_y)
            mask[s, 0, i + 2] = jnp.where(in_x1 & (z >= 3 * shift_y) & (z < total_y + 3 * shift_y), 1.0, 0.0)
            mask[s, 1, i + 2] = jnp.where(in_x2 & in_y, 1.0, 0.0)
            mask[s, 2, i + 2] = jnp.where(in_y, 1.0, 0.0)

    sides_x = ((west, 29, 0, 28, (30, 31)), (east, 24, 21, 27, (24, 25)))
    for there, beyond, own, zero, _ in sides_x:

        @pl.when(there)
        def _(beyond=beyond, own=own, zero=zero):
            for f in range(3):
                for j in range(3):
                    cut = slice(LANES * j, LANES * j + LANES)
                    ext[j, f, zero] = jnp.zeros(TILE, F32)
                    for c in range(3):
                        ext[j, f, beyond + c] = jnp.where(out_x, strip[c, f, :, cut], 0.0)
                        ext[j, f, own + c] = jnp.where(out_x, ext[j, f, own + c], 0.0)

    def first_rows(r):
        return half_w * in_first(r)

    def second_rows(r):
        return half_w * in_second(r)

    def x_wait(sem, there):
        @pl.when(there)
        def _():
            wait_bytes(ext.at[:, 0, 0 : sum(X_ROWS)], sem)

    for turn in range(2):
        westward = odd if turn == 0 else even

        @pl.when(westward)
        def _():
            x_wait(received.at[0], has(-1, 0))

        @pl.when(jnp.logical_not(westward))
        def _():
            x_wait(received.at[1], has(1, 0))

        if turn == 1:
            edge_windows(3)
        substep_1(jnp.where(westward, -2, 19), 7, first_rows)
        for there, _, own, _, outside in sides_x:

            @pl.when(there)
            def _(own=own, outside=outside):
                for f in range(3):
                    for r in outside:
                        mid[f, r] = jnp.zeros((LEVELS, WIDE), F32)
                    for c in range(3):
                        mid[f, own + c] = jnp.where(out_x, mid[f, own + c], strip[c, f])

        substep_2(jnp.where(westward, 0, 17), 7, second_rows)

    @pl.when(y_edge)
    def _():
        wait_recv(north_sends)
        lower_band = jnp.where(has_x[-1], north_in[0, 0], 0.0)
        upper_band = jnp.where(has_x[1], north_in[1, 0], 0.0)
        lower_tab = jnp.where(has_x[-1], north_in[0, 1], 0.0)
        upper_tab = jnp.where(has_x[1], north_in[1, 1], 0.0)
        tab = jnp.where(
            lane >= 112,
            roll(lower_tab, 128 - ROWS),
            jnp.where((lane >= ROWS) & (lane < 2 * ROWS), roll(upper_tab, ROWS), ntab[...]),
        )
        tab = pick_shift(tab, by_x, 3)
        parents = []
        for b in range(2):
            for f in range(3):
                k = 3 * b + f
                v = jnp.where((lane >= 8) & (lane < 16), roll(upper_band, 8 - 8 * k), north_parents(b, f))
                parents.append(jnp.where(lane >= 120, roll(lower_band, -8 - 8 * k), v))
        place = lane & 7
        slot = slots()
        step = jnp.where(place < 4, place, place - 5).astype(F32)
        a = jnp.where(place < 4, (2.0 * step + 1.0) / 6.0, (5.0 - 2.0 * step) / 6.0)
        real = (place != 3) & (place != 4)
        for h in range(2):
            x = slot + (16 * h - HALO)
            base = third(x)
            tab_x = take(tab, x)
            upper = jnp.broadcast_to(jnp.where(side_y == 0, tab_x[0:1], tab_x[1:2]), TILE)
            weight = jnp.broadcast_to(jnp.where(side_y == 0, tab_x[2:3], tab_x[3:4]), TILE)
            whole = x + gx * ROWS - 3 * by_x
            fits = real & (whole >= 0) & (whole < total_x)
            values = blend(parents, base, upper, weight, by_x)
            for f in range(3):
                v = jnp.where(fits, values[f] * (1.0 - a) + values[3 + f] * a, 0.0)
                ns[h, f] = jnp.where(north, roll(v, -60), roll(v, -124))
        for r in range(SPAN):
            h, i = divmod(r, 16)
            for f in range(3):
                ns_stage[f, (r - HALO) % SPAN] = roll(ns[h, f], -8 * i)
        staged = ns_stage.reshape(3 * SPAN * LEVELS, LANES)
        late = jnp.where(north, 1, 0)
        for t in range(4):
            v = jnp.zeros(TILE, F32)
            for f in range(3):
                for l in range(LEVELS):
                    rows = staged[pl.ds((f * SPAN + 8 * t) * LEVELS + l, 8, stride=LEVELS), :]
                    v = jnp.where((lane >> 2) == 4 * l + f + late, roll(rows, 16 * l + 4 * f), v)
            for there, s in ((south, 0), (north, 1)):

                @pl.when(there)
                def _(s=s, t=t, v=v):
                    if t < 3:
                        from_y[s, t] = v
                    else:
                        from_d[0, s] = v
                        from_d[1, s] = v

            for f in range(3):
                nso[f, 8 * t : 8 * t + 8] = jnp.where(north, roll(v, -4 * f - 3), roll(v, -4 * f + 3))

    def east_edge_strip(s):
        band = jnp.where(jnp.where(s == 0, has_y[-1], has_y[1]), east_in[s, 0], 0.0)
        far_tab = jnp.where(jnp.where(s == 0, has_y[-1], has_y[1]), east_in[s, 1], 0.0)
        beyond = ((lane + 64 * s) & 127) >= 64
        near = []
        for k, v in enumerate(east_rows()):
            v = jnp.where(s == 0, v[:, 0:LANES], v[:, 2 * LANES : WIDE])
            v = jnp.where(beyond, jnp.broadcast_to(far_tab[k : k + 1], TILE), v)
            near.append(pick_shift(v, by_y, 3))
        base = third(jnp.where(lane < 64, lane, lane - LANES) + WIDE * s)
        for f in range(3):
            parents = []
            for b in range(2):
                k = 3 * b + f
                parents.append(jnp.where(beyond, roll(band, -8 * k), east_parents(b, f)))
            inner, outer = blend(parents, base, near[0], near[1], by_y)
            for c in range(3):
                a = outward(c)
                v = inner * (1.0 - a) + outer * a
                stage[f, c] = v
                stage[f, 5 + c] = v
            for c in (3, 4):
                stage[f, c] = jnp.zeros(TILE, F32)
        staged = stage.reshape(3 * 8 * LEVELS, LANES)
        window = ((lane + 8 * s) >> 4) & 7
        for f in range(3):
            acc = None
            for l in range(LEVELS):
                v = roll(staged[pl.ds(f * 8 * LEVELS + l, 8, stride=LEVELS), :], 16 * l + 4)
                acc = v if acc is None else jnp.where(window == l, v, acc)
            for i in range(-2, 3):
                sg[f, i + 2] = roll(acc, -i)

    sub = iota(0)
    beyond_rows = (jnp.where(west, 1, 0) * (sub >= 4).astype(I32) + jnp.where(east, 1, 0) * (sub < 4).astype(I32)) > 0
    own_low = both(west, jnp.logical_not(out_x))
    own_high = both(east, jnp.logical_not(out_x))

    reach = (2, 1, 1)

    def edge_before(s):
        for f in range(3):
            for i in range(-reach[f], reach[f] + 1):
                pre[f, i + 2] = roll(g[s, f], -i)

    def edge_side(s):
        @pl.when(x_edge)
        def _():
            east_edge_strip(s)

        k = jnp.concatenate([factor[s, 0]] * 4, axis=0)
        q = jnp.concatenate([factor[s, 1]] * 4, axis=0)
        lay_strip = both(jnp.where(s == 0, south, north), jnp.logical_not(out_y))
        head = jnp.where(sub < 4, from_d[1, s], from_d[0, s])
        arrived = jnp.concatenate([from_y[s, 0], from_y[s, 1], from_y[s, 2], head], axis=0)
        own_strip = (((part_t - 4 + 3 * s) & 15) < 3) & lay_strip
        state = []
        for f in range(3):
            ahead = {}
            for i in range(-reach[f], reach[f] + 1):
                v = jnp.where(((part_t + i - 4 * s) & 15) < 4, roll(arrived, -4 * f - i), pre[f, i + 2])
                tip = jnp.where(beyond_rows & (mask[s, 2, i + 2, 0:8] > 0.5), sg[f, i + 2], v[24:32])
                v = jnp.concatenate([v[0:24], tip], axis=0)
                ahead[i] = jnp.where(mask[s, 0, i + 2] > 0.5, v, 0.0)
            state.append(ahead)
        state = edge_substep(*state, {i: k * mask[s, 0, i + 2] for i in (-1, 0, 1)}, k, q, SPAN)
        second = mask[s, 1, 2] > 0.5
        laid = []
        for f in range(3):
            v = state[f]
            low = jnp.where((sub < 3) & own_low, sg[f, 2], v[0:8])
            high = jnp.where((sub >= 5) & own_high, sg[f, 2], v[16:24])
            v = jnp.concatenate([low, v[8:16], high, v[24:32]], axis=0)
            v = jnp.where(own_strip, nso[f], v)
            v = jnp.where(second, v, 0.0)
            near = v if f == 0 else v[0:ROWS]
            ahead = {0: v, 1: roll(near, -1), -1: roll(near, 1)}
            if f == 0:
                ahead[2], ahead[-2] = roll(v[0:ROWS], -2), roll(v[0:ROWS], 2)
            laid.append(ahead)
        return edge_substep(*laid, {i: k * mask[s, 1, i + 2] for i in (-1, 0, 1)}, k, q, ROWS)

    @pl.when(at_upper)
    def _():
        wait_recv(y_sends[-1])

    @pl.when(jnp.logical_not(at_upper))
    def _():
        wait_recv(y_sends[1])

    edge_before(side)
    for f, v in enumerate(edge_side(side)):
        done[f] = v
    edge_before(1 - side)

    for a, dx in enumerate((-1, 1)):
        x_wait(sent.at[a], has(dx, 0))
    for there, c, _ in y_sends[-1] + y_sends[1] + north_sends:

        @pl.when(there)
        def _(c=c):
            c.wait_send()

    @pl.when(both(at_lower, last_column))
    def _():
        first_hop.wait_send()

    @pl.when(both(at_lower, beside_last))
    def _():
        last_hop.wait_send()

    @pl.when(both(at_lower, seam_west))
    def _():
        first_seam_hop.wait_send()

    @pl.when(both(at_lower, seam_east))
    def _():
        last_seam_hop.wait_send()

    @pl.when(at_upper)
    def _():
        wait_recv(y_sends[1])

    @pl.when(jnp.logical_not(at_upper))
    def _():
        wait_recv(y_sends[-1])

    lane_r = iota(1, (ROWS, LANES))
    ahead = ((((lane_r & 15) + 12) & 15) < 8).astype(I32)
    fresh = ahead == side
    for f, v in enumerate(edge_side(1 - side)):
        v = jnp.where(fresh, v, done[f])
        for l in range(LEVELS):
            m = roll(v, -16 * l - 4)
            nat[0, f, l] = jnp.where(lane_r < 8, m, nat[0, f, l])
            nat[2, f, l] = jnp.where(lane_r >= 120, m, nat[2, f, l])


def write_kernel(ready, out, sem):
    for j in range(3):
        for f in range(3):
            for l in range(LEVELS):
                cut = slice(LANES * j, LANES * j + LANES)
                pltpu.make_async_copy(ready.at[j, f, l], out.at[f, l, :, cut], sem).start()
    pltpu.make_async_copy(ready, ready, sem).wait()


def body(
    sizes,
    fields,
    east_band,
    north_band,
    east_index,
    north_index,
    east_weight,
    north_weight,
    nest_moves,
    courant,
    diffuse,
):
    vmem = pltpu.VMEM
    dma = pltpu.SemaphoreType.DMA
    ready = pl.pallas_call(
        functools.partial(exchange_kernel, sizes),
        out_shape=vmem((3, 3, LEVELS, ROWS, LANES), F32),
        in_specs=[pl.BlockSpec(memory_space=pl.ANY)] * 10,
        out_specs=pl.BlockSpec(memory_space=pltpu.VMEM),
        scratch_shapes=[
            vmem((3, 3, SPAN) + TILE, F32),
            vmem((3, SPAN, LEVELS, WIDE), F32),
            vmem((2, 3, SPAN, LANES), F32),
            vmem((2, 3) + TILE, F32),
            vmem((2, 3) + TILE, F32),
            vmem((2, 2) + TILE, F32),
            vmem((2,) + TILE, F32),
            vmem((2, 2) + TILE, F32),
            vmem((2,) + TILE, F32),
            vmem((2, 2) + TILE, F32),
            vmem((3, 3, LEVELS, WIDE), F32),
            vmem((3, 8) + TILE, F32),
            vmem((3, 5) + TILE, F32),
            vmem((2, 3) + TILE, F32),
            vmem((3, SPAN) + TILE, F32),
            vmem((3, SPAN, LANES), F32),
            vmem((2,) + TILE, F32),
            vmem((3, 5, SPAN, LANES), F32),
            vmem((2, 3, 5, SPAN, LANES), F32),
            vmem((2, 2) + TILE, F32),
            vmem((3, ROWS, LANES), F32),
            vmem((96, LANES), F32),
            vmem((2, WIDE), I32),
            vmem((2, WIDE), F32),
            vmem((96, 8), F32),
            vmem((96, LANES), F32),
            vmem((2, ROWS), I32),
            vmem((2, ROWS), F32),
            vmem(TILE, F32),
            pltpu.SMEM((2, 2), I32),
            pltpu.SMEM((LEVELS,), F32),
            pltpu.SMEM((LEVELS,), F32),
            dma((10,)),
            dma((10,)),
            pltpu.SemaphoreType.REGULAR,
        ],
        compiler_params=pltpu.CompilerParams(
            collective_id=0, has_side_effects=True, vmem_limit_bytes=VMEM_A
        ),
    )(
        fields,
        east_band.reshape(96, LANES),
        north_band.reshape(96, 8),
        east_index,
        north_index,
        east_weight,
        north_weight,
        nest_moves,
        courant,
        diffuse,
    )
    return pl.pallas_call(
        write_kernel,
        out_shape=jax.ShapeDtypeStruct(fields.shape, F32),
        in_specs=[pl.BlockSpec(memory_space=pltpu.VMEM)],
        out_specs=pl.BlockSpec(memory_space=pl.ANY),
        scratch_shapes=[dma],
        compiler_params=pltpu.CompilerParams(vmem_limit_bytes=VMEM_B),
    )(ready)


VMEM_A = 56 * 1024 * 1024
VMEM_B = 8 * 1024 * 1024


def solution(mesh):
    sizes = (mesh.shape["gx"], mesh.shape["gy"])
    return jax.shard_map(
        functools.partial(body, sizes),
        mesh=mesh,
        in_specs=(
            P(None, None, "gx", "gy"),
            P(None, None, None, None, "gy"),
            P(None, None, None, None, "gx"),
            P(None, "gy"),
            P(None, "gx"),
            P(None, "gy"),
            P(None, "gx"),
            P(),
            P(),
            P(),
        ),
        out_specs=P(None, None, "gx", "gy"),
        check_vma=False,
    )
```

```python
import functools

import jax
import jax.numpy as jnp
from jax import lax
from jax.experimental import pallas as pl
from jax.experimental.pallas import tpu as pltpu
from jax.sharding import PartitionSpec as P

MESH = pl.DeviceIdType.MESH
F32 = jnp.float32
I32 = jnp.int32
HALO = 4
ROWS = 24
SPAN = ROWS + 2 * HALO
WIDE = 384
LANES = 128
LEVELS = 8
X_ROWS = (4, 3, 2)
RUN = 8
TILE = (LEVELS, LANES)


def third(v):
    return (((v + 48) * 43691) >> 17) - 16


def roll(v, by):
    by = by % v.shape[1]
    return pltpu.roll(v, by, 1) if by else v


def roll_rows(v, by):
    return pltpu.roll(v, by % v.shape[0], 0)


def iota(axis=1, shape=TILE):
    return lax.broadcasted_iota(I32, shape, axis)


def take(v, at):
    return jnp.take_along_axis(v, at & (LANES - 1), axis=1)


def pick_shift(v, by, step):
    return jnp.where(by > 0, roll(v, step), jnp.where(by < 0, roll(v, -step), v))


def slots():
    lane = iota()
    return jnp.where((lane & 7) < 4, ((lane + 64) & 127) >> 3, ((lane + 4) & 127) >> 3)


def advance(load, store, lo, count, kk, kk_row, visc):
    def first(r, p_below, p_here, p_above):
        k = kk_row(r)
        u = load(1, r) - k * (p_above - p_below)
        v = load(2, r) - k * (roll(p_here, -1) - roll(p_here, 1))
        return u, v

    p = [load(0, lo - 2 + i) for i in range(4)]
    ub, vb = first(lo - 1, p[0], p[1], p[2])
    u0, v0 = first(lo, p[1], p[2], p[3])
    p0, p1 = p[2], p[3]
    for step in range(count):
        r = lo + step
        p2 = load(0, r + 2)
        ua, va = first(r + 1, p0, p1, p2)
        un, us, vn, vs = roll(u0, -1), roll(u0, 1), roll(v0, -1), roll(v0, 1)
        store(0, r, p0 - kk * ((ua - ub) + (vn - vs)))
        store(1, r, u0 + visc * (((ua + ub) + (un + us)) - 4.0 * u0))
        store(2, r, v0 + visc * (((va + vb) + (vn + vs)) - 4.0 * v0))
        p0, p1, ub, u0, vb, v0 = p1, p2, u0, ua, v0, va


def edge_substep(p, u, v, k_in, kk, visc, keep):
    def across(w):
        return roll_rows(w, -1), roll_rows(w, 1)

    def first(i, rows):
        east, west = across(p[i])
        u1 = u[i][0:rows] - k_in[i][0:rows] * (east - west)[0:rows]
        v1 = v[i][0:rows] - k_in[i][0:rows] * (p[i + 1][0:rows] - p[i - 1][0:rows])
        return u1, v1

    u0, v0 = first(0, SPAN)
    un, vn = first(1, keep)
    us, vs = first(-1, keep)
    (ue, uw), (ve, vw) = ([w[0:keep] for w in across(x)] for x in (u0, v0))
    u0, v0, kk, visc = u0[0:keep], v0[0:keep], kk[0:keep], visc[0:keep]
    return (
        p[0][0:keep] - kk * ((ue - uw) + (vn - vs)),
        u0 + visc * (((ue + uw) + (un + us)) - 4.0 * u0),
        v0 + visc * (((ve + vw) + (vn + vs)) - 4.0 * v0),
    )


def exchange_kernel(
    sizes,
    fields,
    east_band,
    north_band,
    east_index,
    north_index,
    east_weight,
    north_weight,
    moves,
    courant,
    diffuse,
    nat,
    ext,
    mid,
    g,
    to_y,
    from_y,
    from_d,
    east_out,
    east_in,
    north_out,
    north_in,
    strip,
    stage,
    sg,
    ns,
    ns_stage,
    nso,
    hop,
    pre,
    mask,
    factor,
    done,
    eb,
    ei,
    ew,
    nb,
    nbw,
    ni,
    nw,
    ntab,
    mv,
    ks,
    qs,
    sent,
    received,
    ready,
):
    nx, ny = sizes
    gx = lax.axis_index("gx")
    gy = lax.axis_index("gy")
    total_x = nx * ROWS
    total_y = ny * WIDE
    upper_mid = ny // 2
    lower_mid = upper_mid - 1
    west, east = gx == 0, gx == nx - 1
    south, north = gy == 0, gy == ny - 1
    x_edge = jnp.logical_or(west, east)
    y_edge = jnp.logical_or(south, north)
    has_x = {-1: gx > 0, 1: gx < nx - 1}
    has_y = {-1: gy > 0, 1: gy < ny - 1}
    at_lower = gy == lower_mid
    at_upper = gy == upper_mid
    at_mid = jnp.logical_or(at_lower, at_upper)
    under_lower = gy == lower_mid - 1
    above_upper = gy == upper_mid + 1
    at_next = jnp.logical_or(under_lower, above_upper)

    def both(a, b):
        return jnp.logical_and(a, b)

    def has(dx, dy):
        if dx and dy:
            return both(has_x[dx], has_y[dy])
        return has_x[dx] if dx else has_y[dy]

    def over(dy):
        return at_lower if dy > 0 else at_upper

    odd = lax.rem(gx, 2) == 1
    even = jnp.logical_not(odd)

    seam_west = both(lax.rem(gx, RUN) == 0, gx > 0)
    seam_east = both(lax.rem(gx, RUN) == RUN - 1, gx < nx - 1)

    last_column = lax.rem(gx, RUN) == RUN - 1
    beside_last = lax.rem(gx, RUN) == RUN - 2

    barrier = pltpu.get_barrier_semaphore()

    def greet(dx, dy, there):
        @pl.when(both(has(dx, dy), there))
        def _():
            pl.semaphore_signal(barrier, inc=1, device_id=(gx + dx, gy + dy), device_id_type=MESH)

    for dy in (1, -1):
        for dx in (-1, 1, 0):
            there = over(dy)
            if dx > 0 and dy < 0:
                there = both(there, jnp.logical_not(jnp.logical_or(seam_east, beside_last)))
            greet(dx, dy, there)
    for dy in (1, -1):
        ahead = (gy + dy == lower_mid - 1) if dy > 0 else (gy + dy == upper_mid + 1)
        to_mid = (under_lower if dy > 0 else above_upper) | ahead
        for dx in (-1, 1, 0):
            greet(dx, dy, jnp.logical_not(jnp.logical_or(over(dy), to_mid)))
    for dx in (-1, 1):
        greet(dx, 0, jnp.logical_not(at_mid))

    loads = [
        pltpu.make_async_copy(
            fields.at[f, l, :, LANES * j : LANES * j + LANES], ext.at[j, f, 0:ROWS, l, :], sent.at[j & 1]
        )
        for j in (0, 2, 1)
        for f in range(3)
        for l in range(LEVELS)
    ]
    smalls = [
        pltpu.make_async_copy(s, d, sent.at[2 + k])
        for k, (s, d) in enumerate(
            ((moves, mv), (courant, ks), (diffuse, qs), (east_band, eb), (east_index, ei), (east_weight, ew))
        )
    ]
    norths = [
        pltpu.make_async_copy(s, d, sent.at[2 + k])
        for k, (s, d) in enumerate(((north_band, nb), (north_index, ni), (north_weight, nw)))
    ]
    for c in loads + smalls:
        c.start()

    def wait_bytes(block, sem):
        pltpu.make_async_copy(block, block, sem).wait()

    wait_bytes(ext.at[0:2, :, 0:ROWS], sent.at[0])

    lane = iota()
    part = lane & 15
    ext_rows = ext.reshape(9 * SPAN * LEVELS, LANES)

    def edge_windows(t):
        for f in range(3):
            low, high = None, None
            for l in range(LEVELS):
                at = (f * SPAN + 8 * t) * LEVELS + l
                head = ext_rows[pl.ds(at, 8, stride=LEVELS), :]
                tail = ext_rows[pl.ds(at + 6 * SPAN * LEVELS, 8, stride=LEVELS), :]
                v = roll(jnp.where(lane < 64, head, tail), 16 * l + 4)
                low = v if low is None else jnp.where((lane >> 4) == l, v, low)
                high = v if high is None else jnp.where((((lane + 8) >> 4) & 7) == l, v, high)
            g[0, f, 8 * t : 8 * t + 8] = low
            g[1, f, 8 * t : 8 * t + 8] = high

    for t in range(3):
        edge_windows(t)
        for d in range(2):
            v = g[d, 0, 8 * t : 8 * t + 8]
            for f in range(1, 3):
                v = jnp.where((part >> 2) == f + 1 - d, roll(g[d, f, 8 * t : 8 * t + 8], 4 * f), v)
            to_y[d, t] = v
    for c in smalls:
        c.wait()

    shift_x = mv[0, 0]
    shift_y = mv[0, 1]
    side_x = jnp.where(west, 0, 1)
    side_y = jnp.where(south, 0, 1)
    out_x = shift_x == 2 * side_x - 1
    out_y = shift_y == 2 * side_y - 1
    by_y = jnp.where(out_x, shift_y, 0)
    by_x = jnp.where(out_y, shift_x, 0)

    def east_rows():
        cell = iota(1, (1, WIDE))
        index = jnp.where(side_x == 0, ei[0:1, :], ei[1:2, :])
        upper = (index - (gy * LANES + third(cell)) + 1).astype(F32)
        weight = jnp.where(side_x == 0, ew[0:1, :], ew[1:2, :])
        wide = (LEVELS, WIDE)
        return jnp.broadcast_to(upper, wide), jnp.broadcast_to(weight, wide)

    def east_parents(b, f):
        return eb[pl.ds(side_x * 48 + f * 16 + b, LEVELS, stride=2), :]

    def north_parents(b, f):
        return nbw[pl.ds(side_y * 48 + f * 16 + b, LEVELS, stride=2), :]

    @pl.when(x_edge)
    def _():
        acc = jnp.zeros(TILE, F32)
        for b in range(2):
            for f in range(3):
                k = 3 * b + f
                near = (((lane - 8 * k + 4) & 127) >> 3) == 0
                acc = jnp.where(near, roll(east_parents(b, f), 8 * k), acc)
        east_out[0] = acc
        rows = [jnp.where(lane < 64, v[:, 0:LANES], v[:, 2 * LANES : WIDE]) for v in east_rows()]
        east_out[1] = jnp.where(iota(0) == 0, rows[0], rows[1])

    @pl.when(y_edge)
    def _():
        for c in norths:
            c.start()
        for c in norths:
            c.wait()
        nbw[...] = jnp.zeros((96, LANES), F32)
        nbw[:, 0:8] = nb[...]
        cell = iota(1, (2, ROWS))
        ntab[...] = jnp.zeros(TILE, F32)
        ntab[0:2, 0:ROWS] = (ni[...] - (gx * 8 + third(cell)) + 1).astype(F32)
        ntab[2:4, 0:ROWS] = nw[...]
        acc = jnp.zeros(TILE, F32)
        for b in range(2):
            for f in range(3):
                k = 3 * b + f
                acc = jnp.where((lane >> 3) == k, roll(north_parents(b, f), 8 * k), acc)
        north_out[0] = acc
        north_out[1] = ntab[...]

    def to(dx, dy, src, dst, send, recv):
        return pltpu.make_async_remote_copy(
            src_ref=src,
            dst_ref=dst,
            send_sem=send,
            recv_sem=recv,
            device_id=(gx + dx, gy + dy),
            device_id_type=MESH,
        )

    y_sends = {}
    for s, dy in enumerate((-1, 1)):
        group = []
        for a, dx in enumerate((-1, 1)):
            c = to(
                dx,
                dy,
                to_y.at[s, 2 * a],
                from_d.at[1 - a, 1 - s],
                sent.at[4 + 2 * a + s],
                received.at[4 + 2 * (1 - a) + 1 - s],
            )
            there = has(dx, dy)
            if dx < 0 and dy > 0:
                there = both(there, jnp.logical_not(both(at_lower, jnp.logical_or(seam_west, last_column))))
            group.append((there, c, has(-dx, -dy)))
        c = to(0, dy, to_y.at[s], from_y.at[1 - s], sent.at[2 + s], received.at[2 + 1 - s])
        group.append((has(0, dy), c, has(0, -dy)))
        send, recv = sent.at[4 + 2 * side_x + s], received.at[4 + 2 * side_x + 1 - s]
        c = to(0, dy, east_out, east_in.at[1 - s], send, recv)
        group.append((both(x_edge, has(0, dy)), c, both(x_edge, has(0, -dy))))
        y_sends[dy] = group
    x_sends = []
    north_sends = []
    for a, dx in enumerate((-1, 1)):
        for f in range(3):
            n = X_ROWS[f]
            if dx < 0:
                src, dst = ext.at[:, f, 0:n], ext.at[:, f, ROWS : ROWS + n]
            else:
                src, dst = ext.at[:, f, ROWS - n : ROWS], ext.at[:, f, SPAN - n : SPAN]
            x_sends.append((has(dx, 0), to(dx, 0, src, dst, sent.at[a], received.at[1 - a]), None))
        send, recv = sent.at[4 + 2 * a + side_y], received.at[4 + 2 * (1 - a) + side_y]
        c = to(dx, 0, north_out, north_in.at[1 - a], send, recv)
        north_sends.append((both(y_edge, has(dx, 0)), c, both(y_edge, has(-dx, 0))))

    side = jnp.where(at_upper, 1, 0)
    east_one = odd.astype(I32)
    mate = 1 - 2 * east_one
    first_hop = to(mate, 0, to_y.at[1, 2 * (1 - east_one)], hop.at[0], sent.at[8], received.at[8])
    last_hop = to(
        0, 1, hop.at[0], from_d.at[1 - east_one, 0], sent.at[8], received.at[4 + 2 * (1 - east_one)]
    )
    first_seam_hop = to(-1, 0, to_y.at[1, 0], hop.at[0], sent.at[5], received.at[8])
    last_seam_hop = to(0, 1, hop.at[0], from_d.at[1, 0], sent.at[5], received.at[6])

    def start(group, extra=None):
        for there, c, _ in group:

            @pl.when(there if extra is None else both(there, extra))
            def _(c=c):
                c.start()

    def wait_recv(group):
        for _, c, there in group:

            @pl.when(there)
            def _(c=c):
                c.wait_recv()

    count_x = 1 + has_x[-1].astype(I32) + has_x[1].astype(I32)
    count_y = 1 + has_y[-1].astype(I32) + has_y[1].astype(I32)

    wait_bytes(ext.at[1, :, 0:ROWS], sent.at[1])

    @pl.when(at_upper)
    def _():
        pl.semaphore_wait(barrier, count_x)
        start(y_sends[-1])
        pl.semaphore_wait(ready, 1)
        start(x_sends)
        start(y_sends[1])

    @pl.when(jnp.logical_not(at_mid))
    def _():
        pl.semaphore_wait(barrier, jnp.where(at_next, 2 * count_x, count_x * count_y) - 1)

        @pl.when(jnp.logical_or(under_lower, gy == lower_mid - 2))
        def _():
            pl.semaphore_signal(ready, inc=1, device_id=(gx, gy + 1), device_id_type=MESH)

        @pl.when(jnp.logical_or(above_upper, gy == upper_mid + 2))
        def _():
            pl.semaphore_signal(ready, inc=1, device_id=(gx, gy - 1), device_id_type=MESH)

        start(y_sends[-1], jnp.logical_not(under_lower))
        start(y_sends[1], jnp.logical_not(above_upper))
        start(north_sends)
        start(x_sends)

    def spread(values, level, scale):
        v = jnp.zeros(TILE, F32)
        for l in range(LEVELS):
            v = jnp.where(level == l, scale * values[l], v)
        return v

    level = iota(0)
    half = spread(ks, level, 0.5)
    visc = spread(qs, level, 1.0)
    half_w = jnp.concatenate([half] * 3, axis=1)
    visc_w = jnp.concatenate([visc] * 3, axis=1)
    nat_rows = nat.reshape(9 * ROWS * LEVELS, LANES)

    def in_first(r):
        x = gx * ROWS + r
        return jnp.where(both(x >= 3 * shift_x, x < total_x + 3 * shift_x), 1.0, 0.0).astype(F32)

    def in_second(r):
        x = gx * ROWS + r
        return jnp.where(both(x >= 0, x < total_x), 1.0, 0.0).astype(F32)

    def load_ext(f, r):
        return jnp.concatenate([ext[j, f, r & (SPAN - 1)] for j in range(3)], axis=1)

    def load_mid(f, r):
        return mid[f, r & (SPAN - 1)]

    def store_mid(f, r, v):
        mid[f, r & (SPAN - 1)] = v

    def store_nat(f, r, v):
        for j in range(3):
            at = (3 * j + f) * LEVELS * ROWS + r
            nat_rows[pl.ds(at, LEVELS, stride=ROWS), :] = v[:, LANES * j : LANES * j + LANES]

    def substep_1(lo, count, kk_row):
        advance(load_ext, store_mid, lo, count, half_w, kk_row, visc_w)

    def substep_2(lo, count, kk_row):
        advance(load_mid, store_nat, lo, count, half_w, kk_row, visc_w)

    def everywhere(r):
        return half_w

    substep_1(5, 14, everywhere)
    substep_2(7, 10, everywhere)

    @pl.when(at_next)
    def _():
        pl.semaphore_wait(ready, 1)
        start(y_sends[-1], under_lower)
        start(y_sends[1], above_upper)

    @pl.when(at_lower)
    def _():
        pl.semaphore_wait(ready, 1)

        @pl.when(last_column)
        def _():
            first_hop.start()

        @pl.when(seam_west)
        def _():
            first_seam_hop.start()

        start(x_sends)
        start(y_sends[-1])

    @pl.when(at_lower)
    def _():
        pl.semaphore_wait(barrier, count_x - jnp.logical_or(seam_west, last_column).astype(I32))
        start(y_sends[1])

        @pl.when(beside_last)
        def _():
            first_hop.wait_recv()
            last_hop.start()

        @pl.when(seam_east)
        def _():
            first_seam_hop.wait_recv()
            last_seam_hop.start()

    def blend(parents, base, upper, weight, by):
        c0 = (1.0 - upper) * (1.0 - weight)
        c1 = (1.0 - upper) * weight + upper * (1.0 - weight)
        c2 = upper * weight
        values = []
        for v in parents:
            v = pick_shift(v, by, 1)
            values.append(c0 * take(v, base - 1) + c1 * take(v, base) + c2 * take(v, base + 1))
        return values

    def outward(c):
        return jnp.where(side_x > 0, (2.0 * c + 1.0) / 6.0, (5.0 - 2.0 * c) / 6.0).astype(F32)

    @pl.when(x_edge)
    def _():
        upper, weight = east_rows()
        upper = pick_shift(upper, by_y, 3)
        weight = pick_shift(weight, by_y, 3)
        for j in range(3):
            cut = slice(LANES * j, LANES * j + LANES)
            base = third(lane + LANES * j)
            for f in range(3):
                inner, outer = blend([east_parents(b, f) for b in range(2)], base, upper[:, cut], weight[:, cut], by_y)
                for c in range(3):
                    a = outward(c)
                    strip[c, f, :, cut] = inner * (1.0 - a) + outer * a

    tall = (SPAN, LANES)
    row = iota(0, tall)
    row = jnp.where(row < SPAN - HALO, row, row - SPAN) + gx * ROWS
    part_t = iota(1, tall) & 15
    in_x1 = (row >= 3 * shift_x) & (row < total_x + 3 * shift_x)
    in_x2 = (row >= 0) & (row < total_x)
    for s, (window, origin) in enumerate((((lane >> 4), -HALO), (((lane + 8) >> 4) & 7, WIDE - 12))):
        factor[s, 0] = spread(ks, window, 0.5)
        factor[s, 1] = spread(qs, window, 1.0)
        y = (part_t if origin < 0 else ((part_t + 8) & 15)) + (origin + gy * WIDE)
        for i in range(-2, 3):
            z = y + i
            in_y = (z >= 0) & (z < total_y)
            mask[s, 0, i + 2] = jnp.where(in_x1 & (z >= 3 * shift_y) & (z < total_y + 3 * shift_y), 1.0, 0.0)
            mask[s, 1, i + 2] = jnp.where(in_x2 & in_y, 1.0, 0.0)
            mask[s, 2, i + 2] = jnp.where(in_y, 1.0, 0.0)

    sides_x = ((west, 29, 0, 28, (30, 31)), (east, 24, 21, 27, (24, 25)))
    for there, beyond, own, zero, _ in sides_x:

        @pl.when(there)
        def _(beyond=beyond, own=own, zero=zero):
            for f in range(3):
                for j in range(3):
                    cut = slice(LANES * j, LANES * j + LANES)
                    ext[j, f, zero] = jnp.zeros(TILE, F32)
                    for c in range(3):
                        ext[j, f, beyond + c] = jnp.where(out_x, strip[c, f, :, cut], 0.0)
                        ext[j, f, own + c] = jnp.where(out_x, ext[j, f, own + c], 0.0)

    def first_rows(r):
        return half_w * in_first(r)

    def second_rows(r):
        return half_w * in_second(r)

    def x_wait(sem, there):
        @pl.when(there)
        def _():
            wait_bytes(ext.at[:, 0, 0 : sum(X_ROWS)], sem)

    for turn in range(2):
        westward = odd if turn == 0 else even

        @pl.when(westward)
        def _():
            x_wait(received.at[0], has(-1, 0))

        @pl.when(jnp.logical_not(westward))
        def _():
            x_wait(received.at[1], has(1, 0))

        if turn == 1:
            edge_windows(3)
        substep_1(jnp.where(westward, -2, 19), 7, first_rows)
        for there, _, own, _, outside in sides_x:

            @pl.when(there)
            def _(own=own, outside=outside):
                for f in range(3):
                    for r in outside:
                        mid[f, r] = jnp.zeros((LEVELS, WIDE), F32)
                    for c in range(3):
                        mid[f, own + c] = jnp.where(out_x, mid[f, own + c], strip[c, f])

        substep_2(jnp.where(westward, 0, 17), 7, second_rows)

    @pl.when(y_edge)
    def _():
        wait_recv(north_sends)
        lower_band = jnp.where(has_x[-1], north_in[0, 0], 0.0)
        upper_band = jnp.where(has_x[1], north_in[1, 0], 0.0)
        lower_tab = jnp.where(has_x[-1], north_in[0, 1], 0.0)
        upper_tab = jnp.where(has_x[1], north_in[1, 1], 0.0)
        tab = jnp.where(
            lane >= 112,
            roll(lower_tab, 128 - ROWS),
            jnp.where((lane >= ROWS) & (lane < 2 * ROWS), roll(upper_tab, ROWS), ntab[...]),
        )
        tab = pick_shift(tab, by_x, 3)
        parents = []
        for b in range(2):
            for f in range(3):
                k = 3 * b + f
                v = jnp.where((lane >= 8) & (lane < 16), roll(upper_band, 8 - 8 * k), north_parents(b, f))
                parents.append(jnp.where(lane >= 120, roll(lower_band, -8 - 8 * k), v))
        place = lane & 7
        slot = slots()
        step = jnp.where(place < 4, place, place - 5).astype(F32)
        a = jnp.where(place < 4, (2.0 * step + 1.0) / 6.0, (5.0 - 2.0 * step) / 6.0)
        real = (place != 3) & (place != 4)
        for h in range(2):
            x = slot + (16 * h - HALO)
            base = third(x)
            tab_x = take(tab, x)
            upper = jnp.broadcast_to(jnp.where(side_y == 0, tab_x[0:1], tab_x[1:2]), TILE)
            weight = jnp.broadcast_to(jnp.where(side_y == 0, tab_x[2:3], tab_x[3:4]), TILE)
            whole = x + gx * ROWS - 3 * by_x
            fits = real & (whole >= 0) & (whole < total_x)
            values = blend(parents, base, upper, weight, by_x)
            for f in range(3):
                v = jnp.where(fits, values[f] * (1.0 - a) + values[3 + f] * a, 0.0)
                ns[h, f] = jnp.where(north, roll(v, -60), roll(v, -124))
        for r in range(SPAN):
            h, i = divmod(r, 16)
            for f in range(3):
                ns_stage[f, (r - HALO) % SPAN] = roll(ns[h, f], -8 * i)
        staged = ns_stage.reshape(3 * SPAN * LEVELS, LANES)
        late = jnp.where(north, 1, 0)
        for t in range(4):
            v = jnp.zeros(TILE, F32)
            for f in range(3):
                for l in range(LEVELS):
                    rows = staged[pl.ds((f * SPAN + 8 * t) * LEVELS + l, 8, stride=LEVELS), :]
                    v = jnp.where((lane >> 2) == 4 * l + f + late, roll(rows, 16 * l + 4 * f), v)
            for there, s in ((south, 0), (north, 1)):

                @pl.when(there)
                def _(s=s, t=t, v=v):
                    if t < 3:
                        from_y[s, t] = v
                    else:
                        from_d[0, s] = v
                        from_d[1, s] = v

            for f in range(3):
                nso[f, 8 * t : 8 * t + 8] = jnp.where(north, roll(v, -4 * f - 3), roll(v, -4 * f + 3))

    def east_edge_strip(s):
        band = jnp.where(jnp.where(s == 0, has_y[-1], has_y[1]), east_in[s, 0], 0.0)
        far_tab = jnp.where(jnp.where(s == 0, has_y[-1], has_y[1]), east_in[s, 1], 0.0)
        beyond = ((lane + 64 * s) & 127) >= 64
        near = []
        for k, v in enumerate(east_rows()):
            v = jnp.where(s == 0, v[:, 0:LANES], v[:, 2 * LANES : WIDE])
            v = jnp.where(beyond, jnp.broadcast_to(far_tab[k : k + 1], TILE), v)
            near.append(pick_shift(v, by_y, 3))
        base = third(jnp.where(lane < 64, lane, lane - LANES) + WIDE * s)
        for f in range(3):
            parents = []
            for b in range(2):
                k = 3 * b + f
                parents.append(jnp.where(beyond, roll(band, -8 * k), east_parents(b, f)))
            inner, outer = blend(parents, base, near[0], near[1], by_y)
            for c in range(3):
                a = outward(c)
                v = inner * (1.0 - a) + outer * a
                stage[f, c] = v
                stage[f, 5 + c] = v
            for c in (3, 4):
                stage[f, c] = jnp.zeros(TILE, F32)
        staged = stage.reshape(3 * 8 * LEVELS, LANES)
        window = ((lane + 8 * s) >> 4) & 7
        for f in range(3):
            acc = None
            for l in range(LEVELS):
                v = roll(staged[pl.ds(f * 8 * LEVELS + l, 8, stride=LEVELS), :], 16 * l + 4)
                acc = v if acc is None else jnp.where(window == l, v, acc)
            for i in range(-2, 3):
                sg[f, i + 2] = roll(acc, -i)

    sub = iota(0)
    beyond_rows = (jnp.where(west, 1, 0) * (sub >= 4).astype(I32) + jnp.where(east, 1, 0) * (sub < 4).astype(I32)) > 0
    own_low = both(west, jnp.logical_not(out_x))
    own_high = both(east, jnp.logical_not(out_x))

    reach = (2, 1, 1)

    def edge_before(s):
        for f in range(3):
            for i in range(-reach[f], reach[f] + 1):
                pre[f, i + 2] = roll(g[s, f], -i)

    def edge_side(s):
        @pl.when(x_edge)
        def _():
            east_edge_strip(s)

        k = jnp.concatenate([factor[s, 0]] * 4, axis=0)
        q = jnp.concatenate([factor[s, 1]] * 4, axis=0)
        lay_strip = both(jnp.where(s == 0, south, north), jnp.logical_not(out_y))
        head = jnp.where(sub < 4, from_d[1, s], from_d[0, s])
        arrived = jnp.concatenate([from_y[s, 0], from_y[s, 1], from_y[s, 2], head], axis=0)
        own_strip = (((part_t - 4 + 3 * s) & 15) < 3) & lay_strip
        state = []
        for f in range(3):
            ahead = {}
            for i in range(-reach[f], reach[f] + 1):
                v = jnp.where(((part_t + i - 4 * s) & 15) < 4, roll(arrived, -4 * f - i), pre[f, i + 2])
                tip = jnp.where(beyond_rows & (mask[s, 2, i + 2, 0:8] > 0.5), sg[f, i + 2], v[24:32])
                v = jnp.concatenate([v[0:24], tip], axis=0)
                ahead[i] = jnp.where(mask[s, 0, i + 2] > 0.5, v, 0.0)
            state.append(ahead)
        state = edge_substep(*state, {i: k * mask[s, 0, i + 2] for i in (-1, 0, 1)}, k, q, SPAN)
        second = mask[s, 1, 2] > 0.5
        laid = []
        for f in range(3):
            v = state[f]
            low = jnp.where((sub < 3) & own_low, sg[f, 2], v[0:8])
            high = jnp.where((sub >= 5) & own_high, sg[f, 2], v[16:24])
            v = jnp.concatenate([low, v[8:16], high, v[24:32]], axis=0)
            v = jnp.where(own_strip, nso[f], v)
            v = jnp.where(second, v, 0.0)
            near = v if f == 0 else v[0:ROWS]
            ahead = {0: v, 1: roll(near, -1), -1: roll(near, 1)}
            if f == 0:
                ahead[2], ahead[-2] = roll(v[0:ROWS], -2), roll(v[0:ROWS], 2)
            laid.append(ahead)
        return edge_substep(*laid, {i: k * mask[s, 1, i + 2] for i in (-1, 0, 1)}, k, q, ROWS)

    @pl.when(at_upper)
    def _():
        wait_recv(y_sends[-1])

    @pl.when(jnp.logical_not(at_upper))
    def _():
        wait_recv(y_sends[1])

    edge_before(side)
    for f, v in enumerate(edge_side(side)):
        done[f] = v
    edge_before(1 - side)

    for a, dx in enumerate((-1, 1)):
        x_wait(sent.at[a], has(dx, 0))
    for there, c, _ in y_sends[-1] + y_sends[1] + north_sends:

        @pl.when(there)
        def _(c=c):
            c.wait_send()

    @pl.when(both(at_lower, last_column))
    def _():
        first_hop.wait_send()

    @pl.when(both(at_lower, beside_last))
    def _():
        last_hop.wait_send()

    @pl.when(both(at_lower, seam_west))
    def _():
        first_seam_hop.wait_send()

    @pl.when(both(at_lower, seam_east))
    def _():
        last_seam_hop.wait_send()

    @pl.when(at_upper)
    def _():
        wait_recv(y_sends[1])

    @pl.when(jnp.logical_not(at_upper))
    def _():
        wait_recv(y_sends[-1])

    lane_r = iota(1, (ROWS, LANES))
    ahead = ((((lane_r & 15) + 12) & 15) < 8).astype(I32)
    fresh = ahead == side
    for f, v in enumerate(edge_side(1 - side)):
        v = jnp.where(fresh, v, done[f])
        for l in range(LEVELS):
            m = roll(v, -16 * l - 4)
            nat[0, f, l] = jnp.where(lane_r < 8, m, nat[0, f, l])
            nat[2, f, l] = jnp.where(lane_r >= 120, m, nat[2, f, l])


def write_kernel(ready, out, sem):
    for j in range(3):
        for f in range(3):
            for l in range(LEVELS):
                cut = slice(LANES * j, LANES * j + LANES)
                pltpu.make_async_copy(ready.at[j, f, l], out.at[f, l, :, cut], sem).start()
    pltpu.make_async_copy(ready, ready, sem).wait()


def body(
    sizes,
    fields,
    east_band,
    north_band,
    east_index,
    north_index,
    east_weight,
    north_weight,
    nest_moves,
    courant,
    diffuse,
):
    vmem = pltpu.VMEM
    dma = pltpu.SemaphoreType.DMA
    ready = pl.pallas_call(
        functools.partial(exchange_kernel, sizes),
        out_shape=vmem((3, 3, LEVELS, ROWS, LANES), F32),
        in_specs=[pl.BlockSpec(memory_space=pl.ANY)] * 10,
        out_specs=pl.BlockSpec(memory_space=pltpu.VMEM),
        scratch_shapes=[
            vmem((3, 3, SPAN) + TILE, F32),
            vmem((3, SPAN, LEVELS, WIDE), F32),
            vmem((2, 3, SPAN, LANES), F32),
            vmem((2, 3) + TILE, F32),
            vmem((2, 3) + TILE, F32),
            vmem((2, 2) + TILE, F32),
            vmem((2,) + TILE, F32),
            vmem((2, 2) + TILE, F32),
            vmem((2,) + TILE, F32),
            vmem((2, 2) + TILE, F32),
            vmem((3, 3, LEVELS, WIDE), F32),
            vmem((3, 8) + TILE, F32),
            vmem((3, 5) + TILE, F32),
            vmem((2, 3) + TILE, F32),
            vmem((3, SPAN) + TILE, F32),
            vmem((3, SPAN, LANES), F32),
            vmem((1,) + TILE, F32),
            vmem((3, 5, SPAN, LANES), F32),
            vmem((2, 3, 5, SPAN, LANES), F32),
            vmem((2, 2) + TILE, F32),
            vmem((3, ROWS, LANES), F32),
            vmem((96, LANES), F32),
            vmem((2, WIDE), I32),
            vmem((2, WIDE), F32),
            vmem((96, 8), F32),
            vmem((96, LANES), F32),
            vmem((2, ROWS), I32),
            vmem((2, ROWS), F32),
            vmem(TILE, F32),
            pltpu.SMEM((2, 2), I32),
            pltpu.SMEM((LEVELS,), F32),
            pltpu.SMEM((LEVELS,), F32),
            dma((9,)),
            dma((9,)),
            pltpu.SemaphoreType.REGULAR,
        ],
        compiler_params=pltpu.CompilerParams(
            collective_id=0, has_side_effects=True, vmem_limit_bytes=VMEM_A
        ),
    )(
        fields,
        east_band.reshape(96, LANES),
        north_band.reshape(96, 8),
        east_index,
        north_index,
        east_weight,
        north_weight,
        nest_moves,
        courant,
        diffuse,
    )
    return pl.pallas_call(
        write_kernel,
        out_shape=jax.ShapeDtypeStruct(fields.shape, F32),
        in_specs=[pl.BlockSpec(memory_space=pltpu.VMEM)],
        out_specs=pl.BlockSpec(memory_space=pl.ANY),
        scratch_shapes=[dma],
        compiler_params=pltpu.CompilerParams(vmem_limit_bytes=VMEM_B),
    )(ready)


VMEM_A = 56 * 1024 * 1024
VMEM_B = 8 * 1024 * 1024


def solution(mesh):
    sizes = (mesh.shape["gx"], mesh.shape["gy"])
    return jax.shard_map(
        functools.partial(body, sizes),
        mesh=mesh,
        in_specs=(
            P(None, None, "gx", "gy"),
            P(None, None, None, None, "gy"),
            P(None, None, None, None, "gx"),
            P(None, "gy"),
            P(None, "gx"),
            P(None, "gy"),
            P(None, "gx"),
            P(),
            P(),
            P(),
        ),
        out_specs=P(None, None, "gx", "gy"),
        check_vma=False,
    )
```

```python
import functools

import jax
import jax.numpy as jnp
from jax import lax
from jax.experimental import pallas as pl
from jax.experimental.pallas import tpu as pltpu
from jax.sharding import PartitionSpec as P

MESH = pl.DeviceIdType.MESH
F32 = jnp.float32
I32 = jnp.int32
HALO = 4
ROWS = 24
SPAN = ROWS + 2 * HALO
WIDE = 384
LANES = 128
LEVELS = 8
X_ROWS = (4, 3, 2)
RUN = 8
TILE = (LEVELS, LANES)


def third(v):
    return (((v + 48) * 43691) >> 17) - 16


def roll(v, by):
    by = by % v.shape[1]
    return pltpu.roll(v, by, 1) if by else v


def roll_rows(v, by):
    return pltpu.roll(v, by % v.shape[0], 0)


def iota(axis=1, shape=TILE):
    return lax.broadcasted_iota(I32, shape, axis)


def take(v, at):
    return jnp.take_along_axis(v, at & (LANES - 1), axis=1)


def pick_shift(v, by, step):
    return jnp.where(by > 0, roll(v, step), jnp.where(by < 0, roll(v, -step), v))


def slots():
    lane = iota()
    return jnp.where((lane & 7) < 4, ((lane + 64) & 127) >> 3, ((lane + 4) & 127) >> 3)


def advance(load, store, lo, count, kk, kk_row, visc):
    def first(r, p_below, p_here, p_above):
        k = kk_row(r)
        u = load(1, r) - k * (p_above - p_below)
        v = load(2, r) - k * (roll(p_here, -1) - roll(p_here, 1))
        return u, v

    p = [load(0, lo - 2 + i) for i in range(4)]
    ub, vb = first(lo - 1, p[0], p[1], p[2])
    u0, v0 = first(lo, p[1], p[2], p[3])
    p0, p1 = p[2], p[3]
    for step in range(count):
        r = lo + step
        p2 = load(0, r + 2)
        ua, va = first(r + 1, p0, p1, p2)
        un, us, vn, vs = roll(u0, -1), roll(u0, 1), roll(v0, -1), roll(v0, 1)
        store(0, r, p0 - kk * ((ua - ub) + (vn - vs)))
        store(1, r, u0 + visc * (((ua + ub) + (un + us)) - 4.0 * u0))
        store(2, r, v0 + visc * (((va + vb) + (vn + vs)) - 4.0 * v0))
        p0, p1, ub, u0, vb, v0 = p1, p2, u0, ua, v0, va


def edge_substep(p, u, v, k_in, kk, visc, keep):
    def across(w):
        return roll_rows(w, -1), roll_rows(w, 1)

    def first(i, rows):
        east, west = across(p[i])
        u1 = u[i][0:rows] - k_in[i][0:rows] * (east - west)[0:rows]
        v1 = v[i][0:rows] - k_in[i][0:rows] * (p[i + 1][0:rows] - p[i - 1][0:rows])
        return u1, v1

    u0, v0 = first(0, SPAN)
    un, vn = first(1, keep)
    us, vs = first(-1, keep)
    (ue, uw), (ve, vw) = ([w[0:keep] for w in across(x)] for x in (u0, v0))
    u0, v0, kk, visc = u0[0:keep], v0[0:keep], kk[0:keep], visc[0:keep]
    return (
        p[0][0:keep] - kk * ((ue - uw) + (vn - vs)),
        u0 + visc * (((ue + uw) + (un + us)) - 4.0 * u0),
        v0 + visc * (((ve + vw) + (vn + vs)) - 4.0 * v0),
    )


def exchange_kernel(
    sizes,
    fields,
    east_band,
    north_band,
    east_index,
    north_index,
    east_weight,
    north_weight,
    moves,
    courant,
    diffuse,
    nat,
    ext,
    mid,
    g,
    to_y,
    from_y,
    from_d,
    east_out,
    east_in,
    north_out,
    north_in,
    strip,
    stage,
    sg,
    ns,
    ns_stage,
    nso,
    hop,
    pre,
    mask,
    factor,
    done,
    eb,
    ei,
    ew,
    nb,
    nbw,
    ni,
    nw,
    ntab,
    mv,
    ks,
    qs,
    sent,
    received,
    ready,
):
    nx, ny = sizes
    gx = lax.axis_index("gx")
    gy = lax.axis_index("gy")
    total_x = nx * ROWS
    total_y = ny * WIDE
    upper_mid = ny // 2
    lower_mid = upper_mid - 1
    west, east = gx == 0, gx == nx - 1
    south, north = gy == 0, gy == ny - 1
    x_edge = jnp.logical_or(west, east)
    y_edge = jnp.logical_or(south, north)
    has_x = {-1: gx > 0, 1: gx < nx - 1}
    has_y = {-1: gy > 0, 1: gy < ny - 1}
    at_lower = gy == lower_mid
    at_upper = gy == upper_mid
    at_mid = jnp.logical_or(at_lower, at_upper)
    under_lower = gy == lower_mid - 1
    above_upper = gy == upper_mid + 1
    at_next = jnp.logical_or(under_lower, above_upper)

    def both(a, b):
        return jnp.logical_and(a, b)

    def has(dx, dy):
        if dx and dy:
            return both(has_x[dx], has_y[dy])
        return has_x[dx] if dx else has_y[dy]

    def over(dy):
        return at_lower if dy > 0 else at_upper

    odd = lax.rem(gx, 2) == 1
    even = jnp.logical_not(odd)

    seam_west = both(lax.rem(gx, RUN) == 0, gx > 0)
    seam_east = both(lax.rem(gx, RUN) == RUN - 1, gx < nx - 1)

    last_column = lax.rem(gx, RUN) == RUN - 1
    beside_last = lax.rem(gx, RUN) == RUN - 2

    barrier = pltpu.get_barrier_semaphore()

    def greet(dx, dy, there):
        @pl.when(both(has(dx, dy), there))
        def _():
            pl.semaphore_signal(barrier, inc=1, device_id=(gx + dx, gy + dy), device_id_type=MESH)

    for dy in (1, -1):
        for dx in (-1, 1, 0):
            there = over(dy)
            if dx > 0 and dy < 0:
                there = both(there, jnp.logical_not(jnp.logical_or(seam_east, beside_last)))
            greet(dx, dy, there)
    for dy in (1, -1):
        ahead = (gy + dy == lower_mid - 1) if dy > 0 else (gy + dy == upper_mid + 1)
        to_mid = (under_lower if dy > 0 else above_upper) | ahead
        for dx in (-1, 1, 0):
            greet(dx, dy, jnp.logical_not(jnp.logical_or(over(dy), to_mid)))
    for dx in (-1, 1):
        greet(dx, 0, jnp.logical_not(at_mid))

    loads = [
        pltpu.make_async_copy(
            fields.at[f, l, :, LANES * j : LANES * j + LANES], ext.at[j, f, 0:ROWS, l, :], sent.at[j & 1]
        )
        for j in (0, 2, 1)
        for f in range(3)
        for l in range(LEVELS)
    ]
    smalls = [
        pltpu.make_async_copy(s, d, sent.at[2 + k])
        for k, (s, d) in enumerate(
            ((moves, mv), (courant, ks), (diffuse, qs), (east_band, eb), (east_index, ei), (east_weight, ew))
        )
    ]
    norths = [
        pltpu.make_async_copy(s, d, sent.at[2 + k])
        for k, (s, d) in enumerate(((north_band, nb), (north_index, ni), (north_weight, nw)))
    ]
    for c in loads + smalls:
        c.start()

    def wait_bytes(block, sem):
        pltpu.make_async_copy(block, block, sem).wait()

    wait_bytes(ext.at[0:2, :, 0:ROWS], sent.at[0])

    lane = iota()
    part = lane & 15
    ext_rows = ext.reshape(9 * SPAN * LEVELS, LANES)

    def edge_windows(t):
        for f in range(3):
            low, high = None, None
            for l in range(LEVELS):
                at = (f * SPAN + 8 * t) * LEVELS + l
                head = ext_rows[pl.ds(at, 8, stride=LEVELS), :]
                tail = ext_rows[pl.ds(at + 6 * SPAN * LEVELS, 8, stride=LEVELS), :]
                v = roll(jnp.where(lane < 64, head, tail), 16 * l + 4)
                low = v if low is None else jnp.where((lane >> 4) == l, v, low)
                high = v if high is None else jnp.where((((lane + 8) >> 4) & 7) == l, v, high)
            g[0, f, 8 * t : 8 * t + 8] = low
            g[1, f, 8 * t : 8 * t + 8] = high

    for t in range(3):
        edge_windows(t)
        for d in range(2):
            v = g[d, 0, 8 * t : 8 * t + 8]
            for f in range(1, 3):
                v = jnp.where((part >> 2) == f + 1 - d, roll(g[d, f, 8 * t : 8 * t + 8], 4 * f), v)
            to_y[d, t] = v
    for c in smalls:
        c.wait()

    shift_x = mv[0, 0]
    shift_y = mv[0, 1]
    side_x = jnp.where(west, 0, 1)
    side_y = jnp.where(south, 0, 1)
    out_x = shift_x == 2 * side_x - 1
    out_y = shift_y == 2 * side_y - 1
    by_y = jnp.where(out_x, shift_y, 0)
    by_x = jnp.where(out_y, shift_x, 0)

    def east_rows():
        cell = iota(1, (1, WIDE))
        index = jnp.where(side_x == 0, ei[0:1, :], ei[1:2, :])
        upper = (index - (gy * LANES + third(cell)) + 1).astype(F32)
        weight = jnp.where(side_x == 0, ew[0:1, :], ew[1:2, :])
        wide = (LEVELS, WIDE)
        return jnp.broadcast_to(upper, wide), jnp.broadcast_to(weight, wide)

    def east_parents(b, f):
        return eb[pl.ds(side_x * 48 + f * 16 + b, LEVELS, stride=2), :]

    def north_parents(b, f):
        return nbw[pl.ds(side_y * 48 + f * 16 + b, LEVELS, stride=2), :]

    @pl.when(x_edge)
    def _():
        acc = jnp.zeros(TILE, F32)
        for b in range(2):
            for f in range(3):
                k = 3 * b + f
                near = (((lane - 8 * k + 4) & 127) >> 3) == 0
                acc = jnp.where(near, roll(east_parents(b, f), 8 * k), acc)
        east_out[0] = acc
        rows = [jnp.where(lane < 64, v[:, 0:LANES], v[:, 2 * LANES : WIDE]) for v in east_rows()]
        east_out[1] = jnp.where(iota(0) == 0, rows[0], rows[1])

    @pl.when(y_edge)
    def _():
        for c in norths:
            c.start()
        for c in norths:
            c.wait()
        nbw[...] = jnp.zeros((96, LANES), F32)
        nbw[:, 0:8] = nb[...]
        cell = iota(1, (2, ROWS))
        ntab[...] = jnp.zeros(TILE, F32)
        ntab[0:2, 0:ROWS] = (ni[...] - (gx * 8 + third(cell)) + 1).astype(F32)
        ntab[2:4, 0:ROWS] = nw[...]
        acc = jnp.zeros(TILE, F32)
        for b in range(2):
            for f in range(3):
                k = 3 * b + f
                acc = jnp.where((lane >> 3) == k, roll(north_parents(b, f), 8 * k), acc)
        north_out[0] = acc
        north_out[1] = ntab[...]

    def to(dx, dy, src, dst, send, recv):
        return pltpu.make_async_remote_copy(
            src_ref=src,
            dst_ref=dst,
            send_sem=send,
            recv_sem=recv,
            device_id=(gx + dx, gy + dy),
            device_id_type=MESH,
        )

    y_sends = {}
    for s, dy in enumerate((-1, 1)):
        group = []
        for a, dx in enumerate((-1, 1)):
            c = to(
                dx,
                dy,
                to_y.at[s, 2 * a],
                from_d.at[1 - a, 1 - s],
                sent.at[4 + 2 * a + s],
                received.at[4 + 2 * (1 - a) + 1 - s],
            )
            there = has(dx, dy)
            if dx < 0 and dy > 0:
                there = both(there, jnp.logical_not(both(at_lower, jnp.logical_or(seam_west, last_column))))
            group.append((there, c, has(-dx, -dy)))
        c = to(0, dy, to_y.at[s], from_y.at[1 - s], sent.at[2 + s], received.at[2 + 1 - s])
        group.append((has(0, dy), c, has(0, -dy)))
        send, recv = sent.at[4 + 2 * side_x + s], received.at[4 + 2 * side_x + 1 - s]
        c = to(0, dy, east_out, east_in.at[1 - s], send, recv)
        group.append((both(x_edge, has(0, dy)), c, both(x_edge, has(0, -dy))))
        y_sends[dy] = group
    x_sends = []
    north_sends = []
    for a, dx in enumerate((-1, 1)):
        for f in range(3):
            n = X_ROWS[f]
            if dx < 0:
                src, dst = ext.at[:, f, 0:n], ext.at[:, f, ROWS : ROWS + n]
            else:
                src, dst = ext.at[:, f, ROWS - n : ROWS], ext.at[:, f, SPAN - n : SPAN]
            x_sends.append((has(dx, 0), to(dx, 0, src, dst, sent.at[a], received.at[1 - a]), None))
        send, recv = sent.at[4 + 2 * a + side_y], received.at[4 + 2 * (1 - a) + side_y]
        c = to(dx, 0, north_out, north_in.at[1 - a], send, recv)
        north_sends.append((both(y_edge, has(dx, 0)), c, both(y_edge, has(-dx, 0))))

    side = jnp.where(at_upper, 1, 0)
    east_one = odd.astype(I32)
    mate = 1 - 2 * east_one
    first_hop = to(mate, 0, to_y.at[1, 2 * (1 - east_one)], hop.at[0], sent.at[8], received.at[8])
    last_hop = to(
        0, 1, hop.at[0], from_d.at[1 - east_one, 0], sent.at[8], received.at[4 + 2 * (1 - east_one)]
    )
    first_seam_hop = to(-1, 0, to_y.at[1, 0], hop.at[0], sent.at[5], received.at[8])
    last_seam_hop = to(0, 1, hop.at[0], from_d.at[1, 0], sent.at[5], received.at[6])

    def start(group, extra=None):
        for there, c, _ in group:

            @pl.when(there if extra is None else both(there, extra))
            def _(c=c):
                c.start()

    def wait_recv(group):
        for _, c, there in group:

            @pl.when(there)
            def _(c=c):
                c.wait_recv()

    count_x = 1 + has_x[-1].astype(I32) + has_x[1].astype(I32)
    count_y = 1 + has_y[-1].astype(I32) + has_y[1].astype(I32)

    wait_bytes(ext.at[1, :, 0:ROWS], sent.at[1])

    @pl.when(at_upper)
    def _():
        pl.semaphore_wait(barrier, count_x)
        start(y_sends[-1])
        pl.semaphore_wait(ready, 1)
        start(x_sends)
        start(y_sends[1])

    @pl.when(jnp.logical_not(at_mid))
    def _():
        pl.semaphore_wait(barrier, jnp.where(at_next, 2 * count_x, count_x * count_y) - 1)

        @pl.when(jnp.logical_or(under_lower, gy == lower_mid - 2))
        def _():
            pl.semaphore_signal(ready, inc=1, device_id=(gx, gy + 1), device_id_type=MESH)

        @pl.when(jnp.logical_or(above_upper, gy == upper_mid + 2))
        def _():
            pl.semaphore_signal(ready, inc=1, device_id=(gx, gy - 1), device_id_type=MESH)

        start(y_sends[-1], jnp.logical_not(under_lower))
        start(y_sends[1], jnp.logical_not(above_upper))
        start(north_sends)
        start(x_sends)

    def spread(values, level, scale):
        v = jnp.zeros(TILE, F32)
        for l in range(LEVELS):
            v = jnp.where(level == l, scale * values[l], v)
        return v

    level = iota(0)
    half = spread(ks, level, 0.5)
    visc = spread(qs, level, 1.0)
    half_w = jnp.concatenate([half] * 3, axis=1)
    visc_w = jnp.concatenate([visc] * 3, axis=1)
    nat_rows = nat.reshape(9 * ROWS * LEVELS, LANES)

    def in_first(r):
        x = gx * ROWS + r
        return jnp.where(both(x >= 3 * shift_x, x < total_x + 3 * shift_x), 1.0, 0.0).astype(F32)

    def in_second(r):
        x = gx * ROWS + r
        return jnp.where(both(x >= 0, x < total_x), 1.0, 0.0).astype(F32)

    def load_ext(f, r):
        return jnp.concatenate([ext[j, f, r & (SPAN - 1)] for j in range(3)], axis=1)

    def load_mid(f, r):
        return mid[f, r & (SPAN - 1)]

    def store_mid(f, r, v):
        mid[f, r & (SPAN - 1)] = v

    def store_nat(f, r, v):
        for j in range(3):
            at = (3 * j + f) * LEVELS * ROWS + r
            nat_rows[pl.ds(at, LEVELS, stride=ROWS), :] = v[:, LANES * j : LANES * j + LANES]

    def substep_1(lo, count, kk_row):
        advance(load_ext, store_mid, lo, count, half_w, kk_row, visc_w)

    def substep_2(lo, count, kk_row):
        advance(load_mid, store_nat, lo, count, half_w, kk_row, visc_w)

    def everywhere(r):
        return half_w

    substep_1(5, 14, everywhere)
    substep_2(7, 10, everywhere)

    @pl.when(at_next)
    def _():
        pl.semaphore_wait(ready, 1)
        start(y_sends[-1], under_lower)
        start(y_sends[1], above_upper)

    @pl.when(at_lower)
    def _():
        pl.semaphore_wait(ready, 1)

        @pl.when(last_column)
        def _():
            first_hop.start()

        @pl.when(seam_west)
        def _():
            first_seam_hop.start()

        start(x_sends)
        start(y_sends[-1])

    @pl.when(at_lower)
    def _():
        pl.semaphore_wait(barrier, count_x - jnp.logical_or(seam_west, last_column).astype(I32))
        start(y_sends[1])

        @pl.when(beside_last)
        def _():
            first_hop.wait_recv()
            last_hop.start()

        @pl.when(seam_east)
        def _():
            first_seam_hop.wait_recv()
            last_seam_hop.start()

    def blend(parents, base, upper, weight, by):
        c0 = (1.0 - upper) * (1.0 - weight)
        c1 = (1.0 - upper) * weight + upper * (1.0 - weight)
        c2 = upper * weight
        values = []
        for v in parents:
            v = pick_shift(v, by, 1)
            values.append(c0 * take(v, base - 1) + c1 * take(v, base) + c2 * take(v, base + 1))
        return values

    def outward(c):
        return jnp.where(side_x > 0, (2.0 * c + 1.0) / 6.0, (5.0 - 2.0 * c) / 6.0).astype(F32)

    @pl.when(x_edge)
    def _():
        upper, weight = east_rows()
        upper = pick_shift(upper, by_y, 3)
        weight = pick_shift(weight, by_y, 3)
        for j in range(3):
            cut = slice(LANES * j, LANES * j + LANES)
            base = third(lane + LANES * j)
            for f in range(3):
                inner, outer = blend([east_parents(b, f) for b in range(2)], base, upper[:, cut], weight[:, cut], by_y)
                for c in range(3):
                    a = outward(c)
                    strip[c, f, :, cut] = inner * (1.0 - a) + outer * a

    tall = (SPAN, LANES)
    row = iota(0, tall)
    row = jnp.where(row < SPAN - HALO, row, row - SPAN) + gx * ROWS
    part_t = iota(1, tall) & 15
    in_x1 = (row >= 3 * shift_x) & (row < total_x + 3 * shift_x)
    in_x2 = (row >= 0) & (row < total_x)
    for s, (window, origin) in enumerate((((lane >> 4), -HALO), (((lane + 8) >> 4) & 7, WIDE - 12))):
        factor[s, 0] = spread(ks, window, 0.5)
        factor[s, 1] = spread(qs, window, 1.0)
        y = (part_t if origin < 0 else ((part_t + 8) & 15)) + (origin + gy * WIDE)
        for i in range(-2, 3):
            z = y + i
            in_y = (z >= 0) & (z < total_y)
            mask[s, 0, i + 2] = jnp.where(in_x1 & (z >= 3 * shift_y) & (z < total_y + 3 * shift_y), 1.0, 0.0)
            mask[s, 1, i + 2] = jnp.where(in_x2 & in_y, 1.0, 0.0)
            mask[s, 2, i + 2] = jnp.where(in_y, 1.0, 0.0)

    sides_x = ((west, 29, 0, 28, (30, 31)), (east, 24, 21, 27, (24, 25)))
    for there, beyond, own, zero, _ in sides_x:

        @pl.when(there)
        def _(beyond=beyond, own=own, zero=zero):
            for f in range(3):
                for j in range(3):
                    cut = slice(LANES * j, LANES * j + LANES)
                    ext[j, f, zero] = jnp.zeros(TILE, F32)
                    for c in range(3):
                        ext[j, f, beyond + c] = jnp.where(out_x, strip[c, f, :, cut], 0.0)
                        ext[j, f, own + c] = jnp.where(out_x, ext[j, f, own + c], 0.0)

    def first_rows(r):
        return half_w * in_first(r)

    def second_rows(r):
        return half_w * in_second(r)

    def x_wait(sem, there):
        @pl.when(there)
        def _():
            wait_bytes(ext.at[:, 0, 0 : sum(X_ROWS)], sem)

    for turn in range(2):
        westward = odd if turn == 0 else even

        @pl.when(westward)
        def _():
            x_wait(received.at[0], has(-1, 0))

        @pl.when(jnp.logical_not(westward))
        def _():
            x_wait(received.at[1], has(1, 0))

        if turn == 1:
            edge_windows(3)
        substep_1(jnp.where(westward, -2, 19), 7, first_rows)
        for there, _, own, _, outside in sides_x:

            @pl.when(there)
            def _(own=own, outside=outside):
                for f in range(3):
                    for r in outside:
                        mid[f, r] = jnp.zeros((LEVELS, WIDE), F32)
                    for c in range(3):
                        mid[f, own + c] = jnp.where(out_x, mid[f, own + c], strip[c, f])

        substep_2(jnp.where(westward, 0, 17), 7, second_rows)

    @pl.when(y_edge)
    def _():
        wait_recv(north_sends)
        lower_band = jnp.where(has_x[-1], north_in[0, 0], 0.0)
        upper_band = jnp.where(has_x[1], north_in[1, 0], 0.0)
        lower_tab = jnp.where(has_x[-1], north_in[0, 1], 0.0)
        upper_tab = jnp.where(has_x[1], north_in[1, 1], 0.0)
        tab = jnp.where(
            lane >= 112,
            roll(lower_tab, 128 - ROWS),
            jnp.where((lane >= ROWS) & (lane < 2 * ROWS), roll(upper_tab, ROWS), ntab[...]),
        )
        tab = pick_shift(tab, by_x, 3)
        parents = []
        for b in range(2):
            for f in range(3):
                k = 3 * b + f
                v = jnp.where((lane >= 8) & (lane < 16), roll(upper_band, 8 - 8 * k), north_parents(b, f))
                parents.append(jnp.where(lane >= 120, roll(lower_band, -8 - 8 * k), v))
        place = lane & 7
        slot = slots()
        step = jnp.where(place < 4, place, place - 5).astype(F32)
        a = jnp.where(place < 4, (2.0 * step + 1.0) / 6.0, (5.0 - 2.0 * step) / 6.0)
        real = (place != 3) & (place != 4)
        for h in range(2):
            x = slot + (16 * h - HALO)
            base = third(x)
            tab_x = take(tab, x)
            upper = jnp.broadcast_to(jnp.where(side_y == 0, tab_x[0:1], tab_x[1:2]), TILE)
            weight = jnp.broadcast_to(jnp.where(side_y == 0, tab_x[2:3], tab_x[3:4]), TILE)
            whole = x + gx * ROWS - 3 * by_x
            fits = real & (whole >= 0) & (whole < total_x)
            values = blend(parents, base, upper, weight, by_x)
            for f in range(3):
                v = jnp.where(fits, values[f] * (1.0 - a) + values[3 + f] * a, 0.0)
                ns[h, f] = jnp.where(north, roll(v, -60), roll(v, -124))
        for r in range(SPAN):
            h, i = divmod(r, 16)
            for f in range(3):
                ns_stage[f, (r - HALO) % SPAN] = roll(ns[h, f], -8 * i)
        staged = ns_stage.reshape(3 * SPAN * LEVELS, LANES)
        late = jnp.where(north, 1, 0)
        for t in range(4):
            v = jnp.zeros(TILE, F32)
            for f in range(3):
                for l in range(LEVELS):
                    rows = staged[pl.ds((f * SPAN + 8 * t) * LEVELS + l, 8, stride=LEVELS), :]
                    v = jnp.where((lane >> 2) == 4 * l + f + late, roll(rows, 16 * l + 4 * f), v)
            for there, s in ((south, 0), (north, 1)):

                @pl.when(there)
                def _(s=s, t=t, v=v):
                    if t < 3:
                        from_y[s, t] = v
                    else:
                        from_d[0, s] = v
                        from_d[1, s] = v

            for f in range(3):
                nso[f, 8 * t : 8 * t + 8] = jnp.where(north, roll(v, -4 * f - 3), roll(v, -4 * f + 3))

    def east_edge_strip(s):
        band = jnp.where(jnp.where(s == 0, has_y[-1], has_y[1]), east_in[s, 0], 0.0)
        far_tab = jnp.where(jnp.where(s == 0, has_y[-1], has_y[1]), east_in[s, 1], 0.0)
        beyond = ((lane + 64 * s) & 127) >= 64
        near = []
        for k, v in enumerate(east_rows()):
            v = jnp.where(s == 0, v[:, 0:LANES], v[:, 2 * LANES : WIDE])
            v = jnp.where(beyond, jnp.broadcast_to(far_tab[k : k + 1], TILE), v)
            near.append(pick_shift(v, by_y, 3))
        base = third(jnp.where(lane < 64, lane, lane - LANES) + WIDE * s)
        for f in range(3):
            parents = []
            for b in range(2):
                k = 3 * b + f
                parents.append(jnp.where(beyond, roll(band, -8 * k), east_parents(b, f)))
            inner, outer = blend(parents, base, near[0], near[1], by_y)
            for c in range(3):
                a = outward(c)
                v = inner * (1.0 - a) + outer * a
                stage[f, c] = v
                stage[f, 5 + c] = v
            for c in (3, 4):
                stage[f, c] = jnp.zeros(TILE, F32)
        staged = stage.reshape(3 * 8 * LEVELS, LANES)
        window = ((lane + 8 * s) >> 4) & 7
        for f in range(3):
            acc = None
            for l in range(LEVELS):
                v = roll(staged[pl.ds(f * 8 * LEVELS + l, 8, stride=LEVELS), :], 16 * l + 4)
                acc = v if acc is None else jnp.where(window == l, v, acc)
            for i in range(-2, 3):
                sg[f, i + 2] = roll(acc, -i)

    sub = iota(0)
    beyond_rows = (jnp.where(west, 1, 0) * (sub >= 4).astype(I32) + jnp.where(east, 1, 0) * (sub < 4).astype(I32)) > 0
    own_low = both(west, jnp.logical_not(out_x))
    own_high = both(east, jnp.logical_not(out_x))

    reach = (2, 1, 1)

    def edge_before(s):
        for f in range(3):
            for i in range(-reach[f], reach[f] + 1):
                pre[f, i + 2] = roll(g[s, f], -i)

    def edge_side(s):
        @pl.when(x_edge)
        def _():
            east_edge_strip(s)

        k = jnp.concatenate([factor[s, 0]] * 4, axis=0)
        q = jnp.concatenate([factor[s, 1]] * 4, axis=0)
        lay_strip = both(jnp.where(s == 0, south, north), jnp.logical_not(out_y))
        head = jnp.where(sub < 4, from_d[1, s], from_d[0, s])
        arrived = jnp.concatenate([from_y[s, 0], from_y[s, 1], from_y[s, 2], head], axis=0)
        own_strip = (((part_t - 4 + 3 * s) & 15) < 3) & lay_strip
        state = []
        for f in range(3):
            ahead = {}
            for i in range(-reach[f], reach[f] + 1):
                v = jnp.where(((part_t + i - 4 * s) & 15) < 4, roll(arrived, -4 * f - i), pre[f, i + 2])
                tip = jnp.where(beyond_rows & (mask[s, 2, i + 2, 0:8] > 0.5), sg[f, i + 2], v[24:32])
                v = jnp.concatenate([v[0:24], tip], axis=0)
                ahead[i] = jnp.where(mask[s, 0, i + 2] > 0.5, v, 0.0)
            state.append(ahead)
        state = edge_substep(*state, {i: k * mask[s, 0, i + 2] for i in (-1, 0, 1)}, k, q, SPAN)
        second = mask[s, 1, 2] > 0.5
        laid = []
        for f in range(3):
            v = state[f]
            low = jnp.where((sub < 3) & own_low, sg[f, 2], v[0:8])
            high = jnp.where((sub >= 5) & own_high, sg[f, 2], v[16:24])
            v = jnp.concatenate([low, v[8:16], high, v[24:32]], axis=0)
            v = jnp.where(own_strip, nso[f], v)
            v = jnp.where(second, v, 0.0)
            near = v if f == 0 else v[0:ROWS]
            ahead = {0: v, 1: roll(near, -1), -1: roll(near, 1)}
            if f == 0:
                ahead[2], ahead[-2] = roll(v[0:ROWS], -2), roll(v[0:ROWS], 2)
            laid.append(ahead)
        return edge_substep(*laid, {i: k * mask[s, 1, i + 2] for i in (-1, 0, 1)}, k, q, ROWS)

    @pl.when(at_upper)
    def _():
        wait_recv(y_sends[-1])

    @pl.when(jnp.logical_not(at_upper))
    def _():
        wait_recv(y_sends[1])

    edge_before(side)
    for f, v in enumerate(edge_side(side)):
        done[f] = v
    edge_before(1 - side)

    for a, dx in enumerate((-1, 1)):
        x_wait(sent.at[a], has(dx, 0))
    for there, c, _ in y_sends[-1] + y_sends[1] + north_sends:

        @pl.when(there)
        def _(c=c):
            c.wait_send()

    @pl.when(both(at_lower, last_column))
    def _():
        first_hop.wait_send()

    @pl.when(both(at_lower, beside_last))
    def _():
        last_hop.wait_send()

    @pl.when(both(at_lower, seam_west))
    def _():
        first_seam_hop.wait_send()

    @pl.when(both(at_lower, seam_east))
    def _():
        last_seam_hop.wait_send()

    @pl.when(at_upper)
    def _():
        wait_recv(y_sends[1])

    @pl.when(jnp.logical_not(at_upper))
    def _():
        wait_recv(y_sends[-1])

    lane_r = iota(1, (ROWS, LANES))
    ahead = ((((lane_r & 15) + 12) & 15) < 8).astype(I32)
    fresh = ahead == side
    for f, v in enumerate(edge_side(1 - side)):
        v = jnp.where(fresh, v, done[f])
        for l in range(LEVELS):
            m = roll(v, -16 * l - 4)
            nat[0, f, l] = jnp.where(lane_r < 8, m, nat[0, f, l])
            nat[2, f, l] = jnp.where(lane_r >= 120, m, nat[2, f, l])


def write_kernel(ready, out, sem):
    for f in range(3):
        for l in range(LEVELS):
            for j in range(3):
                cut = slice(LANES * j, LANES * j + LANES)
                pltpu.make_async_copy(ready.at[j, f, l], out.at[f, l, :, cut], sem).start()
    pltpu.make_async_copy(ready, ready, sem).wait()


def body(
    sizes,
    fields,
    east_band,
    north_band,
    east_index,
    north_index,
    east_weight,
    north_weight,
    nest_moves,
    courant,
    diffuse,
):
    vmem = pltpu.VMEM
    dma = pltpu.SemaphoreType.DMA
    ready = pl.pallas_call(
        functools.partial(exchange_kernel, sizes),
        out_shape=vmem((3, 3, LEVELS, ROWS, LANES), F32),
        in_specs=[pl.BlockSpec(memory_space=pl.ANY)] * 10,
        out_specs=pl.BlockSpec(memory_space=pltpu.VMEM),
        scratch_shapes=[
            vmem((3, 3, SPAN) + TILE, F32),
            vmem((3, SPAN, LEVELS, WIDE), F32),
            vmem((2, 3, SPAN, LANES), F32),
            vmem((2, 3) + TILE, F32),
            vmem((2, 3) + TILE, F32),
            vmem((2, 2) + TILE, F32),
            vmem((2,) + TILE, F32),
            vmem((2, 2) + TILE, F32),
            vmem((2,) + TILE, F32),
            vmem((2, 2) + TILE, F32),
            vmem((3, 3, LEVELS, WIDE), F32),
            vmem((3, 8) + TILE, F32),
            vmem((3, 5) + TILE, F32),
            vmem((2, 3) + TILE, F32),
            vmem((3, SPAN) + TILE, F32),
            vmem((3, SPAN, LANES), F32),
            vmem((1,) + TILE, F32),
            vmem((3, 5, SPAN, LANES), F32),
            vmem((2, 3, 5, SPAN, LANES), F32),
            vmem((2, 2) + TILE, F32),
            vmem((3, ROWS, LANES), F32),
            vmem((96, LANES), F32),
            vmem((2, WIDE), I32),
            vmem((2, WIDE), F32),
            vmem((96, 8), F32),
            vmem((96, LANES), F32),
            vmem((2, ROWS), I32),
            vmem((2, ROWS), F32),
            vmem(TILE, F32),
            pltpu.SMEM((2, 2), I32),
            pltpu.SMEM((LEVELS,), F32),
            pltpu.SMEM((LEVELS,), F32),
            dma((9,)),
            dma((9,)),
            pltpu.SemaphoreType.REGULAR,
        ],
        compiler_params=pltpu.CompilerParams(
            collective_id=0, has_side_effects=True, vmem_limit_bytes=VMEM_A
        ),
    )(
        fields,
        east_band.reshape(96, LANES),
        north_band.reshape(96, 8),
        east_index,
        north_index,
        east_weight,
        north_weight,
        nest_moves,
        courant,
        diffuse,
    )
    return pl.pallas_call(
        write_kernel,
        out_shape=jax.ShapeDtypeStruct(fields.shape, F32),
        in_specs=[pl.BlockSpec(memory_space=pltpu.VMEM)],
        out_specs=pl.BlockSpec(memory_space=pl.ANY),
        scratch_shapes=[dma],
        compiler_params=pltpu.CompilerParams(vmem_limit_bytes=VMEM_B),
    )(ready)


VMEM_A = 56 * 1024 * 1024
VMEM_B = 8 * 1024 * 1024


def solution(mesh):
    sizes = (mesh.shape["gx"], mesh.shape["gy"])
    return jax.shard_map(
        functools.partial(body, sizes),
        mesh=mesh,
        in_specs=(
            P(None, None, "gx", "gy"),
            P(None, None, None, None, "gy"),
            P(None, None, None, None, "gx"),
            P(None, "gy"),
            P(None, "gx"),
            P(None, "gy"),
            P(None, "gx"),
            P(),
            P(),
            P(),
        ),
        out_specs=P(None, None, "gx", "gy"),
        check_vma=False,
    )
```
